32 devices in a mesh: batch: 4 (over y, x), seq: 8 (over z, core).
Axes of the slice: x: 2, y: 2, z: 4, core: 2. Of those that a mesh axis runs over, the one named last changes fastest.
Arguments:
- hidden_in: bfloat16 [16, 2048, 1024], P('batch', 'seq'), may hold values from -6 to 6
- cotangent: bfloat16 [16, 2048, 1024], P('batch', 'seq'), may hold values from -6 to 6
- lengths: int32 [16], P('batch'), may hold values from 256 to 2048, as said below
- key_mask: int32 [16, 2048], P('batch', 'seq'), may hold values 0 or 1
- ln1_gain: float32 [1024], replicated, may hold values from 0.5 to 1.5
- ln1_bias: float32 [1024], replicated, may hold values from -1.25 to 1.25
- ln2_gain: float32 [1024], replicated, may hold values from 0.5 to 1.5
- ln2_bias: float32 [1024], replicated, may hold values from -1.25 to 1.25
- w_qkv: bfloat16 [1024, 3072], replicated, may hold values from -0.1875 to 0.1875
- b_qkv: float32 [3072], replicated, may hold values from -1.25 to 1.25
- w_out: bfloat16 [1024, 1024], replicated, may hold values from -4 to 4
- b_out: float32 [1024], replicated, may hold values from -1.25 to 1.25
- w_up: bfloat16 [1024, 4096], replicated, may hold values from -0.1875 to 0.1875
- b_up: float32 [4096], replicated, may hold values from -1.25 to 1.25
- w_down: bfloat16 [4096, 1024], replicated, may hold values from -0.09375 to 0.09375
- b_down: float32 [1024], replicated, may hold values from -1.25 to 1.25
- feat_weight: float32 [1024], replicated, may hold values from 0.3 to 3
- directions: float32 [64, 64], replicated, may hold values from -2 to 2
Outputs:
- result: bfloat16 [16, 2048, 1024], P('batch', 'seq')
- grad_input: float32 [16, 2048, 1024], P('batch', 'seq')
- ln1_gain_grad: float32 [1024], P('seq')
- ln1_bias_grad: float32 [1024], P('seq')
- ln2_gain_grad: float32 [1024], P('seq')
- ln2_bias_grad: float32 [1024], P('seq')
- w_qkv_grad: float32 [1024, 3072], P('seq', 'batch')
- b_qkv_grad: float32 [3072], P('seq')
- w_out_grad: float32 [1024, 1024], P('seq', 'batch')
- b_out_grad: float32 [1024], P('seq')
- w_up_grad: float32 [1024, 4096], P('seq', 'batch')
- b_up_grad: float32 [4096], P('seq')
- w_down_grad: float32 [4096, 1024], P('seq', 'batch')
- b_down_grad: float32 [1024], P('seq')
- feat_weight_grad: float32 [1024], P('seq')
The draws below stay inside these ranges and needn't reach their ends.
Inputs may be any that keep to these rules, and one draw needn't show every extreme that they name: `lengths`: of each 4 consecutive sequences (one index of batch), one, chosen by the seed, has length 2048; the others from 256 to 2048.
All inputs are finite; a program needn't handle non-finite values. No bound on the sum of `key_mask` on one device may be relied on, other than what follows from the above.
Results may differ from the reference program's by a relative error of at most 0.0089.
Values sent between devices are 32-bit elements; how exact they have to be, the bound alone decides.
No kernel may reach another device: no remote copies, remote signals or barrier semaphores. Data moves between devices by JAX's collectives and lax.ppermute only.
A program may use at most 448 MiB of HBM per device.

```python
import math
import jax
import jax.numpy as jnp
from jax import lax

D = 1024
HEADS = 16
HEAD_DIM = 64
ROT = 16
FF = 4096
FEATS = 64
GROUP = 64
SEQ_GRP = 4
LEN = 2048
SEQS = 16


def draw_lengths(key, part):
    key = jax.random.fold_in(key, 11)
    base = jax.random.randint(jax.random.fold_in(key, 1), (SEQS,), LEN // 8, LEN + 1)
    picks = jax.random.randint(jax.random.fold_in(key, 2), (SEQS // SEQ_GRP,), 0, SEQ_GRP)
    index = jnp.arange(SEQS, dtype=jnp.int32)
    chosen = index % SEQ_GRP == picks[index // SEQ_GRP]
    return jnp.where(chosen, LEN, base).astype(jnp.int32)


def with_ends(values, own_key, low, top_value):
    longest = values.shape.index(max(values.shape))
    spots = []
    for shift in (0, 1):
        where = [jax.random.randint(jax.random.fold_in(own_key, axis), (), 0, length) for axis, length in enumerate(values.shape)]
        where[longest] = (where[longest] + shift) % values.shape[longest]
        spots.append(tuple(where))
    return values.at[spots[0]].set(low).at[spots[1]].set(top_value)


def levels(stream_key, extent, pieces, smallest, high):
    level = 1.0
    for dim, parts in pieces:
        heights = jax.random.uniform(jax.random.fold_in(jax.random.fold_in(stream_key, 6), dim), (parts,), jnp.float32, smallest / len(pieces), high / len(pieces))
        level = level * jnp.repeat(jnp.exp(heights), extent[dim] // parts).reshape((-1,) + (1,) * (len(extent) - 1 - dim))
    return level


def centred(rng, shape, deviation, most, cuts=(), kind=jnp.bfloat16):
    level = levels(rng, shape, cuts, -0.22, 0.18) if cuts else 1.0
    drawn = jax.random.normal(rng, shape, jnp.float32) * deviation * level
    return jnp.minimum(jnp.maximum(drawn, -most), most).astype(kind)


def setup_inputs(seed: int = 0) -> dict:
    seeds = jax.random.split(jax.random.key(seed), 19)
    return {
        "hidden_in": centred(seeds[0], (SEQS, LEN, D), 1.0, 6.0, ((0, 4), (1, 8))),
        "cotangent": centred(seeds[1], (SEQS, LEN, D), 1.0, 6.0, ((0, 4), (1, 8))),
        "lengths": draw_lengths(jax.random.fold_in(seeds[18], 71), 0),
        "key_mask": with_ends((jax.random.randint(seeds[3], (SEQS, LEN), 0, 8) < 7).astype(jnp.int32), jax.random.fold_in(seeds[3], 1), 0, 1),
        "ln1_gain": jnp.clip(1.0 + 0.1 * jax.random.normal(seeds[4], (D,), jnp.float32), 0.5, 1.5),
        "ln1_bias": centred(seeds[5], (D,), 0.2, 1.25, (), jnp.float32),
        "ln2_gain": jnp.clip(1.0 + 0.1 * jax.random.normal(seeds[6], (D,), jnp.float32), 0.5, 1.5),
        "ln2_bias": centred(seeds[7], (D,), 0.2, 1.25, (), jnp.float32),
        "w_qkv": centred(seeds[8], (D, 3 * D), D ** -0.5, 0.1875),
        "b_qkv": centred(seeds[9], (3 * D,), 0.2, 1.25, (), jnp.float32),
        "w_out": centred(seeds[10], (D, D), 2 ** -0.5, 4.0),
        "b_out": centred(seeds[11], (D,), 0.2, 1.25, (), jnp.float32),
        "w_up": centred(seeds[12], (D, FF), D ** -0.5, 0.1875),
        "b_up": centred(seeds[13], (FF,), 0.2, 1.25, (), jnp.float32),
        "w_down": centred(seeds[14], (FF, D), FF ** -0.5, 0.09375),
        "b_down": centred(seeds[15], (D,), 0.2, 1.25, (), jnp.float32),
        "feat_weight": jnp.clip(jnp.exp(jax.random.uniform(seeds[16], (HEADS * FEATS,), jnp.float32, math.log(0.3), math.log(3.0))), 0.3, 3.0),
        "directions": centred(seeds[17], (FEATS, HEAD_DIM), (1.2 * HEAD_DIM ** -0.5), 2.0, (), jnp.float32),
    }


@jax.custom_vjp
def low(v):
    return lax.optimization_barrier(v.astype(jnp.bfloat16)).astype(jnp.float32)

@jax.custom_vjp
def low_back(v):
    return v

def low_keep(v):
    return (low(v), None)

def low_pass(kept, grad):
    return (grad,)

def back_keep(v):
    return (v, None)

def back_low(kept, grad):
    return (low(grad),)
low.defvjp(low_keep, low_pass)
low_back.defvjp(back_keep, back_low)
norm_epsilon = 1e-05
rope_base = 10000.0

def layer_norm(values, gain, shift):
    centre = values - lax.optimization_barrier(jnp.mean(values, axis=-1, keepdims=True))
    spread = lax.optimization_barrier(jnp.mean(centre * centre, axis=-1, keepdims=True))
    return centre * lax.rsqrt(spread + norm_epsilon) * gain + shift

def dct_table(order):
    degree = jnp.arange(order, dtype=jnp.float32)[:, None]
    sample = jnp.arange(order, dtype=jnp.float32)[None, :]
    table = jnp.cos(math.pi * (sample + 0.5) * degree / order) * math.sqrt(2.0 / order)
    return jnp.where(degree == 0.0, table * math.sqrt(0.5), table)

def rotate_heads(heads, positions):
    half_rot = ROT // 2
    inverse = rope_base ** (-2.0 * jnp.arange(half_rot, dtype=jnp.float32) / ROT)
    angles = positions[:, None] * inverse[None, :]
    cosine = jnp.cos(angles)[:, None, :]
    sine = jnp.sin(angles)[:, None, :]
    first = heads[..., :half_rot]
    second = heads[..., half_rot:ROT]
    remain = heads[..., ROT:]
    return jnp.concatenate([first * cosine - second * sine, second * cosine + first * sine, remain], axis=-1)

def featurize(heads, weights, directions):
    table = dct_table(HEAD_DIM)
    coeffs = jnp.einsum('lhd,kd->lhk', heads, table, precision=lax.Precision.HIGHEST)
    phases = jnp.einsum('lhk,mk->lhm', coeffs, directions, precision=lax.Precision.HIGHEST)
    return weights * jnp.exp(phases)

def attend_blocks(query_feat, key_feat, values):
    seq_len = query_feat.shape[0]
    count = seq_len // GROUP

    def to_blocks(array):
        return array.reshape((count, GROUP) + array.shape[1:])
    lower = (jnp.arange(GROUP)[:, None] >= jnp.arange(GROUP)[None, :]).astype(jnp.float32)

    def block_step(carry, block):
        state, normal = carry
        query_blk, key_blk, value_blk = block
        scores = jnp.einsum('thf,shf->hts', query_blk, key_blk, precision=lax.Precision.HIGHEST) * lower[None]
        numer = jnp.einsum('hts,shd->thd', scores, value_blk, precision=lax.Precision.HIGHEST)
        numer = numer + jnp.einsum('thf,hfd->thd', query_blk, state, precision=lax.Precision.HIGHEST)
        denom = lax.optimization_barrier(jnp.sum(scores, axis=-1)).T + jnp.einsum('thf,hf->th', query_blk, normal, precision=lax.Precision.HIGHEST)
        mixed = numer / denom[..., None]
        state = state + jnp.einsum('shf,shd->hfd', key_blk, value_blk, precision=lax.Precision.HIGHEST)
        normal = normal + lax.optimization_barrier(jnp.sum(key_blk, axis=0))
        return ((state, normal), mixed)
    start = (jnp.zeros((HEADS, FEATS, HEAD_DIM), jnp.float32), jnp.zeros((HEADS, FEATS), jnp.float32))
    final_state, outputs = lax.scan(jax.checkpoint(block_step), start, (to_blocks(query_feat), to_blocks(key_feat), to_blocks(values)))
    return outputs.reshape(seq_len, HEADS * HEAD_DIM)

def forward_layer(inputs, params, validity, positions):
    ln1_gain, ln1_bias, ln2_gain, ln2_bias, w_qkv, b_qkv, w_out, b_out, w_up, b_up, w_down, b_down, feat_weight = params[:13]
    seq_len = inputs.shape[0]
    norm_one = low(layer_norm(inputs, ln1_gain, ln1_bias))
    norm_two = low(layer_norm(inputs, ln2_gain, ln2_bias))
    proj_all = low_back(jnp.dot(norm_one, w_qkv, precision=lax.Precision.HIGHEST) + b_qkv)
    shape3 = (seq_len, HEADS, HEAD_DIM)
    query = rotate_heads(proj_all[:, :D].reshape(shape3), positions)
    keys = rotate_heads(proj_all[:, D:2 * D].reshape(shape3), positions)
    values = low(proj_all[:, 2 * D:].reshape(shape3))
    weights = feat_weight.reshape(HEADS, FEATS)
    query_feat = low(featurize(query, weights, directions_holder(params)))
    key_feat = low(featurize(keys, weights, directions_holder(params))) * validity[:, None, None]
    mixed = low(attend_blocks(query_feat, key_feat, values))
    attn_out = jnp.dot(mixed, w_out, precision=lax.Precision.HIGHEST) + b_out
    hidden_pre = low_back(jnp.dot(norm_two, w_up, precision=lax.Precision.HIGHEST) + b_up)
    gelu_out = low(jax.nn.gelu(hidden_pre, approximate=False))
    ffn_out = jnp.dot(gelu_out, w_down, precision=lax.Precision.HIGHEST) + b_down
    return inputs + attn_out + ffn_out

def directions_holder(params):
    return params[13]

def reference(hidden_in, cotangent, lengths, key_mask, ln1_gain, ln1_bias, ln2_gain, ln2_bias, w_qkv, b_qkv, w_out, b_out, w_up, b_up, w_down, b_down, feat_weight, directions):
    params = tuple((item.astype(jnp.float32) for item in (ln1_gain, ln1_bias, ln2_gain, ln2_bias, w_qkv, b_qkv, w_out, b_out, w_up, b_up, w_down, b_down, feat_weight)))
    fixed_dirs = directions.astype(jnp.float32)
    positions = jnp.arange(LEN, dtype=jnp.float32)
    places = jnp.arange(LEN, dtype=jnp.int32)

    def per_sequence(totals, item):
        seq_in, seq_cot, seq_len, seq_mask = item
        validity = ((places < seq_len) & ((seq_mask == 1) | (places == 0))).astype(jnp.float32)

        def run_layer(values, weights):
            return forward_layer(values, weights + (fixed_dirs,), validity, positions)
        outcome, pull = jax.vjp(run_layer, seq_in.astype(jnp.float32), params)
        grad_in, grad_params = pull(seq_cot.astype(jnp.float32))
        totals = jax.tree.map(lambda total_part, new_part: total_part + new_part, totals, grad_params)
        return (totals, (outcome.astype(jnp.bfloat16), grad_in))
    start = jax.tree.map(jnp.zeros_like, params)
    totals, outputs = lax.scan(per_sequence, start, (hidden_in, cotangent, lengths, key_mask))
    result, grad_input = outputs
    return (result, grad_input, totals[0], totals[1], totals[2], totals[3], totals[4], totals[5], totals[6], totals[7], totals[8], totals[9], totals[10], totals[11], totals[12])
```

```python
import functools
import math

import jax
import jax.numpy as jnp
from jax import lax
from jax.experimental import pallas as pl
from jax.experimental.pallas import tpu as pltpu
from jax.sharding import PartitionSpec as P

f32 = jnp.float32
bf16 = jnp.bfloat16
struct = jax.ShapeDtypeStruct
HEADS = 16
HEAD_DIM = 64
ROT = 16
LEN_BLK = 256
HG = 256
ROOT_HALF = math.sqrt(0.5)
NORMAL_PEAK = 1.0 / math.sqrt(2.0 * math.pi)
norm_epsilon = 1e-05
rope_base = 10000.0
VMEM_BYTES = 60 * 1024 * 1024


def params():
    return pltpu.CompilerParams(vmem_limit_bytes=VMEM_BYTES)


def dot(a, b, ca, cb):
    return lax.dot_general(a, b, (((ca,), (cb,)), ((), ())), preferred_element_type=f32)


def iota(shape, dim):
    return lax.broadcasted_iota(jnp.int32, shape, dim)


def split(x):
    hi = x.astype(bf16)
    return hi, (x - hi.astype(f32)).astype(bf16)


def split_outside(x):
    hi = lax.reduce_precision(x, 8, 7)
    return hi.astype(bf16), (x - hi).astype(bf16)


def ffn_kernel(aliased, pos, a2, g, wu0, wu1, wd0, wd1, bu0, bu1, *refs):
    refs = refs[4:] if aliased else refs
    gelu_a, gelu_b, gp_a, gp_b, up_send, up_keep, down_send, down_keep, b_sum = refs
    me, core = pos[0], pos[1]
    rows_in = a2[...]
    grad_in = g[...]
    w_up = jnp.concatenate([wu0[...], wu1[...]], axis=1)
    w_down = jnp.concatenate([wd0[...], wd1[...]], axis=0)
    bias = jnp.concatenate([bu0[...], bu1[...]], axis=1)
    pre = dot(rows_in, w_up, 1, 0) + bias
    grad_gelu = dot(grad_in, w_down, 1, 1)
    cdf = 0.5 + 0.5 * lax.erf(pre * ROOT_HALF)
    gelu = (pre * cdf).astype(bf16)
    grad_pre = (grad_gelu * (cdf + pre * (NORMAL_PEAK * jnp.exp(-0.5 * pre * pre)))).astype(bf16)
    gelu_a[...] = gelu[:, :128]
    gelu_b[...] = gelu[:, 128:]
    gp_a[...] = grad_pre[:, :128]
    gp_b[...] = grad_pre[:, 128:]
    b_sum[0] = jnp.sum(grad_pre.astype(f32), axis=0, keepdims=True)
    d_up = dot(grad_pre, rows_in, 0, 0)
    d_down = dot(gelu, grad_in, 0, 0)

    def put(c):
        for z in range(4):
            up_send[0, 0, z] = d_up[:, (2 * z + 1 - c) * 128 : (2 * z + 2 - c) * 128]
            up_keep[0, 0, z] = d_up[:, (2 * z + c) * 128 : (2 * z + c + 1) * 128]
        for b in range(4):
            rel = lax.bitwise_xor(jnp.int32(b), me)
            rx, ry = lax.rem(rel, 2), lax.div(rel, 2)
            down_send[ry, rx, 0] = d_down[(1 - c) * 128 : (2 - c) * 128, b * 256 : (b + 1) * 256]
            down_keep[ry, rx, 0] = d_down[c * 128 : (c + 1) * 128, b * 256 : (b + 1) * 256]

    pl.when(core == 0)(lambda: put(0))
    pl.when(core == 1)(lambda: put(1))


def ffn_chunk(first, count, pos, a2, g, w_up, w_down, b_up, earlier):
    rows, width = a2.shape
    hidden = w_up.shape[1]
    cols = lambda j: (lambda k, b, p: (0, (2 * b + j) * 4 + first + k))
    lines = lambda j: (lambda k, b, p: ((2 * b + j) * 4 + first + k, 0))
    whole = lambda k, b, p: (0, 0)
    place = lambda k, b, p: (0, b * 4 + first + k)

    def up_place(k, b, p):
        rel = lax.bitwise_xor(b, p[0])
        return (lax.rem(rel, 2), lax.div(rel, 2), 0, k, 0)

    down_place = lambda k, b, p: (0, 0, b, k, 0)
    in_specs = (
        [pl.BlockSpec((rows, width), whole)] * 2
        + [pl.BlockSpec((width, 128), cols(j)) for j in range(2)]
        + [pl.BlockSpec((128, width), lines(j)) for j in range(2)]
        + [pl.BlockSpec((1, 128), cols(j)) for j in range(2)]
    )
    args = [pos, a2, g, w_up, w_up, w_down, w_down, b_up, b_up]
    aliases = {}
    if earlier is not None:
        aliases = {len(args) + i: i for i in range(4)}
        in_specs = in_specs + [pl.BlockSpec(memory_space=pl.ANY)] * 4
        args = args + list(earlier)
    return pl.pallas_call(
        functools.partial(ffn_kernel, earlier is not None),
        grid_spec=pltpu.PrefetchScalarGridSpec(
            num_scalar_prefetch=1,
            grid=(count, 4),
            in_specs=in_specs,
            out_specs=[pl.BlockSpec((rows, 128), place)] * 4
            + [pl.BlockSpec((1, 1, 4, 256, 128), up_place)] * 2
            + [pl.BlockSpec((2, 2, 1, 128, 256), down_place)] * 2
            + [pl.BlockSpec((1, 1, 256), lambda k, b, p: (k * 4 + b, 0, 0))],
        ),
        out_shape=[struct((rows, hidden // 2), bf16)] * 4
        + [struct((2, 2, 4, count * 256, 128), f32)] * 2
        + [struct((2, 2, 4, count * 128, 256), f32)] * 2
        + [struct((count * 4, 1, 256), f32)],
        input_output_aliases=aliases,
        compiler_params=params(),
        cost_estimate=pl.CostEstimate(
            flops=8 * rows * width * 1024 * count,
            bytes_accessed=(4 + 20 * count) * 2**20,
            transcendentals=2 * rows * 1024 * count,
        ),
        name="ffn_chunk",
    )(*args)


def wgrad_kernel(pos, left, right, send, keep):
    tile = dot(left[...], right[0], 0, 0)
    core = pos[1]

    def put(c):
        for z in range(4):
            send[0, 0, z, 0] = tile[(2 * z + 1 - c) * 128 : (2 * z + 2 - c) * 128]
            keep[0, 0, z, 0] = tile[(2 * z + c) * 128 : (2 * z + c + 1) * 128]

    pl.when(core == 0)(lambda: put(0))
    pl.when(core == 1)(lambda: put(1))


def wgrad(pos, left, right, units, y_first):
    rows, width = left.shape
    per = len(units)

    def source(b, j, p):
        unit = b * 3 + units[0] + j if units is not WHOLE else b
        return (lax.div(unit, 4), 0, lax.rem(unit, 4))

    def target(b, j, p):
        rel = lax.bitwise_xor(b, p[0])
        rx, ry = lax.rem(rel, 2), lax.div(rel, 2)
        return (ry, rx, 0, j, 0, 0) if y_first else (rx, ry, 0, j, 0, 0)

    return pl.pallas_call(
        wgrad_kernel,
        grid_spec=pltpu.PrefetchScalarGridSpec(
            num_scalar_prefetch=1,
            grid=(4, per),
            in_specs=[
                pl.BlockSpec((rows, width), lambda b, j, p: (0, 0)),
                pl.BlockSpec((1, rows, 256), source),
            ],
            out_specs=[pl.BlockSpec((1, 1, 4, 1, 128, 256), target)] * 2,
        ),
        out_shape=[struct((2, 2, 4, per, 128, 256), f32)] * 2,
        compiler_params=params(),
        cost_estimate=pl.CostEstimate(
            flops=2 * rows * width * 1024 * per,
            bytes_accessed=(2 + 6 * per) * 2**20,
            transcendentals=0,
        ),
        name="wgrad",
    )(pos, left, right)


WHOLE = (0,)


def rotate(x, cos, sin_first, sin_second):
    n = x.shape[1]
    half = ROT // 2
    return x * cos + pltpu.roll(x, n - half, 1) * sin_first + pltpu.roll(x, half, 1) * sin_second


def three(x, w_hi, w_lo):
    hi, lo = split(x)
    return dot(hi, w_hi, 1, 0) + dot(lo, w_hi, 1, 0) + dot(hi, w_lo, 1, 0)


def pair_mask():
    return (iota((128, 128), 0) // 64) == (iota((128, 128), 1) // 64)


def pack(first, second):
    mask = pair_mask()
    first = jnp.where(mask, first, 0.0)
    second = jnp.where(mask, second, 0.0)
    first = first + pltpu.roll(first, 64, 1)
    second = second + pltpu.roll(second, 64, 1)
    return jnp.where(iota((128, 128), 1) < 64, first, second)


def unpack(packed):
    mask = pair_mask()
    low = iota((128, 128), 1) < 64
    turned = pltpu.roll(packed, 64, 1)
    return (
        jnp.where(mask, jnp.where(low, packed, turned), 0.0),
        jnp.where(mask, jnp.where(low, turned, packed), 0.0),
    )


def to_column(row):
    eye = iota((128, 128), 0) == iota((128, 128), 1)
    return jnp.sum(jnp.where(eye, jnp.broadcast_to(row, (128, 128)), 0.0), axis=1, keepdims=True)


def each_head(x):
    mask = iota((1, 128), 1) < 64
    zero = jnp.zeros_like(x)
    return jnp.where(mask, x, zero), jnp.where(mask, zero, x)


def feature_kernel(
    a1, wq, wk, wv, bq, bk, bv, fw, m_hi, m_lo, cos, sin1, sin2, valid, qf_o, kf_o, v_o, st_o
):
    x = a1[...]
    count = x.shape[0] // LEN_BLK
    turns = [jnp.concatenate([t[...]] * count, 0) for t in (cos, sin1, sin2)]
    q = dot(x, wq[...], 1, 0) + bq[...]
    k = dot(x, wk[...], 1, 0) + bk[...]
    v = (dot(x, wv[...], 1, 0) + bv[...]).astype(bf16)
    weight = fw[...]
    qf = (weight * jnp.exp(three(rotate(q, *turns), m_hi[...], m_lo[...]))).astype(bf16)
    kf = (weight * jnp.exp(three(rotate(k, *turns), m_hi[...], m_lo[...]))).astype(bf16)
    kf = kf * valid[...].astype(bf16)
    qf_o[...] = qf
    kf_o[...] = kf
    v_o[...] = v
    for i in range(count):
        r = slice(LEN_BLK * i, LEN_BLK * (i + 1))
        state = [
            dot(kf[r, 128 * p : 128 * p + 128], v[r, 128 * p : 128 * p + 128], 0, 0)
            for p in range(2)
        ]
        st_o[i, 0, :128] = pack(state[0], state[1])
        norm = jnp.sum(kf[r].astype(f32), axis=0, keepdims=True)
        st_o[i, 0, 128:] = norm_rows(norm[:, :128], norm[:, 128:])


def norm_rows(first, second):
    line = iota((8, 128), 0)
    return jnp.where(line == 0, first, jnp.where(line == 1, second, 0.0))


def scores(qp, kp, causal):
    return [jnp.where(causal, dot(qh, kp, 1, 1), 0.0).astype(bf16) for qh in each_head(qp)]


def lower(n):
    return iota((n, n), 0) >= iota((n, n), 1)


def mix_kernel(g, wo, qf, kf, v, st, mix_o, dn_o, dd_o, ds_o):
    count = qf.shape[0] // LEN_BLK
    grad_mixed = dot(g[...], wo[...], 1, 1)
    mask = pair_mask()
    lane = iota((1, 128), 1)
    first = lane < 64
    causal = lower(LEN_BLK)
    one0, one1 = each_head(jnp.ones((LEN_BLK, 128), bf16))
    for i in range(count):
        r = slice(LEN_BLK * i, LEN_BLK * (i + 1))
        state = unpack(st[i, 0, :128])
        grads, norms = [], []
        dd_lines = jnp.zeros((LEN_BLK, 128), f32)
        for p in range(2):
            sl = slice(128 * p, 128 * p + 128)
            qp, kp, vp = qf[r, sl], kf[r, sl], v[r, sl]
            s0, s1 = scores(qp, kp, causal)
            v0, v1 = each_head(vp)
            right = jnp.concatenate(
                [jnp.concatenate([v0, one0], 1), jnp.concatenate([v1, one1], 1)], 0
            )
            both = dot(jnp.concatenate([s0, s1], 1), right, 1, 0)
            column = to_column(st[i, 0, 128 + p : 129 + p])
            norm = jnp.where(mask, jnp.broadcast_to(column, (128, 128)), 0.0)
            hi, lo = split(jnp.concatenate([state[p], norm], 1))
            both = both + dot(jnp.concatenate([qp, qp], 1), jnp.concatenate([hi, lo], 0), 1, 0)
            inverse = 1.0 / both[:, 128:]
            mixed = both[:, :128] * inverse
            mix_o[r, sl] = mixed.astype(bf16)
            dn = (grad_mixed[r, sl] * inverse).astype(bf16)
            dn_o[r, sl] = dn
            product = -(dn.astype(f32) * mixed)
            d0 = jnp.sum(jnp.where(first, product, 0.0), axis=1, keepdims=True)
            d1 = jnp.sum(jnp.where(first, 0.0, product), axis=1, keepdims=True)
            dd_lines = jnp.where(
                lane == 2 * p, d0, jnp.where(lane == 2 * p + 1, d1, dd_lines)
            )
            grads.append(dot(qp, dn, 0, 0))
            norms.append(
                jnp.sum(qp.astype(f32) * jnp.where(first, d0, d1), axis=0, keepdims=True)
            )
        dd_o[0, r] = dd_lines
        ds_o[i, 0, :128] = pack(grads[0], grads[1])
        ds_o[i, 0, 128:] = norm_rows(norms[0], norms[1])


def back_kernel(
    qf, kf, v, dn, dd, st, ds, fw, m_hi, m_lo, cos, sin1, sin2, gp_o, bias_o, fw_o
):
    count = qf.shape[0] // LEN_BLK
    step = pl.program_id(1)
    causal = lower(LEN_BLK)
    lane = iota((1, 128), 1)
    first = lane < 64
    turns = cos[...], -sin1[...], -sin2[...]
    totals = None
    for i in range(count):
        r = slice(LEN_BLK * i, LEN_BLK * (i + 1))
        state, later = unpack(st[i, 0, :128]), unpack(ds[i, 0, :128])
        dq, dk, dv = [], [], []
        for p in range(2):
            sl = slice(128 * p, 128 * p + 128)
            qp, kp, vp, np_ = qf[r, sl], kf[r, sl], v[r, sl], dn[r, sl]
            s = scores(qp, kp, causal)
            dn_heads = each_head(np_)
            column = [
                jnp.sum(jnp.where(lane == 2 * p + h, dd[0, r], 0.0), axis=1, keepdims=True)
                for h in range(2)
            ]
            t = [
                jnp.where(causal, dot(dn_heads[h], vp, 1, 1) + column[h], 0.0).astype(bf16)
                for h in range(2)
            ]
            s_hi, s_lo = split(state[p])
            d_hi, d_lo = split(later[p])
            dqf = dot(jnp.concatenate(t, 1), jnp.concatenate(each_head(kp), 0), 1, 0)
            dqf = dqf + dot(
                jnp.concatenate([np_, np_], 1), jnp.concatenate([s_hi, s_lo], 1), 1, 1
            )
            dqf = dqf + jnp.where(first, column[0], column[1]) * st[i, 0, 128 + p : 129 + p]
            dkf = dot(jnp.concatenate(t, 0), jnp.concatenate(each_head(qp), 0), 0, 0)
            dkf = dkf + dot(
                jnp.concatenate([vp, vp], 1), jnp.concatenate([d_hi, d_lo], 1), 1, 1
            )
            dkf = dkf + ds[i, 0, 128 + p : 129 + p]
            dvv = dot(jnp.concatenate(s, 0), jnp.concatenate(dn_heads, 0), 0, 0)
            dvv = dvv + dot(
                jnp.concatenate([kp, kp], 1), jnp.concatenate([d_hi, d_lo], 0), 1, 0
            )
            dq.append(dqf * qp.astype(f32))
            dk.append(dkf * kp.astype(f32))
            dv.append(dvv)
        dq = jnp.concatenate(dq, 1)
        dk = jnp.concatenate(dk, 1)
        grads = (
            rotate(three(dq, m_hi[...], m_lo[...]), *turns).astype(bf16),
            rotate(three(dk, m_hi[...], m_lo[...]), *turns).astype(bf16),
            jnp.concatenate(dv, 1).astype(bf16),
        )
        for n in range(3):
            gp_o[n, r] = grads[n]
        sums = [jnp.sum(part.astype(f32), axis=0, keepdims=True) for part in grads]
        sums.append(jnp.sum(dq + dk, axis=0, keepdims=True) / fw[...])
        totals = sums if totals is None else [a + b for a, b in zip(totals, sums)]

    @pl.when(step == 0)
    def _():
        for n in range(3):
            bias_o[n] = totals[n]
        fw_o[...] = totals[3]

    @pl.when(step > 0)
    def _():
        for n in range(3):
            bias_o[n] = bias_o[n] + totals[n]
        fw_o[...] = fw_o[...] + totals[3]


def attention_specs(seqs, per):
    rows = LEN_BLK * per
    return dict(
        grid=(4, seqs // per),
        wide=pl.BlockSpec((rows, 1024), lambda h, g: (g, 0)),
        head=pl.BlockSpec((rows, HG), lambda h, g: (g, h)),
        state=pl.BlockSpec((per, 1, 136, 128), lambda h, g: (g, h, 0, 0)),
        row=pl.BlockSpec((1, HG), lambda h, g: (0, h)),
        table=pl.BlockSpec((256, 256), lambda h, g: (0, 0)),
        dden=pl.BlockSpec((1, rows, 128), lambda h, g: (h, g, 0)),
    )


def cost(giga, mega):
    return pl.CostEstimate(
        flops=int(giga * 1e9), bytes_accessed=mega * 2**20, transcendentals=0
    )


def features(a1, w_qkv, b_qkv, feat_weight, tables, turns, valid, per=4):
    rows = a1.shape[0]
    seqs = rows // LEN_BLK
    s = attention_specs(seqs, per)
    weights = [pl.BlockSpec((1024, HG), lambda h, g, o=o: (0, 4 * o + h)) for o in range(3)]
    biases = [pl.BlockSpec((1, HG), lambda h, g, o=o: (0, 4 * o + h)) for o in range(3)]
    return pl.pallas_call(
        feature_kernel,
        grid=s["grid"],
        in_specs=[s["wide"], *weights, *biases, s["row"]]
        + [s["table"]] * 5
        + [pl.BlockSpec((LEN_BLK * per, 1), lambda h, g: (g, 0))],
        out_specs=[s["head"]] * 3 + [s["state"]],
        out_shape=[struct((rows, 1024), bf16)] * 3 + [struct((seqs, 4, 136, 128), f32)],
        compiler_params=params(),
        cost_estimate=cost(15, 20),
        name="features",
    )(a1, w_qkv, w_qkv, w_qkv, b_qkv, b_qkv, b_qkv, feat_weight, *tables, *turns, valid)


def mixing(g, w_out, qf, kf, v, state, per=2):
    rows = g.shape[0]
    seqs = rows // LEN_BLK
    s = attention_specs(seqs, per)
    return pl.pallas_call(
        mix_kernel,
        grid=s["grid"],
        in_specs=[s["wide"], pl.BlockSpec((HG, 1024), lambda h, g: (h, 0))]
        + [s["head"]] * 3
        + [s["state"]],
        out_specs=[s["head"]] * 2 + [s["dden"], s["state"]],
        out_shape=[struct((rows, 1024), bf16)] * 2
        + [struct((4, rows, 128), f32), struct((seqs, 4, 136, 128), f32)],
        compiler_params=params(),
        cost_estimate=cost(16, 20),
        name="mixing",
    )(g, w_out, qf, kf, v, state)


def backward(qf, kf, v, dn, dd, state, later, feat_weight, tables, turns, per=4):
    rows = qf.shape[0]
    seqs = rows // LEN_BLK
    s = attention_specs(seqs, per)
    return pl.pallas_call(
        back_kernel,
        grid=s["grid"],
        in_specs=[s["head"]] * 4
        + [s["dden"], s["state"], s["state"], s["row"]]
        + [s["table"]] * 5,
        out_specs=[
            pl.BlockSpec((3, LEN_BLK * per, HG), lambda h, g: (0, g, h)),
            pl.BlockSpec((3, 1, HG), lambda h, g: (0, 0, h)),
            s["row"],
        ],
        out_shape=[struct((3, rows, 1024), bf16), struct((3, 1, 1024), f32), struct((1, 1024), f32)],
        compiler_params=params(),
        cost_estimate=cost(20, 24),
        name="backward",
    )(qf, kf, v, dn, dd, state, later, feat_weight, *tables, *turns)


def norm_parts(x):
    centre = x - jnp.mean(x, axis=-1, keepdims=True)
    r = lax.rsqrt(jnp.mean(centre * centre, axis=-1, keepdims=True) + norm_epsilon)
    return centre * r, r


def norm_back(grad, xhat, r, gain):
    e = grad * gain
    return r * (
        e
        - jnp.mean(e, axis=-1, keepdims=True)
        - xhat * jnp.mean(e * xhat, axis=-1, keepdims=True)
    )


def add_sums(out, sums):
    step = pl.program_id(0)
    new = jnp.concatenate(sums, 0)

    @pl.when(step == 0)
    def _():
        out[...] = new

    @pl.when(step > 0)
    def _():
        out[...] = out[...] + new


def column_sum(x):
    return jnp.sum(x, axis=0, keepdims=True)


def in_order(a, b):
    parts = []
    for n in range(4):
        parts += [a[:, 512 * n : 512 * n + 512], b[:, 512 * n : 512 * n + 512]]
    return jnp.concatenate(parts, axis=1)


def ends_kernel(
    x, g, mixed, gelu_a, gelu_b, gp_a, gp_b, w_out, w_down, w_up, bias, gain, res_o, part_o, sum_o
):
    value = x[...].astype(f32)
    out = dot(mixed[...], w_out[...], 1, 0)
    out = out + dot(in_order(gelu_a[...], gelu_b[...]), w_down[...], 1, 0)
    res_o[...] = (value + out + bias[...]).astype(bf16)
    grad = dot(in_order(gp_a[...], gp_b[...]), w_up[...], 1, 1)
    xhat, r = norm_parts(value)
    grad_res = g[...].astype(f32)
    part_o[...] = grad_res + norm_back(grad, xhat, r, gain[...])
    zero = jnp.zeros((5, 1024), f32)
    add_sums(sum_o, [column_sum(grad * xhat), column_sum(grad), column_sum(grad_res), zero])


def ends(x, g, mixed, gelu_a, gelu_b, gp_a, gp_b, w_out, w_down, w_up, bias, gain):
    rows = x.shape[0]
    tile = 256
    wide = lambda n: pl.BlockSpec((tile, n), lambda i: (i, 0))
    fixed = lambda a: pl.BlockSpec(a.shape, lambda i: (0, 0), pipeline_mode=pl.Buffered(1))
    return pl.pallas_call(
        ends_kernel,
        grid=(rows // tile,),
        in_specs=[wide(1024)] * 3
        + [wide(2048)] * 4
        + [fixed(a) for a in (w_out, w_down, w_up, bias, gain)],
        out_specs=[wide(1024), wide(1024), pl.BlockSpec((8, 1024), lambda i: (0, 0))],
        out_shape=[struct((rows, 1024), bf16), struct((rows, 1024), f32), struct((8, 1024), f32)],
        compiler_params=params(),
        cost_estimate=cost(19, 48),
        name="ends",
    )(x, g, mixed, gelu_a, gelu_b, gp_a, gp_b, w_out, w_down, w_up, bias, gain)


def last_kernel(x, part, gp, w_qkv, gain, out_o, sum_o):
    value = x[...].astype(f32)
    grad = dot(jnp.concatenate([gp[0], gp[1], gp[2]], 1), w_qkv[...], 1, 1)
    xhat, r = norm_parts(value)
    out_o[...] = part[...] + norm_back(grad, xhat, r, gain[...])
    zero = jnp.zeros((6, 1024), f32)
    add_sums(sum_o, [column_sum(grad * xhat), column_sum(grad), zero])


def last(x, part, gp, w_qkv, gain):
    rows = x.shape[0]
    tile = 256
    wide = pl.BlockSpec((tile, 1024), lambda i: (i, 0))
    fixed = lambda a: pl.BlockSpec(a.shape, lambda i: (0, 0), pipeline_mode=pl.Buffered(1))
    return pl.pallas_call(
        last_kernel,
        grid=(rows // tile,),
        in_specs=[
            wide,
            wide,
            pl.BlockSpec((3, tile, 1024), lambda i: (0, i, 0)),
            fixed(w_qkv),
            fixed(gain),
        ],
        out_specs=[wide, pl.BlockSpec((8, 1024), lambda i: (0, 0))],
        out_shape=[struct((rows, 1024), f32), struct((8, 1024), f32)],
        compiler_params=params(),
        cost_estimate=cost(6.4, 22),
        name="last",
    )(x, part, gp, w_qkv, gain)


class Links:
    def __init__(self, mesh):
        self.nb, self.ns = mesh.shape["batch"], mesh.shape["seq"]
        self.tuned = (self.nb, self.ns) == (4, 8)

    def send(self, value, move):
        pairs = []
        for b in range(self.nb):
            for s in range(self.ns):
                to = move(b, s)
                if to is not None:
                    pairs.append((b * self.ns + s, to[0] * self.ns + to[1]))
        return lax.ppermute(value, ("batch", "seq"), pairs)

    def core(self, value):
        return self.send(value, lambda b, s: (b, s ^ 1))

    def x(self, value):
        return self.send(value, lambda b, s: (b ^ 1, s))

    def y(self, value):
        return self.send(value, lambda b, s: (b ^ 2, s))

    def shift(self, value, by):
        inside = lambda s: 0 <= s < self.ns
        return self.send(value, lambda b, s: (b, s + by) if inside(s + by) else None)


def reduce_pairs(links, send, keep, y_first):
    first, second = (links.y, links.x) if y_first else (links.x, links.y)
    got = links.core(send)
    one = first(keep[1] + got[1])
    two = second(keep[0, 1] + got[0, 1] + one[1])
    return keep[0, 0] + got[0, 0] + one[0] + two


def reduce_z(value):
    groups = [[0, 2, 4, 6], [1, 3, 5, 7]]
    return lax.psum_scatter(
        value, "seq", scatter_dimension=0, axis_index_groups=groups, tiled=True
    )[0]


def carried(links, state, reverse):
    sign = -1 if reverse else 1
    if not links.tuned:
        total, step = state, 1
        while step < links.ns:
            total = total + links.shift(total, sign * step)
            step *= 2
        return links.shift(total, sign)
    core = lax.rem(lax.axis_index("seq"), 2)
    other = links.core(state)
    half = state.shape[0] // 2
    mine = lax.dynamic_slice_in_dim(state, core * half, half, 0)
    mine = mine + lax.dynamic_slice_in_dim(other, core * half, half, 0)
    near = links.shift(mine, sign * 2)
    far = links.shift(mine + near, sign * 4)
    before = near + far
    rest = links.core(before)
    low = jnp.where(core == 0, before, rest)
    high = jnp.where(core == 0, rest, before)
    whole = jnp.concatenate([low, high], 0)
    behind = core == (0 if reverse else 1)
    return whole + jnp.where(behind, other, 0.0)


def dct_table(order):
    degree = jnp.arange(order, dtype=f32)[:, None]
    sample = jnp.arange(order, dtype=f32)[None, :]
    table = jnp.cos(math.pi * (sample + 0.5) * degree / order) * math.sqrt(2.0 / order)
    return jnp.where(degree == 0.0, table * math.sqrt(0.5), table)


def rotation_tables(positions):
    half = ROT // 2
    inverse = rope_base ** (-2.0 * jnp.arange(half, dtype=f32) / ROT)
    angles = positions[:, None] * inverse[None, :]
    cos, sin = jnp.cos(angles), jnp.sin(angles)
    rest = jnp.zeros((positions.shape[0], HEAD_DIM - ROT), f32)
    zero = jnp.zeros_like(cos)
    rows = ([cos, cos, rest + 1.0], [-sin, zero, rest], [zero, sin, rest])
    return tuple(jnp.tile(jnp.concatenate(r, 1), (1, HG // HEAD_DIM)) for r in rows)


def four_blocks(matrix):
    return jnp.kron(jnp.eye(HG // HEAD_DIM, dtype=f32), matrix)


def per_device(
    links,
    hidden_in,
    cotangent,
    lengths,
    key_mask,
    ln1_gain,
    ln1_bias,
    ln2_gain,
    ln2_bias,
    w_qkv,
    b_qkv,
    w_out,
    b_out,
    w_up,
    b_up,
    w_down,
    b_down,
    feat_weight,
    directions,
):
    seqs, block, width = hidden_in.shape
    rows = seqs * block
    tuned = links.tuned
    place = lax.axis_index("seq")
    if tuned:
        pos = jnp.stack([lax.axis_index("batch"), lax.rem(place, 2)]).astype(jnp.int32)
    else:
        pos = jnp.zeros((2,), jnp.int32)
    places = place * block + jnp.arange(block, dtype=jnp.int32)
    valid = (places[None, :] < lengths[:, None]) & ((key_mask == 1) | (places[None, :] == 0))
    valid = valid.astype(f32).reshape(rows, 1)
    x = hidden_in.reshape(rows, width)
    g = cotangent.reshape(rows, width)
    xhat, _ = norm_parts(x.astype(f32))
    a2 = (xhat * ln2_gain + ln2_bias).astype(bf16)
    a1 = (xhat * ln1_gain + ln1_bias).astype(bf16)
    row = lambda v: v.reshape(1, -1)

    table = jnp.dot(directions, dct_table(HEAD_DIM), precision=lax.Precision.HIGHEST)
    forth = split_outside(four_blocks(table.T))
    back = split_outside(four_blocks(table))
    turns = rotation_tables(places.astype(f32))

    ffn = functools.partial(ffn_chunk, pos=pos, a2=a2, g=g, w_up=w_up, w_down=w_down, b_up=row(b_up))
    chunks = []
    earlier = None
    for first, count in ((0, 1), (1, 1), (2, 2)):
        out = ffn(first, count, earlier=earlier)
        earlier = out[:4]
        chunks.append(out[4:])

    qf, kf, v, state = features(a1, w_qkv, row(b_qkv), row(feat_weight), forth, turns, valid)
    state_in = carried(links, state, False)
    mixed, dn, dd, state_grad = mixing(g, w_out, qf, kf, v, state_in)
    state_later = carried(links, state_grad, True)
    out_pair = wgrad(pos, mixed, g[None], WHOLE, False)
    result, partial, sums2 = ends(
        x, g, mixed, *earlier, w_out, w_down, w_up, row(b_out + b_down), row(ln2_gain)
    )
    grad_proj, bias_qkv, grad_feat = backward(
        qf, kf, v, dn, dd, state_in, state_later, row(feat_weight), back, turns
    )
    qkv_pairs = [wgrad(pos, a1, grad_proj, (j,), j != 1) for j in range(3)]
    grad_input, sums1 = last(x, partial, grad_proj, w_qkv, row(ln1_gain))

    b_up_parts = [c[4].reshape(-1, 4, 2, 128) for c in chunks]
    b_up_grad = jnp.concatenate(b_up_parts, 0).transpose(1, 2, 0, 3).reshape(-1)
    vectors = [sums1[0], sums1[1], sums2[0], sums2[1], bias_qkv.reshape(-1), sums2[2], b_up_grad, grad_feat[0]]
    sizes = [v_.shape[0] for v_ in vectors]
    total = lax.psum(jnp.concatenate(vectors), ("batch", "seq"))
    shares, at = [], 0
    for n in sizes:
        share = n // links.ns
        shares.append(lax.dynamic_slice_in_dim(total, at + place * share, share, 0))
        at += n

    if tuned:
        ups, downs = [], []
        for c in chunks:
            u = reduce_pairs(links, c[0], c[1], False)
            d = reduce_pairs(links, c[2], c[3], True)
            n = u.shape[1] // 256
            both = jnp.concatenate([u, d[..., :128], d[..., 128:]], 1)
            both = reduce_z(both)
            ups.append(both[: n * 256].reshape(n, 2, 128, 128))
            downs.append(jnp.concatenate([both[n * 256 : n * 384], both[n * 384 :]], 1))
        w_up_grad = jnp.concatenate(ups, 0).transpose(3, 1, 0, 2).reshape(128, 1024)
        w_down_grad = jnp.concatenate(downs, 0)
        pairs = [reduce_pairs(links, *out_pair, False)] + [
            reduce_pairs(links, *p, j != 1) for j, p in enumerate(qkv_pairs)
        ]
        w_out_grad = reduce_z(pairs[0]).reshape(128, 256)
        w_qkv_grad = jnp.concatenate([reduce_z(p).reshape(128, 256) for p in pairs[1:]], 1)
    else:

        def scatter(full):
            part = lax.psum_scatter(full, "batch", scatter_dimension=1, tiled=True)
            return lax.psum_scatter(part, "seq", scatter_dimension=0, tiled=True)

        ups = [jnp.stack([c[1], c[0]], 3).reshape(2, 2, 4, 2, -1, 2, 128, 128) for c in chunks]
        up = jnp.concatenate(ups, 4)
        up = up.transpose(2, 3, 7, 1, 0, 5, 4, 6).reshape(1024, 4096)
        downs = [jnp.stack([c[3], c[2]], 3).reshape(2, 2, 4, 2, -1, 128, 256) for c in chunks]
        down = jnp.concatenate(downs, 4)
        down = down.transpose(2, 3, 4, 5, 0, 1, 6).reshape(4096, 1024)

        def square(pair, y_first):
            both = jnp.stack([pair[1], pair[0]], 3)
            order = (2, 3, 4, 5, 0, 1, 6) if y_first else (2, 3, 4, 5, 1, 0, 6)
            return both.transpose(order).reshape(1024, 4, 256)

        w_out_full = square(out_pair, False).reshape(1024, 1024)
        qkv = jnp.stack([square(p, j != 1) for j, p in enumerate(qkv_pairs)], 2)
        w_up_grad, w_down_grad = scatter(up), scatter(down)
        w_out_grad, w_qkv_grad = scatter(w_out_full), scatter(qkv.reshape(1024, 3072))

    shape = hidden_in.shape
    return (
        result.reshape(shape),
        grad_input.reshape(shape),
        shares[0],
        shares[1],
        shares[2],
        shares[3],
        w_qkv_grad,
        shares[4],
        w_out_grad,
        shares[5],
        w_up_grad,
        shares[6],
        w_down_grad,
        shares[5],
        shares[7],
    )


def solution(mesh):
    links = Links(mesh)
    rows = P("batch", "seq", None)
    spread = P("seq", "batch")
    return jax.shard_map(
        functools.partial(per_device, links),
        mesh=mesh,
        in_specs=(rows, rows, P("batch"), P("batch", "seq")) + (P(),) * 14,
        out_specs=(rows, rows)
        + (P("seq"),) * 4
        + (spread, P("seq"), spread, P("seq"), spread, P("seq"), spread, P("seq"), P("seq")),
        check_vma=False,
    )
```

```python
import functools
import math

import jax
import jax.numpy as jnp
import numpy as np
from jax import lax
from jax.experimental import pallas as pl
from jax.experimental.pallas import tpu as pltpu
from jax.sharding import PartitionSpec as P

f32 = jnp.float32
bf16 = jnp.bfloat16
struct = jax.ShapeDtypeStruct
HEADS = 16
HEAD_DIM = 64
ROT = 16
LEN_BLK = 256
ROW_TILE = 256
HG = 256
ROOT_HALF = math.sqrt(0.5)
NORMAL_PEAK = 1.0 / math.sqrt(2.0 * math.pi)
norm_epsilon = 1e-05
rope_base = 10000.0
VMEM_BYTES = 60 * 1024 * 1024


def params():
    return pltpu.CompilerParams(vmem_limit_bytes=VMEM_BYTES)


def dot(a, b, ca, cb):
    return lax.dot_general(a, b, (((ca,), (cb,)), ((), ())), preferred_element_type=f32)


def iota(shape, dim):
    return lax.broadcasted_iota(jnp.int32, shape, dim)


def split(x):
    hi = x.astype(bf16)
    return hi, (x - hi.astype(f32)).astype(bf16)


def ordered_call(kernel, args, after, *, in_specs, grid, out_specs, out_shape, prefetch=0, **kw):
    after = [a for a in after if a is not None]
    n_in = len(args)

    def body(*refs):
        kernel(*refs[:n_in], *refs[n_in + len(after) :])

    in_specs = list(in_specs) + [pl.BlockSpec(memory_space=pl.ANY)] * len(after)
    return pl.pallas_call(
        body,
        grid_spec=pltpu.PrefetchScalarGridSpec(
            num_scalar_prefetch=prefetch, grid=grid, in_specs=in_specs, out_specs=out_specs
        ),
        out_shape=out_shape,
        compiler_params=params(),
        **kw,
    )(*args, *after)


def ffn_kernel(aliased, pos, a2_own, a2_other, g_own, g_other, *refs):
    w_ups, w_downs, biases = refs[:2], refs[2:4], refs[4:6]
    refs = refs[6 + aliased :]
    gelus, grads, (up_send, up_keep, down_send, down_keep, b_sum) = refs[:2], refs[2:4], refs[4:]
    me = pos[0]
    w_up = jnp.concatenate([w[...] for w in w_ups], axis=1)
    w_down = jnp.concatenate([w[...] for w in w_downs], axis=0)
    bias = jnp.concatenate([b[...] for b in biases], axis=1)
    d_up = d_down = total = None
    for half, (a2, g) in enumerate(((a2_own, g_own), (a2_other, g_other))):
        rows_in, grad_in = a2[...], g[...]
        pre = dot(rows_in, w_up, 1, 0) + bias
        grad_gelu = dot(grad_in, w_down, 1, 1)
        cdf = 0.5 + 0.5 * lax.erf(pre * ROOT_HALF)
        gelu = (pre * cdf).astype(bf16)
        slope = cdf + pre * (NORMAL_PEAK * jnp.exp(-0.5 * pre * pre))
        grad_pre = (grad_gelu * slope).astype(bf16)
        for j in range(2):
            gelus[j][half, 0] = gelu[:, 128 * j : 128 * j + 128]
            grads[j][half, 0] = grad_pre[:, 128 * j : 128 * j + 128]
        parts = (
            dot(grad_pre, rows_in, 0, 0),
            dot(gelu, grad_in, 0, 0),
            jnp.sum(grad_pre.astype(f32), axis=0, keepdims=True),
        )
        if half == 0:
            d_up, d_down, total = parts
        else:
            d_up, d_down, total = d_up + parts[0], d_down + parts[1], total + parts[2]
    b_sum[0] = total
    mx = lax.rem(me, 2)
    keep, send = swapped(mx, d_up[:128], d_up[128:])
    for n in range(8):
        up_send[0, n // 2, n % 2] = send[:, n * 128 : (n + 1) * 128]
        up_keep[0, n // 2, n % 2] = keep[:, n * 128 : (n + 1) * 128]
    for j in range(2):
        squares = relative(d_down[128 * j : 128 * j + 128], me)
        for rx in range(2):
            for half in range(2):
                part = slice(128 * half, 128 * half + 128)
                down_send[rx, j, half] = squares[rx][1][:, part]
                down_keep[rx, j, half] = squares[rx][0][:, part]


def swapped(bit, first, second):
    return jnp.where(bit == 0, first, second), jnp.where(bit == 0, second, first)


def relative(tile, me):
    by_y = swapped(lax.div(me, 2), tile[:, :512], tile[:, 512:])
    by_yx = [swapped(lax.rem(me, 2), part[:, :256], part[:, 256:]) for part in by_y]
    return [[by_yx[y][x] for y in range(2)] for x in range(2)]


def once(shape, where):
    return pl.BlockSpec(shape, where, pipeline_mode=pl.Buffered(1))


def ffn_chunk(first, count, pos, a2, g, w_up, w_down, b_up, earlier=(), filled=(), more=0, after=()):
    rows, width = a2[0].shape
    block = lambda j, k, i, p: (2 * (2 * i + j) + p[1]) * 4 + first + k
    cols = lambda j: (lambda k, i, p: (0, block(j, k, i, p)))
    lines = lambda j: (lambda k, i, p: (block(j, k, i, p), 0))
    whole = lambda k, i, p: (0, 0)
    place = lambda k, i, p: (0, i * 4 + first + k, 0, 0)
    in_specs = (
        [once((rows, width), whole)] * 4
        + [pl.BlockSpec((width, 128), cols(j)) for j in range(2)]
        + [pl.BlockSpec((128, width), lines(j)) for j in range(2)]
        + [pl.BlockSpec((1, 128), cols(j)) for j in range(2)]
    )
    args = [pos, *a2, *g, w_up, w_up, w_down, w_down, b_up, b_up]
    given = [*enumerate(earlier), *enumerate(filled, 4)]
    aliases = {len(args) + i: out for i, (out, _) in enumerate(given)}
    in_specs = in_specs + [pl.BlockSpec(memory_space=pl.ANY)] * len(given)
    args = args + [value for _, value in given]
    pieces = [struct((2, 4, 2 * count + extra, 128, 128), f32) for extra in (more, 0)] * 2
    pieces = [struct(v.shape, f32) for v in filled] or pieces
    skip = 1 if filled else 0
    return ordered_call(
        functools.partial(ffn_kernel, len(given)),
        args,
        after,
        prefetch=1,
        grid=(count, 2),
        in_specs=in_specs,
        out_specs=[pl.BlockSpec((2, 1, rows, 128), place)] * 4
        + [
            pl.BlockSpec(
                (1, 4, 2, 128, 128),
                lambda k, i, p, n=n: (lax.bitwise_xor(i, lax.div(p[0], 2)), 0, k + n, 0, 0),
            )
            for n in (skip, 0)
        ]
        + [
            pl.BlockSpec((2, 2, 2, 128, 128), lambda k, i, p, n=n: (0, i, k + n, 0, 0))
            for n in (skip, 0)
        ]
        + [pl.BlockSpec((1, 1, 256), lambda k, i, p: (k * 2 + i, 0, 0))],
        out_shape=[struct((2, 8, rows, 128), bf16)] * 4
        + pieces
        + [struct((count * 2, 1, 256), f32)],
        input_output_aliases=aliases,
        cost_estimate=cost(f"ffn{first}"),
        name="ffn_chunk",
    )


def out_grad_kernel(pos, own, early, late, g_own, g_other, x_send, x_keep, y_send, y_keep):
    other = jnp.where(pl.program_id(0) < 2, early[...], late[...]).astype(bf16)
    tile = dot(own[...], g_own[...], 0, 0) + dot(other, g_other[...], 0, 0)
    squares = relative(tile, pos[0])
    for n in range(2):
        x_send[n, 0, 0] = squares[1][n][:, :128]
        x_keep[n, 0, 0] = squares[0][n][:, :128]
        y_send[n, 0, 0] = squares[n][1][:, 128:]
        y_keep[n, 0, 0] = squares[n][0][:, 128:]


def out_grad(pos, mixed, others, g, after=()):
    rows, width = g[0].shape
    whole = lambda z, p: (0, 0)
    return ordered_call(
        out_grad_kernel,
        [pos, mixed, *others, *g],
        after,
        prefetch=1,
        grid=(4,),
        in_specs=[
            pl.BlockSpec((rows, 128), lambda z, p: (0, 2 * z + p[1])),
            pl.BlockSpec((rows, 128), lambda z, p: (0, lax.min(z, 1))),
            pl.BlockSpec((rows, 128), lambda z, p: (0, lax.max(z - 2, 0))),
            once((rows, width), whole),
            once((rows, width), whole),
        ],
        out_specs=[
            pl.BlockSpec((2, 1, 1, 128, 128), lambda z, p: (0, z, 4, 0, 0)),
            pl.BlockSpec((2, 1, 1, 128, 128), lambda z, p: (0, z, 2, 0, 0)),
        ]
        * 2,
        out_shape=[struct((2, 4, 5, 128, 128), f32), struct((2, 4, 3, 128, 128), f32)] * 2,
        cost_estimate=cost("out_grad"),
        name="out_grad",
    )


def second_kernel(at, slots, u_keep, u_one, d_keep, d_one, *refs):
    x_o, y_o = refs[-2:]
    own = slice(at, at + slots)
    y_o[...] = (u_keep[...] + u_one[:, :, own]).reshape(y_o.shape)
    x_o[...] = (d_keep[...] + d_one[:, :, own]).reshape(x_o.shape)


def second_stage(keeps, ones, at, bundles=None, into=0):
    slots, total = keeps[0].shape[2], ones[0].shape[2]
    half = slots // 2
    keep = pl.BlockSpec((1, 2, slots, 128, 128), lambda i: (1, i, 0, 0, 0))
    one = pl.BlockSpec((1, 2, total, 128, 128), lambda i: (1, i, 0, 0, 0))
    if bundles:
        out = pl.BlockSpec((1, 4, half, 128, 128), lambda i: (i, 0, into // half, 0, 0))
        shapes = [struct(v.shape, f32) for v in bundles]
    else:
        out = pl.BlockSpec((2, slots, 128, 128), lambda i: (i, 0, 0, 0))
        shapes = [struct((4, slots, 128, 128), f32)] * 2
    return ordered_call(
        functools.partial(second_kernel, at, slots),
        [keeps[0], ones[0], keeps[1], ones[1], *(bundles or [])],
        [],
        grid=(2,),
        in_specs=[keep, one] * 2 + [pl.BlockSpec(memory_space=pl.ANY)] * len(bundles or []),
        out_specs=[out] * 2,
        out_shape=shapes,
        input_output_aliases={4: 0, 5: 1} if bundles else {},
        cost_estimate=cost("second_stage"),
        name="second_stage",
    )


def finish_kernel(at, slots, cut, u_keep, u_one, u_two, d_keep, d_one, d_two, out):
    own = slice(at, at + slots)
    for n, (keep, one, two) in enumerate(((u_keep, u_one, u_two), (d_keep, d_one, d_two))):
        if cut is None:
            second = two[...]
        else:
            second = two[0, :, cut[0] : cut[1]].reshape(2, slots, 128, 128)
        out[:, n * slots : (n + 1) * slots] = keep[0] + one[0, :, own] + second


def finish(keeps, ones, at, twos, cut):
    slots, total = keeps[0].shape[2], ones[0].shape[2]
    keep = pl.BlockSpec((1, 2, slots, 128, 128), lambda i: (0, i, 0, 0, 0))
    one = pl.BlockSpec((1, 2, total, 128, 128), lambda i: (0, i, 0, 0, 0))
    if cut is None:
        two = pl.BlockSpec((2, slots, 128, 128), lambda i: (i, 0, 0, 0))
    else:
        two = pl.BlockSpec((1, 4, twos[0].shape[2], 128, 128), lambda i: (i, 0, 0, 0, 0))
    return ordered_call(
        functools.partial(finish_kernel, at, slots, cut),
        [keeps[0], ones[0], twos[0], keeps[1], ones[1], twos[1]],
        [],
        grid=(2,),
        in_specs=[keep, one, two] * 2,
        out_specs=pl.BlockSpec((2, 2 * slots, 128, 128), lambda i: (i, 0, 0, 0)),
        out_shape=struct((4, 2 * slots, 128, 128), f32),
        cost_estimate=cost("finish"),
        name="finish",
    )


def qkv_grad_kernel(pos, a1_own, a1_other, *refs):
    own, other, (x_send, x_keep, y_send, y_keep) = refs[:3], refs[3:12], refs[12:]
    left = jnp.concatenate([r[0] for r in own], 1)
    left_other = []
    for j in range(3):
        part = lax.div(lax.bitwise_xor(pl.program_id(0), pos[0]) * 3 + j, 4)
        parts = [r[...] for r in other[3 * j : 3 * j + 3]]
        chosen = jnp.where(part == 0, parts[0], jnp.where(part == 1, parts[1], parts[2]))
        left_other.append(chosen.astype(bf16))
    left_other = jnp.concatenate(left_other, 1)
    tile = dot(left, a1_own[...], 0, 0) + dot(left_other, a1_other[...], 0, 0)
    step = pl.program_id(0)
    block = lambda j, n: tile[128 * j : 128 * j + 128, n * 128 : (n + 1) * 128]

    def put(out, whole, half):
        for z in range(4):
            out[0, z, 0] = block(whole, 2 * z)
            out[0, z, 1] = block(whole, 2 * z + 1)
            out[0, z, 2] = block(2, 2 * z + half)

    pl.when(lax.rem(step, 2) == 1)(lambda: put(x_send, 0, 0))
    pl.when(lax.rem(step, 2) == 0)(lambda: put(x_keep, 0, 0))
    pl.when(step >= 2)(lambda: put(y_send, 1, 1))
    pl.when(step < 2)(lambda: put(y_keep, 1, 1))


def qkv_grad(pos, a1, grad_proj, other, after=()):
    rows, width = a1[0].shape
    whole = lambda n, p: (0, 0)

    def source(j):
        def where(n, p):
            unit = lax.bitwise_xor(n, p[0]) * 3 + j
            return (lax.div(unit, 4), 0, lax.rem(unit, 4) * 2 + p[1])

        return where

    def other_place(j, part):
        if part != j:
            return lambda n, p: (0, [u % 4 for u in range(j, 12, 3) if u // 4 == part][0])
        return lambda n, p: (0, lax.select(lax.bitwise_xor(n, p[0]) <= j, 0 * n, 0 * n + 3))

    out = lambda at: pl.BlockSpec((1, 4, 3, 128, 128), lambda n, p: (at(n), 0, 0, 0, 0))
    return ordered_call(
        qkv_grad_kernel,
        [pos, *a1] + [grad_proj] * 3 + [part for _ in range(3) for part in other],
        after,
        prefetch=1,
        grid=(4,),
        in_specs=[once((rows, width), whole)] * 2
        + [pl.BlockSpec((1, rows, 128), source(j)) for j in range(3)]
        + [pl.BlockSpec((rows, 128), other_place(j, part)) for j in range(3) for part in range(3)],
        out_specs=[
            out(lambda n: lax.div(n, 2)),
            out(lambda n: lax.div(n, 2)),
            out(lambda n: lax.max(n - 2, 0)),
            out(lambda n: lax.min(n, 1)),
        ],
        out_shape=[struct((2, 4, 3, 128, 128), f32)] * 4,
        cost_estimate=cost("qkv_grad"),
        name="qkv_grad",
    )


LONG, SHORT = 10**11, 1
WEIGHTS = {"first_norm": LONG, "hidden0": LONG, "blocks": LONG}


def cost(name):
    flops = WEIGHTS.get(name, SHORT)
    return pl.CostEstimate(flops=flops, bytes_accessed=1, transcendentals=0)


def rotate(x, cos, sin_first, sin_second):
    n = x.shape[1]
    half = ROT // 2
    return x * cos + pltpu.roll(x, n - half, 1) * sin_first + pltpu.roll(x, half, 1) * sin_second


def three(x, w_hi, w_lo):
    hi, lo = split(x)
    return dot(hi, w_hi, 1, 0) + dot(lo, w_hi, 1, 0) + dot(hi, w_lo, 1, 0)


def pair_mask():
    return (iota((128, 128), 0) // 64) == (iota((128, 128), 1) // 64)


def pack(first, second):
    mask = pair_mask()
    first = jnp.where(mask, first, 0.0)
    second = jnp.where(mask, second, 0.0)
    first = first + pltpu.roll(first, 64, 1)
    second = second + pltpu.roll(second, 64, 1)
    return jnp.where(iota((128, 128), 1) < 64, first, second)


def unpack(packed):
    mask = pair_mask()
    low = iota((128, 128), 1) < 64
    turned = pltpu.roll(packed, 64, 1)
    return (
        jnp.where(mask, jnp.where(low, packed, turned), 0.0),
        jnp.where(mask, jnp.where(low, turned, packed), 0.0),
    )


def to_column(row):
    eye = iota((128, 128), 0) == iota((128, 128), 1)
    return jnp.sum(jnp.where(eye, jnp.broadcast_to(row, (128, 128)), 0.0), axis=1, keepdims=True)


def each_head(x):
    mask = iota((1, 128), 1) < 64
    zero = jnp.zeros_like(x)
    return jnp.where(mask, x, zero), jnp.where(mask, zero, x)


def feature_kernel(
    a1, wq, wk, wv, bq, bk, bv, fw, matrix, cos, sin1, sin2, valid, qf_o, kf_o, v_o, st_o
):
    x = a1[...]
    count = x.shape[0] // LEN_BLK
    rows = lambda i: slice(LEN_BLK * i, LEN_BLK * (i + 1))
    turns = cos[...], sin1[...], sin2[...]
    weight = fw[...]
    halves = split(matrix[...])
    q = [dot(x[rows(i)], wq[...], 1, 0) for i in range(count)]
    k = [dot(x[rows(i)], wk[...], 1, 0) for i in range(count)]
    q = [rotate(part + bq[...], *turns) for part in q]
    v = [(dot(x[rows(i)], wv[...], 1, 0) + bv[...]).astype(bf16) for i in range(count)]
    k = [rotate(part + bk[...], *turns) for part in k]
    q = [three(part, *halves) for part in q]
    k = [three(part, *halves) for part in k]
    for i in range(count):
        qf_o[rows(i)] = (weight * jnp.exp(q[i])).astype(bf16)
        kf = (weight * jnp.exp(k[i])).astype(bf16) * valid[rows(i)].astype(bf16)
        kf_o[rows(i)] = kf
        k[i] = kf
        v_o[rows(i)] = v[i]
    for i in range(count):
        state = [
            dot(k[i][:, 128 * p : 128 * p + 128], v[i][:, 128 * p : 128 * p + 128], 0, 0)
            for p in range(2)
        ]
        st_o[i, 0, :128] = pack(state[0], state[1])
        norm = jnp.sum(k[i].astype(f32), axis=0, keepdims=True)
        st_o[i, 0, 128:] = norm_rows(norm[:, :128], norm[:, 128:])


def norm_rows(first, second):
    line = iota((8, 128), 0)
    return jnp.where(line == 0, first, jnp.where(line == 1, second, 0.0))


def scores(qp, kp, causal):
    raw = dot(jnp.concatenate(each_head(qp), 0), kp, 1, 1)
    return [
        jnp.where(causal, raw[LEN_BLK * h : LEN_BLK * (h + 1)], 0.0).astype(bf16)
        for h in range(2)
    ]


def lower(n):
    return iota((n, n), 0) >= iota((n, n), 1)


def mix_kernel(pos, g, wo, qf, kf, v, st, mix_o, dn_o, dd_o, ds_o, *sends):
    count = qf.shape[0] // LEN_BLK
    mask = pair_mask()
    lane = iota((1, 128), 1)
    first = lane < 64
    causal = lower(LEN_BLK)
    one0, one1 = each_head(jnp.ones((LEN_BLK, 128), bf16))
    cells = [(i, p) for i in range(count) for p in range(2)]
    rows = lambda i: slice(LEN_BLK * i, LEN_BLK * (i + 1))
    cols = lambda p: slice(128 * p, 128 * p + 128)
    q = {(i, p): qf[rows(i), cols(p)] for i, p in cells}
    s = {(i, p): scores(q[i, p], kf[rows(i), cols(p)], causal) for i, p in cells}
    grad_mixed = dot(g[...], wo[...], 1, 1)
    both = {}
    for i in range(count):
        state = unpack(st[i, 0, :128])
        for p in range(2):
            column = to_column(st[i, 0, 128 + p : 129 + p])
            norm = jnp.where(mask, jnp.broadcast_to(column, (128, 128)), 0.0)
            hi, lo = split(jnp.concatenate([state[p], norm], 1))
            qp = q[i, p]
            both[i, p] = dot(jnp.concatenate([qp, qp], 1), jnp.concatenate([hi, lo], 0), 1, 0)
    for i, p in cells:
        v0, v1 = each_head(v[rows(i), cols(p)])
        right = jnp.concatenate(
            [jnp.concatenate([v0, one0], 1), jnp.concatenate([v1, one1], 1)], 0
        )
        both[i, p] = both[i, p] + dot(jnp.concatenate(s[i, p], 1), right, 1, 0)
    mixes, dns, norms, grads, sums = {}, {}, {}, {}, {}
    for i, p in cells:
        inverse = 1.0 / both[i, p][:, 128:]
        mixed = both[i, p][:, :128] * inverse
        low = mixed.astype(bf16)
        mix_o[rows(i), cols(p)] = low
        mixes[i, p] = low
        dn = (grad_mixed[rows(i), cols(p)] * inverse).astype(bf16)
        dn_o[rows(i), cols(p)] = dn
        dns[i, p] = dn
        product = -(dn.astype(f32) * mixed)
        d0 = jnp.sum(jnp.where(first, product, 0.0), axis=1, keepdims=True)
        d1 = jnp.sum(jnp.where(first, 0.0, product), axis=1, keepdims=True)
        sums[i, p] = d0, d1
    for i, p in cells:
        grads[i, p] = dot(q[i, p], dns[i, p], 0, 0)
    for i, p in cells:
        d0, d1 = sums[i, p]
        norms[i, p] = column_sum(q[i, p].astype(f32) * jnp.where(first, d0, d1))
    for i in range(count):
        lines = jnp.zeros((LEN_BLK, 128), f32)
        for p in range(2):
            d0, d1 = sums[i, p]
            lines = jnp.where(lane == 2 * p, d0, jnp.where(lane == 2 * p + 1, d1, lines))
        dd_o[0, rows(i)] = lines
        ds_o[i, 0, :128] = pack(grads[i, 0], grads[i, 1])
        ds_o[i, 0, 128:] = norm_rows(norms[i, 0], norms[i, 1])
        other_half = jnp.where(pos[1] == 0, mixes[i, 1].astype(f32), mixes[i, 0].astype(f32))

        def put(out, lines=rows(i), other_half=other_half):
            out[lines] = other_half

        for n, out in enumerate(sends):
            pl.when(lax.div(pl.program_id(0), 2) == n)(functools.partial(put, out))


def back_kernel(
    pos, qf, kf, v, dn, dd, st, ds, fw, matrix, cos, sin1, sin2, gp_o, bias_o, fw_o, *sends
):
    count = qf.shape[0] // LEN_BLK
    step = pl.program_id(1)
    causal = lower(LEN_BLK)
    lane = iota((1, 128), 1)
    first = lane < 64
    turns = cos[...], -sin1[...], -sin2[...]
    halves = split(matrix[...])
    cells = [(i, p) for i in range(count) for p in range(2)]
    rows = lambda i: slice(LEN_BLK * i, LEN_BLK * (i + 1))
    cols = lambda p: slice(128 * p, 128 * p + 128)
    q, k, vv, d, s, t, col = {}, {}, {}, {}, {}, {}, {}
    for i, p in cells:
        q[i, p], k[i, p] = qf[rows(i), cols(p)], kf[rows(i), cols(p)]
        vv[i, p], d[i, p] = v[rows(i), cols(p)], dn[rows(i), cols(p)]
        col[i, p] = [
            jnp.sum(jnp.where(lane == 2 * p + h, dd[0, rows(i)], 0.0), axis=1, keepdims=True)
            for h in range(2)
        ]
    for c in cells:
        s[c] = scores(q[c], k[c], causal)
        raw = dot(jnp.concatenate(each_head(d[c]), 0), vv[c], 1, 1)
        t[c] = [
            jnp.where(causal, raw[LEN_BLK * h : LEN_BLK * (h + 1)] + col[c][h], 0.0).astype(bf16)
            for h in range(2)
        ]
    dq, dk, dv = {}, {}, {}
    for i in range(count):
        state, later = unpack(st[i, 0, :128]), unpack(ds[i, 0, :128])
        for p in range(2):
            c = i, p
            s_hi, s_lo = split(state[p])
            d_hi, d_lo = split(later[p])
            twice = lambda x: jnp.concatenate([x, x], 1)
            dq[c] = dot(twice(d[c]), jnp.concatenate([s_hi, s_lo], 1), 1, 1)
            dk[c] = dot(twice(vv[c]), jnp.concatenate([d_hi, d_lo], 1), 1, 1)
            dv[c] = dot(twice(k[c]), jnp.concatenate([d_hi, d_lo], 0), 1, 0)
    for c in cells:
        dq[c] = dq[c] + dot(jnp.concatenate(t[c], 1), jnp.concatenate(each_head(k[c]), 0), 1, 0)
        dk[c] = dk[c] + dot(jnp.concatenate(t[c], 0), jnp.concatenate(each_head(q[c]), 0), 0, 0)
        dv[c] = dv[c] + dot(jnp.concatenate(s[c], 0), jnp.concatenate(each_head(d[c]), 0), 0, 0)
    for i, p in cells:
        c = i, p
        norm = jnp.where(first, *col[c]) * st[i, 0, 128 + p : 129 + p]
        dq[c] = (dq[c] + norm) * q[c].astype(f32)
        dk[c] = (dk[c] + ds[i, 0, 128 + p : 129 + p]) * k[c].astype(f32)
    whole = lambda parts: jnp.concatenate(
        [jnp.concatenate([parts[i, 0], parts[i, 1]], 1) for i in range(count)], 0
    )
    dq, dk, dv = whole(dq), whole(dk), whole(dv)
    tall = [jnp.concatenate([turn] * count, 0) for turn in turns]
    grads = (
        rotate(three(dq, *halves), *tall).astype(bf16),
        rotate(three(dk, *halves), *tall).astype(bf16),
        dv.astype(bf16),
    )
    for n in range(3):
        gp_o[n] = grads[n]
        wide = grads[n].astype(f32)
        other_half = jnp.where(pos[1] == 0, wide[:, 128:], wide[:, :128])
        sends[n][...] = other_half
    totals = [column_sum(part.astype(f32)) for part in grads]
    totals.append(column_sum(dq + dk) / fw[...])

    @pl.when(step == 0)
    def _():
        for n in range(3):
            bias_o[n] = totals[n]
        fw_o[...] = totals[3]

    @pl.when(step > 0)
    def _():
        for n in range(3):
            bias_o[n] = bias_o[n] + totals[n]
        fw_o[...] = fw_o[...] + totals[3]


def attention_specs(seqs, per, more=0):
    rows = LEN_BLK * per
    return dict(
        grid=(4, seqs // per),
        wide=pl.BlockSpec((rows, 1024), lambda h, g, *_: (g, 0)),
        head=pl.BlockSpec((rows, HG), lambda h, g, *_: (g, h)),
        state=pl.BlockSpec((per, 1, 136, 128), lambda h, g, *_: (g, h, 0, 0)),
        row=pl.BlockSpec((1, HG), lambda h, g, *_: (0, h)),
        table=pl.BlockSpec((256, 256), lambda h, g, *_: (0, 0)),
        dden=pl.BlockSpec((1, rows, 128), lambda h, g, *_: (h, g, 0)),
    )


def features(a1, w_qkv, b_qkv, feat_weight, matrix, turns, valid, after=(), per=4):
    rows = a1.shape[0]
    seqs = rows // LEN_BLK
    s = attention_specs(seqs, per)
    weights = [pl.BlockSpec((1024, HG), lambda h, g, o=o: (0, 4 * o + h)) for o in range(3)]
    biases = [pl.BlockSpec((1, HG), lambda h, g, o=o: (0, 4 * o + h)) for o in range(3)]
    return ordered_call(
        feature_kernel,
        [a1, w_qkv, w_qkv, w_qkv, b_qkv, b_qkv, b_qkv, feat_weight, matrix, *turns, valid],
        after,
        grid=s["grid"],
        in_specs=[s["wide"], *weights, *biases, s["row"]]
        + [s["table"]] * 4
        + [pl.BlockSpec((LEN_BLK * per, 1), lambda h, g: (g, 0))],
        out_specs=[s["head"]] * 3 + [s["state"]],
        out_shape=[struct((rows, 1024), bf16)] * 3 + [struct((seqs, 4, 136, 128), f32)],
        cost_estimate=cost("features"),
        name="features",
    )


def mixing(pos, g, w_out, qf, kf, v, state, after=(), per=2):
    rows = g.shape[0]
    seqs = rows // LEN_BLK
    steps = seqs // per
    s = attention_specs(seqs, per)
    return ordered_call(
        mix_kernel,
        [pos, g, w_out, qf, kf, v, state],
        after,
        prefetch=1,
        grid=s["grid"],
        in_specs=[s["wide"], pl.BlockSpec((HG, 1024), lambda h, g, *_: (h, 0))]
        + [s["head"]] * 3
        + [s["state"]],
        out_specs=[
            s["head"],
            s["head"],
            s["dden"],
            s["state"],
            pl.BlockSpec(
                (LEN_BLK * per, 128),
                lambda h, g, *_: (lax.select(h < 2, g, 0 * g + steps - 1), lax.min(h, 1)),
            ),
            pl.BlockSpec(
                (LEN_BLK * per, 128),
                lambda h, g, *_: (lax.select(h < 2, 0 * g, g), lax.max(h - 2, 0)),
            ),
        ],
        out_shape=[
            struct((rows, 1024), bf16),
            struct((rows, 1024), bf16),
            struct((4, rows, 128), f32),
            struct((seqs, 4, 136, 128), f32),
            struct((rows, 256), f32),
            struct((rows, 256), f32),
        ],
        cost_estimate=cost("mixing"),
        name="mixing",
    )

def backward(pos, qf, kf, v, dn, dd, state, later, feat_weight, matrix, turns, after=(), per=4):
    rows = qf.shape[0]
    seqs = rows // LEN_BLK
    s = attention_specs(seqs, per)
    return ordered_call(
        back_kernel,
        [pos, qf, kf, v, dn, dd, state, later, feat_weight, matrix, *turns],
        after,
        prefetch=1,
        grid=s["grid"],
        in_specs=[s["head"]] * 4
        + [s["dden"], s["state"], s["state"], s["row"]]
        + [s["table"]] * 4,
        out_specs=[
            pl.BlockSpec((3, LEN_BLK * per, HG), lambda h, g, *_: (0, g, h)),
            pl.BlockSpec((3, 1, HG), lambda h, g, *_: (0, 0, h)),
            s["row"],
        ]
        + [pl.BlockSpec((LEN_BLK * per, 128), lambda h, g, *_: (g, h))] * 3,
        out_shape=[
            struct((3, rows, 1024), bf16),
            struct((3, 1, 1024), f32),
            struct((1, 1024), f32),
        ]
        + [struct((rows, 512), f32)] * 3,
        cost_estimate=cost("backward"),
        name="backward",
    )


def norm_parts(x):
    centre = x - jnp.mean(x, axis=-1, keepdims=True)
    r = lax.rsqrt(jnp.mean(centre * centre, axis=-1, keepdims=True) + norm_epsilon)
    return centre * r, r


def norm_back(grad, xhat, r, gain):
    e = grad * gain
    return r * (
        e
        - jnp.mean(e, axis=-1, keepdims=True)
        - xhat * jnp.mean(e * xhat, axis=-1, keepdims=True)
    )


def add_sums(out, sums):
    step = pl.program_id(0)
    new = jnp.concatenate(sums, 0)

    @pl.when(step == 0)
    def _():
        out[...] = new

    @pl.when(step > 0)
    def _():
        out[...] = out[...] + new


def column_sum(x):
    return jnp.sum(x, axis=0, keepdims=True)


def tiles(tile, fixed):
    wide = lambda n: pl.BlockSpec((tile, n), lambda i, *_: (i, 0))
    keep = [once(a.shape, lambda i, *_: (0, 0)) for a in fixed]
    return wide, keep


def norms_kernel(x, g, gain1, bias1, gain2, bias2, a1_o, a2_o, g_o):
    xhat, _ = norm_parts(x[...].astype(f32))
    a1_o[...] = (xhat * gain1[...] + bias1[...]).astype(bf16)
    a2_o[...] = (xhat * gain2[...] + bias2[...]).astype(bf16)
    g_o[...] = g[...].astype(g_o.dtype)


def norms(x, g, *vectors, after=(), g_type=f32):
    rows, tile = x.shape[0], 256
    wide, keep = tiles(tile, vectors)
    return ordered_call(
        norms_kernel,
        [x, g, *vectors],
        after,
        grid=(rows // tile,),
        in_specs=[wide(1024)] * 2 + keep,
        out_specs=[wide(1024)] * 3,
        out_shape=[struct((rows, 1024), bf16)] * 2 + [struct((rows, 1024), g_type)],
        cost_estimate=cost("norms"),
        name="norms",
    )


def hidden_rows_kernel(grad, filled, pos, *refs):
    acts, weights, (send, keep) = refs[:2], refs[2:6], refs[6 + filled :]
    total = None
    for b in range(4):
        act = acts[b % 2]
        act = jnp.concatenate([act[0, 4 * (b // 2) + n] for n in range(4)], 1)
        part = dot(act, weights[b][...], 1, 1 if grad else 0)
        total = part if total is None else total + part
    step = pl.program_id(0)
    steps = pl.num_programs(0) // 2

    @pl.when(step < steps)
    def _():
        send[0] = total

    @pl.when(step >= steps)
    def _():
        keep[...] = total


def hidden_rows(pos, acts, weight, grad, sends=None, after=()):
    rows, tile = acts[0].shape[2], ROW_TILE
    steps = rows // tile
    act = pl.BlockSpec(
        (1, 8, tile, 128), lambda i, p: (1 - lax.div(i, steps), 0, lax.rem(i, steps), 0)
    )
    if grad:
        part = lambda b: once((1024, 512), lambda i, p: (0, 2 * b + p[1]))
    else:
        part = lambda b: once((512, 1024), lambda i, p: (2 * b + p[1], 0))
    filled = [] if sends is None else [sends]
    return ordered_call(
        functools.partial(hidden_rows_kernel, grad, len(filled)),
        [pos, *acts] + [weight] * 4 + filled,
        after,
        prefetch=1,
        grid=(2 * steps,),
        in_specs=[act] * 2
        + [part(b) for b in range(4)]
        + [pl.BlockSpec(memory_space=pl.ANY)] * len(filled),
        out_specs=[
            pl.BlockSpec((1, tile, 1024), lambda i, p: (int(grad), lax.min(i, steps - 1), 0)),
            pl.BlockSpec((tile, 1024), lambda i, p: (lax.max(i - steps, 0), 0)),
        ],
        out_shape=[struct((2, rows, 1024), f32), struct((rows, 1024), f32)],
        input_output_aliases={7: 0} if filled else {},
        cost_estimate=cost(f"hidden{grad:d}"),
        name="hidden_rows",
    )


def result_kernel(x, mixed, own, other, w_out, bias, res_o):
    out = dot(mixed[...], w_out[...], 1, 0) + (own[...] + other[0])
    res_o[...] = (x[...].astype(f32) + out + bias[...]).astype(bf16)


def result_rows(x, mixed, own, other, w_out, bias, after=()):
    rows, tile = x.shape[0], ROW_TILE
    fixed = (w_out, bias)
    wide, keep = tiles(tile, fixed)
    return ordered_call(
        result_kernel,
        [x, mixed, own, other, *fixed],
        after,
        grid=(rows // tile,),
        in_specs=[wide(1024)] * 3 + [pl.BlockSpec((1, tile, 1024), lambda i: (0, i, 0))] + keep,
        out_specs=wide(1024),
        out_shape=struct((rows, 1024), bf16),
        cost_estimate=cost("result_rows"),
        name="result_rows",
    )


def first_norm_kernel(x, g, gp, w_qkv, gain, part_o, sum_o):
    xhat, r = norm_parts(x[...].astype(f32))
    grad_res = g[...].astype(f32)
    grad = dot(jnp.concatenate([gp[0], gp[1], gp[2]], 1), w_qkv[...], 1, 1)
    part_o[...] = grad_res + norm_back(grad, xhat, r, gain[...])
    sums = [column_sum(v) for v in (grad * xhat, grad, grad_res)]
    add_sums(sum_o, sums + [jnp.zeros((5, 1024), f32)])


def first_norm(x, g, gp, w_qkv, gain, after=()):
    rows, tile = x.shape[0], ROW_TILE
    fixed = (w_qkv, gain)
    wide, keep = tiles(tile, fixed)
    return ordered_call(
        first_norm_kernel,
        [x, g, gp, *fixed],
        after,
        grid=(rows // tile,),
        in_specs=[wide(1024)] * 2 + [pl.BlockSpec((3, tile, 1024), lambda i: (0, i, 0))] + keep,
        out_specs=[wide(1024), pl.BlockSpec((8, 1024), lambda i: (0, 0))],
        out_shape=[struct((rows, 1024), f32), struct((8, 1024), f32)],
        cost_estimate=cost("first_norm"),
        name="first_norm",
    )


def second_norm_kernel(x, part, own, other, gain, out_o, sum_o):
    xhat, r = norm_parts(x[...].astype(f32))
    grad = own[...] + other[0]
    out_o[...] = part[...] + norm_back(grad, xhat, r, gain[...])
    sums = [column_sum(v) for v in (grad * xhat, grad)]
    add_sums(sum_o, sums + [jnp.zeros((6, 1024), f32)])


def second_norm(x, part, own, other, gain, after=()):
    rows, tile = x.shape[0], ROW_TILE
    wide, keep = tiles(tile, (gain,))
    return ordered_call(
        second_norm_kernel,
        [x, part, own, other, gain],
        after,
        grid=(rows // tile,),
        in_specs=[wide(1024)] * 3 + [pl.BlockSpec((1, tile, 1024), lambda i: (1, i, 0))] + keep,
        out_specs=[wide(1024), pl.BlockSpec((8, 1024), lambda i: (0, 0))],
        out_shape=[struct((rows, 1024), f32), struct((8, 1024), f32)],
        cost_estimate=cost("second_norm"),
        name="second_norm",
    )


class Links:
    def __init__(self, mesh):
        self.nb, self.ns = mesh.shape["batch"], mesh.shape["seq"]
        self.tuned = (self.nb, self.ns) == (4, 8)

    def send(self, value, move):
        pairs = []
        for b in range(self.nb):
            for s in range(self.ns):
                to = move(b, s)
                if to is not None:
                    pairs.append((b * self.ns + s, to[0] * self.ns + to[1]))
        return lax.ppermute(value, ("batch", "seq"), pairs)

    def core(self, value):
        return self.send(value, lambda b, s: (b, s ^ 1))

    def x(self, value):
        return self.send(value, lambda b, s: (b ^ 1, s))

    def y(self, value):
        return self.send(value, lambda b, s: (b ^ 2, s))

    def ring(self, value, by):
        s = lax.axis_index("seq")
        got = self.send(value, lambda b, s: (b, (s + by) % self.ns))
        kept = s >= by if by > 0 else s < self.ns + by
        return got, kept

    def shift(self, value, by):
        inside = lambda s: 0 <= s < self.ns
        return self.send(value, lambda b, s: (b, s + by) if inside(s + by) else None)


def hold(value, behind):
    behind = [b for b in behind if b is not None]
    return lax.optimization_barrier((value, *behind))[0] if behind else value


class Group:
    def __init__(self, links, x_send, x_keep, y_send, y_keep, at=0):
        self.links, self.at = links, at
        self.keeps = x_keep, y_keep
        self.slots = x_keep.shape[2]
        if links.tuned:
            self.ones = [links.x(x_send), links.y(y_send)]
            self.twos = None

    def arrived(self, *behind):
        self.ones = [hold(one, behind) for one in self.ones]

    def second(self):
        x_out, y_out = second_stage(self.keeps, self.ones, self.at)
        self.twos, self.cut = [self.links.y(y_out), self.links.x(x_out)], None
        return x_out

    def second_in(self, x_send, y_send, into):
        return second_stage(self.keeps, self.ones, self.at, (x_send, y_send), into)

    def second_with(self, group):
        total = group.ones[0].shape[2]
        self.twos = group.ones[::-1]
        self.cut = (0, group.at) if group.at else (group.slots, total)

    def done(self, *behind):
        twos = [hold(two, behind) for two in self.twos]
        return finish(self.keeps, self.ones, self.at, twos, self.cut)


def reduce_z(value):
    groups = [[0, 2, 4, 6], [1, 3, 5, 7]]
    return lax.psum_scatter(
        value, "seq", scatter_dimension=0, axis_index_groups=groups, tiled=True
    )[0]


class Carried:
    def __init__(self, links, state, reverse):
        self.links, self.state, self.reverse = links, state, reverse
        self.sign = -1 if reverse else 1
        self.mine = self.sum = None
        if links.tuned:
            self.core = lax.rem(lax.axis_index("seq"), 2)
            self.half = state.shape[0] // 2
            self.other = links.core(self.of_half(1 - self.core))

    def of_half(self, which):
        return lax.dynamic_slice_in_dim(self.state, which * self.half, self.half, 0)

    def near(self, *behind):
        if not self.links.tuned:
            return None
        self.other = hold(self.other, behind)
        self.mine = self.of_half(self.core) + self.other
        self.one, self.one_kept = self.links.ring(self.mine, self.sign * 2)
        return self.mine

    def far(self, *behind):
        if not self.links.tuned:
            return None
        self.one = jnp.where(self.one_kept, hold(self.one, behind), 0.0)
        self.sum = self.mine + self.one
        self.two, self.two_kept = self.links.ring(self.sum, self.sign * 4)
        return self.sum

    def done(self, *behind):
        links = self.links
        if not links.tuned:
            total, step = self.state, 1
            while step < links.ns:
                total = total + links.shift(total, self.sign * step)
                step *= 2
            return links.shift(total, self.sign)
        self.two = hold(self.two, behind)
        before = self.one + jnp.where(self.two_kept, self.two, 0.0)
        second = self.core == (0 if self.reverse else 1)
        here = before + jnp.where(second, self.other, 0.0)
        there = before + jnp.where(second, 0.0, self.of_half(self.core))
        rest = links.core(there)
        low = jnp.where(self.core == 0, here, rest)
        high = jnp.where(self.core == 0, rest, here)
        return jnp.concatenate([low, high], 0)


class Line:
    def __init__(self, links, value):
        self.z = lax.div(lax.axis_index("seq"), 2)
        self.value = value
        self.parts = []
        for by in (2, 1, 3):
            part = self.pick(lax.rem(self.z + by, 4))
            self.parts.append(links.send(part, lambda b, s: (b, (s + 2 * by) % 8)))

    def pick(self, at):
        return lax.dynamic_index_in_dim(self.value, at, 0, keepdims=False)

    def done(self, *behind):
        total = self.pick(self.z)
        for part in self.parts:
            total = total + hold(part, behind)
        return total


class Halves:
    def __init__(self, links, value):
        self.links = links
        self.z = lax.div(lax.axis_index("seq"), 2)
        both = value.reshape((2, 2) + value.shape[1:])
        low = lax.rem(self.z, 2)
        pick = lambda i: lax.dynamic_index_in_dim(both, i, 1, keepdims=False)
        self.kept = pick(low)
        self.one = links.send(pick(1 - low), lambda b, s: (b, s ^ 2))

    def stage_two(self, *behind):
        self.one = hold(self.one, behind)
        self.high = lax.div(self.z, 2)
        out = self.pick(1 - self.high)
        self.two = self.links.send(out, lambda b, s: (b, s ^ 4))
        return out

    def pick(self, i):
        at = lambda v: lax.dynamic_index_in_dim(v, i, 0, keepdims=False)
        return at(self.kept) + at(self.one)

    def done(self, *behind):
        self.two = hold(self.two, behind)
        return self.pick(self.high) + self.two


def plane_sum(links, rows):
    split_rows = rows.reshape((4, 2) + rows.shape[1:])
    core = lax.rem(lax.axis_index("seq"), 2)
    pick = lambda i: lax.dynamic_index_in_dim(split_rows, i, 1, keepdims=False)
    total = pick(core) + links.core(pick(1 - core))
    total = total + links.x(total)
    return total + links.y(total)


def dct_table(order):
    degree = np.arange(order, dtype=np.float64)[:, None]
    sample = np.arange(order, dtype=np.float64)[None, :]
    table = np.cos(math.pi * (sample + 0.5) * degree / order) * math.sqrt(2.0 / order)
    return np.where(degree == 0.0, table * math.sqrt(0.5), table).astype(np.float32)


def rotation_tables(positions):
    half = ROT // 2
    at = jnp.arange(HG, dtype=jnp.int32) % HEAD_DIM
    inverse = rope_base ** (-2.0 * (at % half).astype(f32) / ROT)
    angles = positions[:, None] * inverse[None, :]
    at = at[None, :]
    sin = jnp.sin(angles)
    return (
        jnp.where(at < ROT, jnp.cos(angles), 1.0),
        jnp.where(at < half, -sin, 0.0),
        jnp.where((at >= half) & (at < ROT), sin, 0.0),
    )


def head_blocks(directions, transposed):
    times = HG // HEAD_DIM
    left = jnp.tile(directions, (times, 1))
    right = np.tile(dct_table(HEAD_DIM), (1, times))
    dims = (((0,), (1,)), ((), ())) if transposed else (((1,), (0,)), ((), ()))
    args = (jnp.asarray(right), left) if transposed else (left, jnp.asarray(right))
    full = lax.dot_general(*args, dims, precision=lax.Precision.HIGHEST)
    block = np.arange(HG) // HEAD_DIM
    return jnp.where(block[:, None] == block[None, :], full, 0.0)


def blocks_kernel(left, right, out):
    full = lax.dot_general(
        left[...],
        right[...],
        (((1,), (0,)), ((), ())),
        precision=lax.Precision.HIGHEST,
        preferred_element_type=f32,
    )
    same = iota((HG, HG), 0) // HEAD_DIM == iota((HG, HG), 1) // HEAD_DIM
    out[...] = jnp.where(same, full, 0.0)


def head_blocks_after(directions, after):
    times = HG // HEAD_DIM
    left = jnp.tile(directions, (times, 1))
    right = jnp.asarray(np.tile(dct_table(HEAD_DIM), (1, times)))
    whole = lambda a: pl.BlockSpec(a.shape, lambda i: (0, 0))
    return ordered_call(
        blocks_kernel,
        [left, right],
        after,
        grid=(1,),
        in_specs=[whole(left), whole(right)],
        out_specs=pl.BlockSpec((HG, HG), lambda i: (0, 0)),
        out_shape=struct((HG, HG), f32),
        cost_estimate=cost("blocks"),
        name="head_blocks",
    )


def per_device(
    links,
    hidden_in,
    cotangent,
    lengths,
    key_mask,
    ln1_gain,
    ln1_bias,
    ln2_gain,
    ln2_bias,
    w_qkv,
    b_qkv,
    w_out,
    b_out,
    w_up,
    b_up,
    w_down,
    b_down,
    feat_weight,
    directions,
):
    seqs, block, width = hidden_in.shape
    rows = seqs * block
    tuned = links.tuned
    place = lax.axis_index("seq")
    me = lax.axis_index("batch") if tuned else 0 * place
    core = lax.rem(place, 2)
    pos = jnp.stack([me, core]).astype(jnp.int32)
    places = place * block + jnp.arange(block, dtype=jnp.int32)
    valid = (places[None, :] < lengths[:, None]) & ((key_mask == 1) | (places[None, :] == 0))
    valid = valid.astype(f32).reshape(rows, 1)
    x = hidden_in.reshape(rows, width)
    g = cotangent.reshape(rows, width)
    row = lambda v: v.reshape(1, -1)
    gains = row(ln1_gain), row(ln1_bias), row(ln2_gain), row(ln2_bias)
    x_other = links.core(x.astype(f32))
    a1, a2, g_wide = norms(x, g, *gains)
    g_other = links.core(g_wide)

    forth = head_blocks(directions, True)
    turns = rotation_tables(places.astype(f32))
    weights = row(feat_weight)

    qf, kf, v, state = features(a1, w_qkv, row(b_qkv), weights, forth, turns, valid)
    forward = Carried(links, state, False)
    a1_o, a2_o, g_o = norms(
        hold(x_other, [state]), hold(g_other, [state]), *gains, g_type=bf16, after=[state]
    )
    ffn = functools.partial(
        ffn_chunk,
        pos=pos,
        a2=(a2, a2_o),
        g=(g, g_o),
        w_up=w_up,
        w_down=w_down,
        b_up=row(b_up),
    )
    c0 = ffn(0, 1, after=[forward.near(a1_o)])
    g0 = Group(links, *c0[4:8])
    c1 = ffn(1, 2, earlier=c0[:4], more=1, after=[forward.far(c0[8])])
    first = list(c1[4:8])
    if tuned:
        g0.arrived(c1[8])
        first[0::2] = g0.second_in(*first[0::2], 4)
    g1 = Group(links, *first)
    state_in = forward.done(c1[8])
    mixed, dn, dd, state_grad, *mixed_send = mixing(
        pos, g, w_out, qf, kf, v, state_in, after=first[:1]
    )
    reverse = Carried(links, state_grad, True)
    mixed_other = [links.core(part) for part in mixed_send]
    back = head_blocks_after(directions, [mixed])
    held = [reverse.near(back)]
    out_pieces = out_grad(
        pos, mixed, [hold(part, [back]) for part in mixed_other], (g, g_o), after=held
    )
    c2 = ffn(3, 1, earlier=c1[:4], filled=out_pieces, after=[reverse.far(out_pieces[0])])
    first = list(c2[4:8])
    z0 = None
    if tuned:
        g1.arrived(c2[8])
        g0.second_with(g1)
        first[0::2] = g1.second_in(*first[0::2], 0)
        z0 = g0.done()
    g2 = Group(links, *first, at=2)
    state_later = reverse.done(c2[8])
    grad_proj, bias_qkv, grad_feat, *grad_send = backward(
        pos,
        qf,
        kf,
        v,
        dn,
        dd,
        state_in,
        state_later,
        weights,
        back,
        turns,
        after=[first[0], z0],
    )
    grad_other = [links.core(part) for part in grad_send]
    last_parts = qkv_grad(
        pos, (a1, a1_o), grad_proj, [hold(part, [grad_proj]) for part in grad_other]
    )
    g3 = Group(links, *last_parts)
    acts = c2[:4]
    held = [last_parts[0]]
    if tuned:
        g2.arrived(last_parts[0])
        g1.second_with(g2)
        z1 = g1.done()
        early = reduce_z(z0), reduce_z(z1)
        held = [z1, g2.second()]
    own_g = hidden_rows(pos, acts[2:], w_up, True, after=held)
    own_r = hidden_rows(pos, acts[:2], w_down, False, own_g[0], after=[own_g[1]])
    others = links.core(own_r[0])
    held = [own_r[1]]
    if tuned:
        g3.arrived(own_r[1])
        held = [g3.second()]
    partial, sums1 = first_norm(x, g, grad_proj, w_qkv, row(ln1_gain), after=held)
    held = [partial]
    if tuned:
        z2 = g2.done(partial)
        middle = Halves(links, z2)
        z3 = g3.done(partial)
        tail = Line(links, z3)
        held = [z2, z3]
    grad_input, sums2 = second_norm(
        x, partial, own_g[1], hold(others, [partial]), row(ln2_gain), after=held
    )
    if tuned:
        middle.stage_two(grad_input)
    result = result_rows(
        x,
        mixed,
        own_r[1],
        hold(others, [partial]),
        w_out,
        row(b_out + b_down),
        after=[grad_input],
    )

    half_up = jnp.concatenate([c[8].reshape(-1, 2, 2, 128) for c in (c0, c1, c2)], 0)
    half_up = half_up.transpose(1, 2, 0, 3).reshape(4, 1, 512)
    b_up_grad = jnp.where(core == np.arange(2)[None, :, None], half_up, 0.0).reshape(-1)
    vectors = [
        sums1[0],
        sums1[1],
        sums2[0],
        sums2[1],
        bias_qkv.reshape(-1),
        sums1[2],
        b_up_grad,
        grad_feat[0],
    ]
    if tuned:
        lines = jnp.concatenate([v_.reshape(8, -1, 128) for v_ in vectors], 1)
        lines = plane_sum(links, jnp.pad(lines, ((0, 0), (0, 3), (0, 0))))
        lines = Line(links, lines).done()
        shares, at = [], 0
        for v_ in vectors:
            n = v_.shape[0] // 1024
            shares.append(lines[at : at + n].reshape(-1))
            at += n
        tail = tail.done(lines)
        middle = middle.done(lines)
        sizes = (1, 2, 1)
        parts = [*early, middle]
        units = [v_[: 2 * n].reshape(n, 2, 128, 128) for v_, n in zip(parts, sizes)]
        halves = jnp.concatenate(units, 0).swapaxes(0, 1)
        start = (2, 4, 3)
        units = [v_[m : m + 2 * n].reshape(n, 2, 128, 128) for v_, n, m in zip(parts, sizes, start)]
        w_down_grad = jnp.concatenate(units, 0).transpose(0, 2, 1, 3).reshape(512, 256)
        w_out_grad = jnp.concatenate([middle[2], middle[5]], 1)
        blocks = [[tail[i] for i in (0, 3, 2)], [tail[i] for i in (1, 4, 5)]]
        blocks = jnp.stack([jnp.stack(b, 0) for b in blocks], 0)
        halves = jnp.concatenate([halves, blocks], 1)
        pick = lambda i: lax.dynamic_index_in_dim(halves, i, 0, keepdims=False)
        mine, other = pick(core), links.core(pick(1 - core))
        first, second = jnp.where(core == 0, mine, other), jnp.where(core == 0, other, mine)
        both = jnp.stack([first, second], 0)
        w_up_grad = both[:, :4].reshape(1024, 128).T
        w_qkv_grad = both[:, 4:].transpose(1, 0, 2, 3).reshape(768, 128).T
    else:
        total = lax.psum(jnp.concatenate(vectors), ("batch", "seq"))
        shares, at = [], 0
        for v_ in vectors:
            share = v_.shape[0] // links.ns
            shares.append(lax.dynamic_slice_in_dim(total, at + place * share, share, 0))
            at += v_.shape[0]

        def scatter(full):
            part = lax.psum_scatter(full, "batch", scatter_dimension=1, tiled=True)
            return lax.psum_scatter(part, "seq", scatter_dimension=0, tiled=True)

        def of_core(half, axis):
            zero = jnp.zeros_like(half)
            pair = jnp.where(core == 0, half, zero), jnp.where(core == 1, half, zero)
            return jnp.stack(pair, axis)

        both = lambda send, keep: jnp.stack([keep, send], 0)
        groups = (c0, c1, c2)
        slots = lambda pair, n, m, k: both(pair[0][:, :, m : m + n], pair[1][:, :, k : k + n])
        sizes = ((2, 0, 0), (4, 0, 0), (2, 2, 0))
        up = [slots(c[4:6], *size) for c, size in zip(groups, sizes)]
        up = jnp.concatenate(up, 3).reshape(2, 2, 4, 4, 2, 128, 128)
        up = of_core(up.transpose(2, 4, 6, 1, 0, 3, 5).reshape(1024, 4, 512), 2)
        down = [slots(c[6:8], *size) for c, size in zip(groups, sizes)]
        down = jnp.concatenate(down, 3).reshape(2, 2, 4, 4, 2, 128, 128)
        down = of_core(down.transpose(2, 3, 5, 0, 1, 4, 6).reshape(4, 512, 1024), 1)
        by_x = slots(out_pieces[:2], 1, 4, 2).swapaxes(0, 1)
        out = jnp.concatenate([by_x, slots(out_pieces[2:], 1, 4, 2)], 3)
        out = out.transpose(2, 4, 0, 1, 3, 5).reshape(4, 128, 1024)
        by_x = both(*last_parts[:2]).swapaxes(0, 1)
        by_y = both(*last_parts[2:])
        parts = [by_x[:, :, :, :2], by_y[:, :, :, :2]]
        parts.append(jnp.stack([by_x[:, :, :, 2], by_y[:, :, :, 2]], 3))
        qkv = [p.transpose(2, 3, 5, 0, 1, 4).reshape(1024, 4, 128) for p in parts]
        w_up_grad = scatter(up.reshape(1024, 4096))
        w_down_grad = scatter(down.reshape(4096, 1024))
        w_out_grad = scatter(of_core(out, 1).reshape(1024, 1024))
        w_qkv_grad = scatter(of_core(jnp.stack(qkv, 2), 3).reshape(1024, 3072))

    shape = hidden_in.shape
    return (
        result.reshape(shape),
        grad_input.reshape(shape),
        shares[0],
        shares[1],
        shares[2],
        shares[3],
        w_qkv_grad,
        shares[4],
        w_out_grad,
        shares[5],
        w_up_grad,
        shares[6],
        w_down_grad,
        shares[5],
        shares[7],
    )


def solution(mesh):
    links = Links(mesh)
    rows = P("batch", "seq", None)
    spread = P("seq", "batch")
    return jax.shard_map(
        functools.partial(per_device, links),
        mesh=mesh,
        in_specs=(rows, rows, P("batch"), P("batch", "seq")) + (P(),) * 14,
        out_specs=(rows, rows)
        + (P("seq"),) * 4
        + (spread, P("seq"), spread, P("seq"), spread, P("seq"), spread, P("seq"), P("seq")),
        check_vma=False,
    )
```

```python
import functools
import math

import jax
import jax.numpy as jnp
import numpy as np
from jax import lax
from jax.experimental import pallas as pl
from jax.experimental.pallas import tpu as pltpu
from jax.sharding import PartitionSpec as P

f32 = jnp.float32
bf16 = jnp.bfloat16
struct = jax.ShapeDtypeStruct
HEADS = 16
HEAD_DIM = 64
ROT = 16
LEN_BLK = 256
ROW_TILE = 256
HG = 256
ROOT_HALF = math.sqrt(0.5)
NORMAL_PEAK = 1.0 / math.sqrt(2.0 * math.pi)
norm_epsilon = 1e-05
rope_base = 10000.0
VMEM_BYTES = 60 * 1024 * 1024


def params():
    return pltpu.CompilerParams(vmem_limit_bytes=VMEM_BYTES)


def dot(a, b, ca, cb):
    return lax.dot_general(a, b, (((ca,), (cb,)), ((), ())), preferred_element_type=f32)


def iota(shape, dim):
    return lax.broadcasted_iota(jnp.int32, shape, dim)


def split(x):
    hi = x.astype(bf16)
    return hi, (x - hi.astype(f32)).astype(bf16)


def ordered_call(kernel, args, after, *, in_specs, grid, out_specs, out_shape, prefetch=0, **kw):
    after = [a for a in after if a is not None]
    n_in = len(args)

    def body(*refs):
        kernel(*refs[:n_in], *refs[n_in + len(after) :])

    in_specs = list(in_specs) + [pl.BlockSpec(memory_space=pl.ANY)] * len(after)
    return pl.pallas_call(
        body,
        grid_spec=pltpu.PrefetchScalarGridSpec(
            num_scalar_prefetch=prefetch, grid=grid, in_specs=in_specs, out_specs=out_specs
        ),
        out_shape=out_shape,
        compiler_params=params(),
        **kw,
    )(*args, *after)


def ffn_kernel(aliased, pos, a2_own, a2_other, g_own, g_other, *refs):
    w_ups, w_downs, biases = refs[:2], refs[2:4], refs[4:6]
    refs = refs[6 + aliased :]
    gelus, grads, (up_send, up_keep, down_send, down_keep, b_sum) = refs[:2], refs[2:4], refs[4:]
    me = pos[0]
    w_up = jnp.concatenate([w[...] for w in w_ups], axis=1)
    w_down = jnp.concatenate([w[...] for w in w_downs], axis=0)
    bias = jnp.concatenate([b[...] for b in biases], axis=1)
    d_up = d_down = total = None
    for half, (a2, g) in enumerate(((a2_own, g_own), (a2_other, g_other))):
        rows_in, grad_in = a2[...], g[...]
        pre = dot(rows_in, w_up, 1, 0) + bias
        grad_gelu = dot(grad_in, w_down, 1, 1)
        cdf = 0.5 + 0.5 * lax.erf(pre * ROOT_HALF)
        gelu = (pre * cdf).astype(bf16)
        slope = cdf + pre * (NORMAL_PEAK * jnp.exp(-0.5 * pre * pre))
        grad_pre = (grad_gelu * slope).astype(bf16)
        for j in range(2):
            gelus[j][half, 0] = gelu[:, 128 * j : 128 * j + 128]
            grads[j][half, 0] = grad_pre[:, 128 * j : 128 * j + 128]
        parts = (
            dot(grad_pre, rows_in, 0, 0),
            dot(gelu, grad_in, 0, 0),
            jnp.sum(grad_pre.astype(f32), axis=0, keepdims=True),
        )
        if half == 0:
            d_up, d_down, total = parts
        else:
            d_up, d_down, total = d_up + parts[0], d_down + parts[1], total + parts[2]
    b_sum[0] = total
    mx = lax.rem(me, 2)
    keep, send = swapped(mx, d_up[:128], d_up[128:])
    for n in range(8):
        up_send[0, n // 2, n % 2] = send[:, n * 128 : (n + 1) * 128]
        up_keep[0, n // 2, n % 2] = keep[:, n * 128 : (n + 1) * 128]
    for j in range(2):
        squares = relative(d_down[128 * j : 128 * j + 128], me)
        for rx in range(2):
            for half in range(2):
                part = slice(128 * half, 128 * half + 128)
                down_send[rx, j, half] = squares[rx][1][:, part]
                down_keep[rx, j, half] = squares[rx][0][:, part]


def swapped(bit, first, second):
    return jnp.where(bit == 0, first, second), jnp.where(bit == 0, second, first)


def relative(tile, me):
    by_y = swapped(lax.div(me, 2), tile[:, :512], tile[:, 512:])
    by_yx = [swapped(lax.rem(me, 2), part[:, :256], part[:, 256:]) for part in by_y]
    return [[by_yx[y][x] for y in range(2)] for x in range(2)]


def once(shape, where):
    return pl.BlockSpec(shape, where, pipeline_mode=pl.Buffered(1))


def ffn_chunk(first, count, pos, a2, g, w_up, w_down, b_up, earlier=(), filled=(), more=0, after=()):
    rows, width = a2[0].shape
    block = lambda j, k, i, p: (2 * (2 * i + j) + p[1]) * 4 + first + k
    cols = lambda j: (lambda k, i, p: (0, block(j, k, i, p)))
    lines = lambda j: (lambda k, i, p: (block(j, k, i, p), 0))
    whole = lambda k, i, p: (0, 0)
    place = lambda k, i, p: (0, i * 4 + first + k, 0, 0)
    in_specs = (
        [once((rows, width), whole)] * 4
        + [pl.BlockSpec((width, 128), cols(j)) for j in range(2)]
        + [pl.BlockSpec((128, width), lines(j)) for j in range(2)]
        + [pl.BlockSpec((1, 128), cols(j)) for j in range(2)]
    )
    args = [pos, *a2, *g, w_up, w_up, w_down, w_down, b_up, b_up]
    given = [*enumerate(earlier), *enumerate(filled, 4)]
    aliases = {len(args) + i: out for i, (out, _) in enumerate(given)}
    in_specs = in_specs + [pl.BlockSpec(memory_space=pl.ANY)] * len(given)
    args = args + [value for _, value in given]
    pieces = [struct((2, 4, 2 * count + extra, 128, 128), f32) for extra in (more, 0)] * 2
    pieces = [struct(v.shape, f32) for v in filled] or pieces
    return ordered_call(
        functools.partial(ffn_kernel, len(given)),
        args,
        after,
        prefetch=1,
        grid=(count, 2),
        in_specs=in_specs,
        out_specs=[pl.BlockSpec((2, 1, rows, 128), place)] * 4
        + [
            pl.BlockSpec(
                (1, 4, 2, 128, 128),
                lambda k, i, p: (lax.bitwise_xor(i, lax.div(p[0], 2)), 0, k, 0, 0),
            )
        ]
        * 2
        + [pl.BlockSpec((2, 2, 2, 128, 128), lambda k, i, p: (0, i, k, 0, 0))] * 2
        + [pl.BlockSpec((1, 1, 256), lambda k, i, p: (k * 2 + i, 0, 0))],
        out_shape=[struct((2, 8, rows, 128), bf16)] * 4
        + pieces
        + [struct((count * 2, 1, 256), f32)],
        input_output_aliases=aliases,
        cost_estimate=cost(f"ffn{first}"),
        name="ffn_chunk",
    )


def out_grad_kernel(pos, own, early, late, g_own, g_other, x_send, x_keep, y_send, y_keep):
    other = jnp.where(pl.program_id(0) < 2, early[...], late[...]).astype(bf16)
    tile = dot(own[...], g_own[...], 0, 0) + dot(other, g_other[...], 0, 0)
    squares = relative(tile, pos[0])
    for n in range(2):
        x_send[n, 0, 0] = squares[1][n][:, :128]
        x_keep[n, 0, 0] = squares[0][n][:, :128]
        y_send[n, 0, 0] = squares[n][1][:, 128:]
        y_keep[n, 0, 0] = squares[n][0][:, 128:]


def out_grad(pos, mixed, others, g, after=()):
    rows, width = g[0].shape
    whole = lambda z, p: (0, 0)
    return ordered_call(
        out_grad_kernel,
        [pos, mixed, *others, *g],
        after,
        prefetch=1,
        grid=(4,),
        in_specs=[
            pl.BlockSpec((rows, 128), lambda z, p: (0, 2 * z + p[1])),
            pl.BlockSpec((rows, 128), lambda z, p: (0, lax.min(z, 1))),
            pl.BlockSpec((rows, 128), lambda z, p: (0, lax.max(z - 2, 0))),
            once((rows, width), whole),
            once((rows, width), whole),
        ],
        out_specs=[pl.BlockSpec((2, 1, 1, 128, 128), lambda z, p: (0, z, 2, 0, 0))] * 4,
        out_shape=[struct((2, 4, 3, 128, 128), f32)] * 4,
        cost_estimate=cost("out_grad"),
        name="out_grad",
    )


def second_kernel(at, slots, u_keep, u_one, d_keep, d_one, *refs):
    x_o, y_o = refs[-2:]
    own = slice(at, at + slots)
    y_o[...] = (u_keep[...] + u_one[:, :, own]).reshape(y_o.shape)
    x_o[...] = (d_keep[...] + d_one[:, :, own]).reshape(x_o.shape)


def second_stage(keeps, ones, at, bundles=None, into=0):
    slots, total = keeps[0].shape[2], ones[0].shape[2]
    half = slots // 2
    keep = pl.BlockSpec((1, 2, slots, 128, 128), lambda i: (1, i, 0, 0, 0))
    one = pl.BlockSpec((1, 2, total, 128, 128), lambda i: (1, i, 0, 0, 0))
    if bundles:
        out = pl.BlockSpec((1, 4, half, 128, 128), lambda i: (i, 0, into // half, 0, 0))
        shapes = [struct(v.shape, f32) for v in bundles]
    else:
        out = pl.BlockSpec((2, slots, 128, 128), lambda i: (i, 0, 0, 0))
        shapes = [struct((4, slots, 128, 128), f32)] * 2
    return ordered_call(
        functools.partial(second_kernel, at, slots),
        [keeps[0], ones[0], keeps[1], ones[1], *(bundles or [])],
        [],
        grid=(2,),
        in_specs=[keep, one] * 2 + [pl.BlockSpec(memory_space=pl.ANY)] * len(bundles or []),
        out_specs=[out] * 2,
        out_shape=shapes,
        input_output_aliases={4: 0, 5: 1} if bundles else {},
        cost_estimate=cost("second_stage"),
        name="second_stage",
    )


def finish_kernel(at, slots, cut, u_keep, u_one, u_two, d_keep, d_one, d_two, out):
    own = slice(at, at + slots)
    for n, (keep, one, two) in enumerate(((u_keep, u_one, u_two), (d_keep, d_one, d_two))):
        if cut is None:
            second = two[...]
        else:
            second = two[0, :, cut[0] : cut[1]].reshape(2, slots, 128, 128)
        out[:, n * slots : (n + 1) * slots] = keep[0] + one[0, :, own] + second


def finish(keeps, ones, at, twos, cut):
    slots, total = keeps[0].shape[2], ones[0].shape[2]
    keep = pl.BlockSpec((1, 2, slots, 128, 128), lambda i: (0, i, 0, 0, 0))
    one = pl.BlockSpec((1, 2, total, 128, 128), lambda i: (0, i, 0, 0, 0))
    if cut is None:
        two = pl.BlockSpec((2, slots, 128, 128), lambda i: (i, 0, 0, 0))
    else:
        two = pl.BlockSpec((1, 4, twos[0].shape[2], 128, 128), lambda i: (i, 0, 0, 0, 0))
    return ordered_call(
        functools.partial(finish_kernel, at, slots, cut),
        [keeps[0], ones[0], twos[0], keeps[1], ones[1], twos[1]],
        [],
        grid=(2,),
        in_specs=[keep, one, two] * 2,
        out_specs=pl.BlockSpec((2, 2 * slots, 128, 128), lambda i: (i, 0, 0, 0)),
        out_shape=struct((4, 2 * slots, 128, 128), f32),
        cost_estimate=cost(f"finish{slots}"),
        name="finish",
    )


def qkv_grad_kernel(pos, a1_own, a1_other, *refs):
    own, other, (x_send, x_keep, y_send, y_keep) = refs[:3], refs[3:6], refs[6:]
    left = jnp.concatenate([r[0] for r in own], 1)
    left_other = jnp.concatenate([r[0].astype(bf16) for r in other], 1)
    tile = dot(left, a1_own[...], 0, 0) + dot(left_other, a1_other[...], 0, 0)
    step = pl.program_id(0)
    block = lambda j, n: tile[128 * j : 128 * j + 128, n * 128 : (n + 1) * 128]

    def put(out, whole, half):
        for z in range(4):
            out[0, z, 0] = block(whole, 2 * z)
            out[0, z, 1] = block(whole, 2 * z + 1)
            out[0, z, 2] = block(2, 2 * z + half)

    pl.when(lax.rem(step, 2) == 1)(lambda: put(x_send, 0, 0))
    pl.when(lax.rem(step, 2) == 0)(lambda: put(x_keep, 0, 0))
    pl.when(step >= 2)(lambda: put(y_send, 1, 1))
    pl.when(step < 2)(lambda: put(y_keep, 1, 1))


def qkv_grad(pos, a1, grad_proj, other, after=()):
    rows, width = a1[0].shape
    whole = lambda n, p: (0, 0)

    def source(j, halves):
        def where(n, p):
            unit = lax.bitwise_xor(n, p[0]) * 3 + j
            at = lax.rem(unit, 4)
            return (lax.div(unit, 4), 0, at * 2 + p[1] if halves else at)

        return where

    out = lambda at: pl.BlockSpec((1, 4, 3, 128, 128), lambda n, p: (at(n), 0, 0, 0, 0))
    return ordered_call(
        qkv_grad_kernel,
        [pos, *a1] + [grad_proj] * 3 + [other] * 3,
        after,
        prefetch=1,
        grid=(4,),
        in_specs=[once((rows, width), whole)] * 2
        + [pl.BlockSpec((1, rows, 128), source(j, True)) for j in range(3)]
        + [pl.BlockSpec((1, rows, 128), source(j, False)) for j in range(3)],
        out_specs=[
            out(lambda n: lax.div(n, 2)),
            out(lambda n: lax.div(n, 2)),
            out(lambda n: lax.max(n - 2, 0)),
            out(lambda n: lax.min(n, 1)),
        ],
        out_shape=[struct((2, 4, 3, 128, 128), f32)] * 4,
        cost_estimate=cost("qkv_grad"),
        name="qkv_grad",
    )


LONG, SHORT = 10**11, 1
WEIGHTS = {"first_norm": LONG, "hidden0": LONG, "blocks": LONG, "in_place": LONG, "ends": LONG, "finish2": LONG}


def cost(name):
    flops = WEIGHTS.get(name, SHORT)
    return pl.CostEstimate(flops=flops, bytes_accessed=1, transcendentals=0)


def rotate(x, cos, sin_first, sin_second):
    n = x.shape[1]
    half = ROT // 2
    return x * cos + pltpu.roll(x, n - half, 1) * sin_first + pltpu.roll(x, half, 1) * sin_second


def three(x, w_hi, w_lo):
    hi, lo = split(x)
    return dot(hi, w_hi, 1, 0) + dot(lo, w_hi, 1, 0) + dot(hi, w_lo, 1, 0)


def pair_mask():
    return (iota((128, 128), 0) // 64) == (iota((128, 128), 1) // 64)


def pack(first, second):
    mask = pair_mask()
    first = jnp.where(mask, first, 0.0)
    second = jnp.where(mask, second, 0.0)
    first = first + pltpu.roll(first, 64, 1)
    second = second + pltpu.roll(second, 64, 1)
    return jnp.where(iota((128, 128), 1) < 64, first, second)


def unpack(packed):
    mask = pair_mask()
    low = iota((128, 128), 1) < 64
    turned = pltpu.roll(packed, 64, 1)
    return (
        jnp.where(mask, jnp.where(low, packed, turned), 0.0),
        jnp.where(mask, jnp.where(low, turned, packed), 0.0),
    )


def to_column(row):
    eye = iota((128, 128), 0) == iota((128, 128), 1)
    return jnp.sum(jnp.where(eye, jnp.broadcast_to(row, (128, 128)), 0.0), axis=1, keepdims=True)


def each_head(x):
    mask = iota((1, 128), 1) < 64
    zero = jnp.zeros_like(x)
    return jnp.where(mask, x, zero), jnp.where(mask, zero, x)


def feature_kernel(
    a1, wq, wk, wv, bq, bk, bv, fw, matrix, cos, sin1, sin2, valid, qf_o, kf_o, v_o, st_o
):
    x = a1[...]
    count = x.shape[0] // LEN_BLK
    rows = lambda i: slice(LEN_BLK * i, LEN_BLK * (i + 1))
    turns = cos[...], sin1[...], sin2[...]
    weight = fw[...]
    halves = split(matrix[...])
    q = [dot(x[rows(i)], wq[...], 1, 0) for i in range(count)]
    k = [dot(x[rows(i)], wk[...], 1, 0) for i in range(count)]
    q = [rotate(part + bq[...], *turns) for part in q]
    v = [(dot(x[rows(i)], wv[...], 1, 0) + bv[...]).astype(bf16) for i in range(count)]
    k = [rotate(part + bk[...], *turns) for part in k]
    q = [three(part, *halves) for part in q]
    k = [three(part, *halves) for part in k]
    for i in range(count):
        qf_o[rows(i)] = (weight * jnp.exp(q[i])).astype(bf16)
        kf = (weight * jnp.exp(k[i])).astype(bf16) * valid[rows(i)].astype(bf16)
        kf_o[rows(i)] = kf
        k[i] = kf
        v_o[rows(i)] = v[i]
    for i in range(count):
        state = [
            dot(k[i][:, 128 * p : 128 * p + 128], v[i][:, 128 * p : 128 * p + 128], 0, 0)
            for p in range(2)
        ]
        st_o[i, 0, :128] = pack(state[0], state[1])
        norm = jnp.sum(k[i].astype(f32), axis=0, keepdims=True)
        st_o[i, 0, 128:] = norm_rows(norm[:, :128], norm[:, 128:])


def norm_rows(first, second):
    line = iota((8, 128), 0)
    return jnp.where(line == 0, first, jnp.where(line == 1, second, 0.0))


def scores(qp, kp, causal):
    raw = dot(jnp.concatenate(each_head(qp), 0), kp, 1, 1)
    return [
        jnp.where(causal, raw[LEN_BLK * h : LEN_BLK * (h + 1)], 0.0).astype(bf16)
        for h in range(2)
    ]


def lower(n):
    return iota((n, n), 0) >= iota((n, n), 1)


def mix_kernel(pos, g, wo, qf, kf, v, st, mix_o, dn_o, dd_o, ds_o, *sends):
    count = qf.shape[0] // LEN_BLK
    mask = pair_mask()
    lane = iota((1, 128), 1)
    first = lane < 64
    causal = lower(LEN_BLK)
    one0, one1 = each_head(jnp.ones((LEN_BLK, 128), bf16))
    cells = [(i, p) for i in range(count) for p in range(2)]
    rows = lambda i: slice(LEN_BLK * i, LEN_BLK * (i + 1))
    cols = lambda p: slice(128 * p, 128 * p + 128)
    q = {(i, p): qf[rows(i), cols(p)] for i, p in cells}
    s = {(i, p): scores(q[i, p], kf[rows(i), cols(p)], causal) for i, p in cells}
    grad_mixed = dot(g[...], wo[...], 1, 1)
    both = {}
    for i in range(count):
        state = unpack(st[i, 0, :128])
        for p in range(2):
            column = to_column(st[i, 0, 128 + p : 129 + p])
            norm = jnp.where(mask, jnp.broadcast_to(column, (128, 128)), 0.0)
            hi, lo = split(jnp.concatenate([state[p], norm], 1))
            qp = q[i, p]
            both[i, p] = dot(jnp.concatenate([qp, qp], 1), jnp.concatenate([hi, lo], 0), 1, 0)
    for i, p in cells:
        v0, v1 = each_head(v[rows(i), cols(p)])
        right = jnp.concatenate(
            [jnp.concatenate([v0, one0], 1), jnp.concatenate([v1, one1], 1)], 0
        )
        both[i, p] = both[i, p] + dot(jnp.concatenate(s[i, p], 1), right, 1, 0)
    mixes, dns, norms, grads, sums = {}, {}, {}, {}, {}
    for i, p in cells:
        inverse = 1.0 / both[i, p][:, 128:]
        mixed = both[i, p][:, :128] * inverse
        low = mixed.astype(bf16)
        mix_o[rows(i), cols(p)] = low
        mixes[i, p] = low
        dn = (grad_mixed[rows(i), cols(p)] * inverse).astype(bf16)
        dn_o[rows(i), cols(p)] = dn
        dns[i, p] = dn
        product = -(dn.astype(f32) * mixed)
        d0 = jnp.sum(jnp.where(first, product, 0.0), axis=1, keepdims=True)
        d1 = jnp.sum(jnp.where(first, 0.0, product), axis=1, keepdims=True)
        sums[i, p] = d0, d1
    for i, p in cells:
        grads[i, p] = dot(q[i, p], dns[i, p], 0, 0)
    for i, p in cells:
        d0, d1 = sums[i, p]
        norms[i, p] = column_sum(q[i, p].astype(f32) * jnp.where(first, d0, d1))
    for i in range(count):
        lines = jnp.zeros((LEN_BLK, 128), f32)
        for p in range(2):
            d0, d1 = sums[i, p]
            lines = jnp.where(lane == 2 * p, d0, jnp.where(lane == 2 * p + 1, d1, lines))
        dd_o[0, rows(i)] = lines
        ds_o[i, 0, :128] = pack(grads[i, 0], grads[i, 1])
        ds_o[i, 0, 128:] = norm_rows(norms[i, 0], norms[i, 1])
        other_half = jnp.where(pos[1] == 0, mixes[i, 1].astype(f32), mixes[i, 0].astype(f32))

        def put(out, lines=rows(i), other_half=other_half):
            out[lines] = other_half

        for n, out in enumerate(sends):
            pl.when(lax.div(pl.program_id(0), 2) == n)(functools.partial(put, out))


def back_kernel(
    pos, qf, kf, v, dn, dd, st, ds, fw, matrix, cos, sin1, sin2, gp_o, send_o, bias_o, fw_o
):
    count = qf.shape[0] // LEN_BLK
    step = pl.program_id(1)
    causal = lower(LEN_BLK)
    lane = iota((1, 128), 1)
    first = lane < 64
    turns = cos[...], -sin1[...], -sin2[...]
    halves = split(matrix[...])
    cells = [(i, p) for i in range(count) for p in range(2)]
    rows = lambda i: slice(LEN_BLK * i, LEN_BLK * (i + 1))
    cols = lambda p: slice(128 * p, 128 * p + 128)
    q, k, vv, d, s, t, col = {}, {}, {}, {}, {}, {}, {}
    for i, p in cells:
        q[i, p], k[i, p] = qf[rows(i), cols(p)], kf[rows(i), cols(p)]
        vv[i, p], d[i, p] = v[rows(i), cols(p)], dn[rows(i), cols(p)]
        col[i, p] = [
            jnp.sum(jnp.where(lane == 2 * p + h, dd[0, rows(i)], 0.0), axis=1, keepdims=True)
            for h in range(2)
        ]
    for c in cells:
        s[c] = scores(q[c], k[c], causal)
        raw = dot(jnp.concatenate(each_head(d[c]), 0), vv[c], 1, 1)
        t[c] = [
            jnp.where(causal, raw[LEN_BLK * h : LEN_BLK * (h + 1)] + col[c][h], 0.0).astype(bf16)
            for h in range(2)
        ]
    dq, dk, dv = {}, {}, {}
    for i in range(count):
        state, later = unpack(st[i, 0, :128]), unpack(ds[i, 0, :128])
        for p in range(2):
            c = i, p
            s_hi, s_lo = split(state[p])
            d_hi, d_lo = split(later[p])
            twice = lambda x: jnp.concatenate([x, x], 1)
            dq[c] = dot(twice(d[c]), jnp.concatenate([s_hi, s_lo], 1), 1, 1)
            dk[c] = dot(twice(vv[c]), jnp.concatenate([d_hi, d_lo], 1), 1, 1)
            dv[c] = dot(twice(k[c]), jnp.concatenate([d_hi, d_lo], 0), 1, 0)
    for c in cells:
        dq[c] = dq[c] + dot(jnp.concatenate(t[c], 1), jnp.concatenate(each_head(k[c]), 0), 1, 0)
        dk[c] = dk[c] + dot(jnp.concatenate(t[c], 0), jnp.concatenate(each_head(q[c]), 0), 0, 0)
        dv[c] = dv[c] + dot(jnp.concatenate(s[c], 0), jnp.concatenate(each_head(d[c]), 0), 0, 0)
    for i, p in cells:
        c = i, p
        norm = jnp.where(first, *col[c]) * st[i, 0, 128 + p : 129 + p]
        dq[c] = (dq[c] + norm) * q[c].astype(f32)
        dk[c] = (dk[c] + ds[i, 0, 128 + p : 129 + p]) * k[c].astype(f32)
    whole = lambda parts: jnp.concatenate(
        [jnp.concatenate([parts[i, 0], parts[i, 1]], 1) for i in range(count)], 0
    )
    dq, dk, dv = whole(dq), whole(dk), whole(dv)
    tall = [jnp.concatenate([turn] * count, 0) for turn in turns]
    grads = (
        rotate(three(dq, *halves), *tall).astype(bf16),
        rotate(three(dk, *halves), *tall).astype(bf16),
        dv.astype(bf16),
    )
    for n in range(3):
        gp_o[n] = grads[n]
        wide = grads[n].astype(f32)
        other_half = jnp.where(pos[1] == 0, wide[:, 128:], wide[:, :128])
        send_o[n] = other_half
    totals = [column_sum(part.astype(f32)) for part in grads]
    totals.append(column_sum(dq + dk) / fw[...])

    @pl.when(step == 0)
    def _():
        for n in range(3):
            bias_o[n] = totals[n]
        fw_o[...] = totals[3]

    @pl.when(step > 0)
    def _():
        for n in range(3):
            bias_o[n] = bias_o[n] + totals[n]
        fw_o[...] = fw_o[...] + totals[3]


def attention_specs(seqs, per, more=0):
    rows = LEN_BLK * per
    return dict(
        grid=(4, seqs // per),
        wide=pl.BlockSpec((rows, 1024), lambda h, g, *_: (g, 0)),
        head=pl.BlockSpec((rows, HG), lambda h, g, *_: (g, h)),
        state=pl.BlockSpec((per, 1, 136, 128), lambda h, g, *_: (g, h, 0, 0)),
        row=pl.BlockSpec((1, HG), lambda h, g, *_: (0, h)),
        table=pl.BlockSpec((256, 256), lambda h, g, *_: (0, 0)),
        dden=pl.BlockSpec((1, rows, 128), lambda h, g, *_: (h, g, 0)),
    )


def features(a1, w_qkv, b_qkv, feat_weight, matrix, turns, valid, after=(), per=4):
    rows = a1.shape[0]
    seqs = rows // LEN_BLK
    s = attention_specs(seqs, per)
    weights = [pl.BlockSpec((1024, HG), lambda h, g, o=o: (0, 4 * o + h)) for o in range(3)]
    biases = [pl.BlockSpec((1, HG), lambda h, g, o=o: (0, 4 * o + h)) for o in range(3)]
    return ordered_call(
        feature_kernel,
        [a1, w_qkv, w_qkv, w_qkv, b_qkv, b_qkv, b_qkv, feat_weight, matrix, *turns, valid],
        after,
        grid=s["grid"],
        in_specs=[s["wide"], *weights, *biases, s["row"]]
        + [s["table"]] * 4
        + [pl.BlockSpec((LEN_BLK * per, 1), lambda h, g: (g, 0))],
        out_specs=[s["head"]] * 3 + [s["state"]],
        out_shape=[struct((rows, 1024), bf16)] * 3 + [struct((seqs, 4, 136, 128), f32)],
        cost_estimate=cost("features"),
        name="features",
    )


def mixing(pos, g, w_out, qf, kf, v, state, after=(), per=2):
    rows = g.shape[0]
    seqs = rows // LEN_BLK
    steps = seqs // per
    s = attention_specs(seqs, per)
    return ordered_call(
        mix_kernel,
        [pos, g, w_out, qf, kf, v, state],
        after,
        prefetch=1,
        grid=s["grid"],
        in_specs=[s["wide"], pl.BlockSpec((HG, 1024), lambda h, g, *_: (h, 0))]
        + [s["head"]] * 3
        + [s["state"]],
        out_specs=[
            s["head"],
            s["head"],
            s["dden"],
            s["state"],
            pl.BlockSpec(
                (LEN_BLK * per, 128),
                lambda h, g, *_: (lax.select(h < 2, g, 0 * g + steps - 1), lax.min(h, 1)),
            ),
            pl.BlockSpec(
                (LEN_BLK * per, 128),
                lambda h, g, *_: (lax.select(h < 2, 0 * g, g), lax.max(h - 2, 0)),
            ),
        ],
        out_shape=[
            struct((rows, 1024), bf16),
            struct((rows, 1024), bf16),
            struct((4, rows, 128), f32),
            struct((seqs, 4, 136, 128), f32),
            struct((rows, 256), f32),
            struct((rows, 256), f32),
        ],
        cost_estimate=cost("mixing"),
        name="mixing",
    )

def backward(pos, qf, kf, v, dn, dd, state, later, feat_weight, matrix, turns, after=(), per=4):
    rows = qf.shape[0]
    seqs = rows // LEN_BLK
    s = attention_specs(seqs, per)
    return ordered_call(
        back_kernel,
        [pos, qf, kf, v, dn, dd, state, later, feat_weight, matrix, *turns],
        after,
        prefetch=1,
        grid=s["grid"],
        in_specs=[s["head"]] * 4
        + [s["dden"], s["state"], s["state"], s["row"]]
        + [s["table"]] * 4,
        out_specs=[
            pl.BlockSpec((3, LEN_BLK * per, HG), lambda h, g, *_: (0, g, h)),
            pl.BlockSpec((3, LEN_BLK * per, 128), lambda h, g, *_: (0, g, h)),
            pl.BlockSpec((3, 1, HG), lambda h, g, *_: (0, 0, h)),
            s["row"],
        ],
        out_shape=[
            struct((3, rows, 1024), bf16),
            struct((3, rows, 512), f32),
            struct((3, 1, 1024), f32),
            struct((1, 1024), f32),
        ],
        cost_estimate=cost("backward"),
        name="backward",
    )


def norm_parts(x):
    centre = x - jnp.mean(x, axis=-1, keepdims=True)
    r = lax.rsqrt(jnp.mean(centre * centre, axis=-1, keepdims=True) + norm_epsilon)
    return centre * r, r


def norm_back(grad, xhat, r, gain):
    e = grad * gain
    return r * (
        e
        - jnp.mean(e, axis=-1, keepdims=True)
        - xhat * jnp.mean(e * xhat, axis=-1, keepdims=True)
    )


def add_sums(out, sums):
    step = pl.program_id(0)
    new = jnp.concatenate(sums, 0)

    @pl.when(step == 0)
    def _():
        out[...] = new

    @pl.when(step > 0)
    def _():
        out[...] = out[...] + new


def column_sum(x):
    return jnp.sum(x, axis=0, keepdims=True)


def tiles(tile, fixed):
    wide = lambda n: pl.BlockSpec((tile, n), lambda i, *_: (i, 0))
    keep = [once(a.shape, lambda i, *_: (0, 0)) for a in fixed]
    return wide, keep


def norms_kernel(x, g, gain1, bias1, gain2, bias2, a1_o, a2_o, g_o, *x_o):
    xhat, _ = norm_parts(x[...].astype(f32))
    a1_o[...] = (xhat * gain1[...] + bias1[...]).astype(bf16)
    a2_o[...] = (xhat * gain2[...] + bias2[...]).astype(bf16)
    g_o[...] = g[...].astype(g_o.dtype)
    for out in x_o:
        out[...] = x[...].astype(f32)


def norms(x, g, *vectors, after=(), g_type=f32):
    rows, tile = x.shape[0], 256
    wide, keep = tiles(tile, vectors)
    return ordered_call(
        norms_kernel,
        [x, g, *vectors],
        after,
        grid=(rows // tile,),
        in_specs=[wide(1024)] * 2 + keep,
        out_specs=[wide(1024)] * (4 if g_type == f32 else 3),
        out_shape=[struct((rows, 1024), bf16)] * 2
        + [struct((rows, 1024), g_type)] * (2 if g_type == f32 else 1),
        cost_estimate=cost("norms"),
        name="norms",
    )


def hidden_rows_kernel(grad, filled, pos, *refs):
    acts, weights, outs = refs[:2], refs[2:6], refs[6 + filled :]
    send, keep = outs[-2:] if not grad else outs[2:4]
    total = None
    for b in range(4):
        act = acts[b % 2]
        act = jnp.concatenate([act[0, 4 * (b // 2) + n] for n in range(4)], 1)
        part = dot(act, weights[b][...], 1, 1 if grad else 0)
        total = part if total is None else total + part
    step = pl.program_id(0)
    steps = pl.num_programs(0) // 2

    @pl.when(step < steps)
    def _():
        send[0] = total

    @pl.when(step >= steps)
    def _():
        keep[...] = total

    if grad:
        x_own, x_other, sum_o = outs[0], outs[1], outs[4]
        xhat, _ = norm_parts(jnp.where(step < steps, x_other[...], x_own[...].astype(f32)))
        sums = [column_sum(total * xhat), column_sum(total)]
        add_sums(sum_o, sums + [jnp.zeros((6, 1024), f32)])


def hidden_rows(pos, acts, weight, rows_in=None, sends=None, after=()):
    grad = rows_in is not None
    rows, tile = acts[0].shape[2], ROW_TILE
    steps = rows // tile
    act = pl.BlockSpec(
        (1, 8, tile, 128), lambda i, p: (1 - lax.div(i, steps), 0, lax.rem(i, steps), 0)
    )
    if grad:
        part = lambda b: once((1024, 512), lambda i, p: (0, 2 * b + p[1]))
    else:
        part = lambda b: once((512, 1024), lambda i, p: (2 * b + p[1], 0))
    filled = [] if sends is None else [sends]
    ours = pl.BlockSpec((tile, 1024), lambda i, p: (lax.max(i - steps, 0), 0))
    theirs = pl.BlockSpec((tile, 1024), lambda i, p: (lax.min(i, steps - 1), 0))
    return ordered_call(
        functools.partial(hidden_rows_kernel, grad, len(filled)),
        [pos, *acts] + [weight] * 4 + filled + list(rows_in or ()),
        after,
        prefetch=1,
        grid=(2 * steps,),
        in_specs=[act] * 2
        + [part(b) for b in range(4)]
        + [pl.BlockSpec(memory_space=pl.ANY)] * len(filled)
        + [ours, theirs][: 2 * grad],
        out_specs=[
            pl.BlockSpec((1, tile, 1024), lambda i, p: (int(grad), lax.min(i, steps - 1), 0)),
            ours,
        ]
        + [pl.BlockSpec((8, 1024), lambda i, p: (0, 0))] * grad,
        out_shape=[struct((2, rows, 1024), f32), struct((rows, 1024), f32)]
        + [struct((8, 1024), f32)] * grad,
        input_output_aliases={7: 0} if filled else {},
        cost_estimate=cost(f"hidden{grad:d}"),
        name="hidden_rows",
    )


def first_norm_kernel(x, g, gp, w_qkv, gain, part_o, sum_o):
    xhat, r = norm_parts(x[...].astype(f32))
    grad_res = g[...].astype(f32)
    grad = dot(jnp.concatenate([gp[0], gp[1], gp[2]], 1), w_qkv[...], 1, 1)
    part_o[...] = grad_res + norm_back(grad, xhat, r, gain[...])
    sums = [column_sum(v) for v in (grad * xhat, grad, grad_res)]
    add_sums(sum_o, sums + [jnp.zeros((5, 1024), f32)])


def first_norm(x, g, gp, w_qkv, gain, after=()):
    rows, tile = x.shape[0], ROW_TILE
    fixed = (w_qkv, gain)
    wide, keep = tiles(tile, fixed)
    return ordered_call(
        first_norm_kernel,
        [x, g, gp, *fixed],
        after,
        grid=(rows // tile,),
        in_specs=[wide(1024)] * 2 + [pl.BlockSpec((3, tile, 1024), lambda i: (0, i, 0))] + keep,
        out_specs=[wide(1024), pl.BlockSpec((8, 1024), lambda i: (0, 0))],
        out_shape=[struct((rows, 1024), f32), struct((8, 1024), f32)],
        cost_estimate=cost("first_norm"),
        name="first_norm",
    )


def ends_kernel(x, mixed, part, own_r, other_r, own_g, other_g, w_out, bias, gain, res_o, out_o):
    value = x[...].astype(f32)
    out = dot(mixed[...], w_out[...], 1, 0) + (own_r[...] + other_r[0])
    res_o[...] = (value + out + bias[...]).astype(bf16)
    xhat, r = norm_parts(value)
    out_o[...] = part[...] + norm_back(own_g[...] + other_g[0], xhat, r, gain[...])


def ends(x, mixed, part, own_r, own_g, others, w_out, bias, gain, after=()):
    rows, tile = x.shape[0], ROW_TILE
    fixed = (w_out, bias, gain)
    wide, keep = tiles(tile, fixed)
    half = lambda n: pl.BlockSpec((1, tile, 1024), lambda i: (n, i, 0))
    return ordered_call(
        ends_kernel,
        [x, mixed, part, own_r, others, own_g, others, *fixed],
        after,
        grid=(rows // tile,),
        in_specs=[wide(1024)] * 4 + [half(0), wide(1024), half(1)] + keep,
        out_specs=[wide(1024)] * 2,
        out_shape=[struct((rows, 1024), bf16), struct((rows, 1024), f32)],
        cost_estimate=cost("ends"),
        name="ends",
    )


class Links:
    def __init__(self, mesh):
        self.nb, self.ns = mesh.shape["batch"], mesh.shape["seq"]
        self.tuned = (self.nb, self.ns) == (4, 8)

    def send(self, value, move):
        pairs = []
        for b in range(self.nb):
            for s in range(self.ns):
                to = move(b, s)
                if to is not None:
                    pairs.append((b * self.ns + s, to[0] * self.ns + to[1]))
        return lax.ppermute(value, ("batch", "seq"), pairs)

    def core(self, value):
        return self.send(value, lambda b, s: (b, s ^ 1))

    def x(self, value):
        return self.send(value, lambda b, s: (b ^ 1, s))

    def y(self, value):
        return self.send(value, lambda b, s: (b ^ 2, s))

    def ring(self, value, by):
        s = lax.axis_index("seq")
        got = self.send(value, lambda b, s: (b, (s + by) % self.ns))
        kept = s >= by if by > 0 else s < self.ns + by
        return got, kept

    def shift(self, value, by):
        inside = lambda s: 0 <= s < self.ns
        return self.send(value, lambda b, s: (b, s + by) if inside(s + by) else None)


def hold(value, behind):
    behind = [b for b in behind if b is not None]
    return lax.optimization_barrier((value, *behind))[0] if behind else value


class Group:
    def __init__(self, links, x_send, x_keep, y_send, y_keep, at=0):
        self.links, self.at = links, at
        self.keeps = x_keep, y_keep
        self.slots = x_keep.shape[2]
        if links.tuned:
            self.ones = [links.x(x_send), links.y(y_send)]
            self.twos = None

    def arrived(self, *behind):
        self.ones = [hold(one, behind) for one in self.ones]

    def second(self):
        x_out, y_out = second_stage(self.keeps, self.ones, self.at)
        self.twos, self.cut = [self.links.y(y_out), self.links.x(x_out)], None
        return x_out

    def second_in(self, x_send, y_send, into):
        return second_stage(self.keeps, self.ones, self.at, (x_send, y_send), into)

    def second_with(self, group):
        total = group.ones[0].shape[2]
        self.twos = group.ones[::-1]
        self.cut = (0, group.at) if group.at else (group.slots, total)

    def done(self, *behind):
        twos = [hold(two, behind) for two in self.twos]
        return finish(self.keeps, self.ones, self.at, twos, self.cut)


def reduce_z(value):
    groups = [[0, 2, 4, 6], [1, 3, 5, 7]]
    return lax.psum_scatter(
        value, "seq", scatter_dimension=0, axis_index_groups=groups, tiled=True
    )[0]


class Carried:
    def __init__(self, links, state, reverse):
        self.links, self.state, self.reverse = links, state, reverse
        self.sign = -1 if reverse else 1
        self.mine = self.sum = None
        if links.tuned:
            self.core = lax.rem(lax.axis_index("seq"), 2)
            self.half = state.shape[0] // 2
            self.other = links.core(self.of_half(1 - self.core))

    def of_half(self, which):
        return lax.dynamic_slice_in_dim(self.state, which * self.half, self.half, 0)

    def near(self, *behind):
        if not self.links.tuned:
            return None
        self.other = hold(self.other, behind)
        self.mine = self.of_half(self.core) + self.other
        self.one, self.one_kept = self.links.ring(self.mine, self.sign * 2)
        return self.mine

    def far(self, *behind):
        if not self.links.tuned:
            return None
        self.one = jnp.where(self.one_kept, hold(self.one, behind), 0.0)
        self.sum = self.mine + self.one
        self.two, self.two_kept = self.links.ring(self.sum, self.sign * 4)
        return self.sum

    def done(self, *behind):
        links = self.links
        if not links.tuned:
            total, step = self.state, 1
            while step < links.ns:
                total = total + links.shift(total, self.sign * step)
                step *= 2
            return links.shift(total, self.sign)
        self.two = hold(self.two, behind)
        before = self.one + jnp.where(self.two_kept, self.two, 0.0)
        second = self.core == (0 if self.reverse else 1)
        here = before + jnp.where(second, self.other, 0.0)
        there = before + jnp.where(second, 0.0, self.of_half(self.core))
        rest = links.core(there)
        low = jnp.where(self.core == 0, here, rest)
        high = jnp.where(self.core == 0, rest, here)
        return jnp.concatenate([low, high], 0)


class Line:
    def __init__(self, links, value):
        self.z = lax.div(lax.axis_index("seq"), 2)
        self.value = value
        self.parts = []
        for by in (2, 1, 3):
            part = self.pick(lax.rem(self.z + by, 4))
            self.parts.append(links.send(part, lambda b, s: (b, (s + 2 * by) % 8)))

    def pick(self, at):
        return lax.dynamic_index_in_dim(self.value, at, 0, keepdims=False)

    def done(self, *behind):
        total = self.pick(self.z)
        for part in self.parts:
            total = total + hold(part, behind)
        return total


class Halves:
    def __init__(self, links, value):
        self.links = links
        self.z = lax.div(lax.axis_index("seq"), 2)
        both = value.reshape((2, 2) + value.shape[1:])
        low = lax.rem(self.z, 2)
        pick = lambda i: lax.dynamic_index_in_dim(both, i, 1, keepdims=False)
        self.kept = pick(low)
        self.one = links.send(pick(1 - low), lambda b, s: (b, s ^ 2))

    def stage_two(self, *behind):
        self.one = hold(self.one, behind)
        self.high = lax.div(self.z, 2)
        out = self.pick(1 - self.high)
        self.two = self.links.send(out, lambda b, s: (b, s ^ 4))
        return out

    def pick(self, i):
        at = lambda v: lax.dynamic_index_in_dim(v, i, 0, keepdims=False)
        return at(self.kept) + at(self.one)

    def done(self, *behind):
        self.two = hold(self.two, behind)
        return self.pick(self.high) + self.two


def dct_table(order):
    degree = np.arange(order, dtype=np.float64)[:, None]
    sample = np.arange(order, dtype=np.float64)[None, :]
    table = np.cos(math.pi * (sample + 0.5) * degree / order) * math.sqrt(2.0 / order)
    return np.where(degree == 0.0, table * math.sqrt(0.5), table).astype(np.float32)


def rotation_tables(positions):
    half = ROT // 2
    at = jnp.arange(HG, dtype=jnp.int32) % HEAD_DIM
    inverse = rope_base ** (-2.0 * (at % half).astype(f32) / ROT)
    angles = positions[:, None] * inverse[None, :]
    at = at[None, :]
    sin = jnp.sin(angles)
    return (
        jnp.where(at < ROT, jnp.cos(angles), 1.0),
        jnp.where(at < half, -sin, 0.0),
        jnp.where((at >= half) & (at < ROT), sin, 0.0),
    )


def head_blocks(directions, transposed):
    times = HG // HEAD_DIM
    left = jnp.tile(directions, (times, 1))
    right = np.tile(dct_table(HEAD_DIM), (1, times))
    dims = (((0,), (1,)), ((), ())) if transposed else (((1,), (0,)), ((), ()))
    args = (jnp.asarray(right), left) if transposed else (left, jnp.asarray(right))
    full = lax.dot_general(*args, dims, precision=lax.Precision.HIGHEST)
    block = np.arange(HG) // HEAD_DIM
    return jnp.where(block[:, None] == block[None, :], full, 0.0)


def in_place_kernel(count, start, blocks, down_o, up_o):
    for k in range(count):
        lines = slice(128 * k, 128 * k + 128)
        for half in range(2):
            down_o[lines, 128 * half : 128 * half + 128] = blocks[start + 2 * k + half]
            up_o[half, k] = blocks[2 * k + half]


def in_place(blocks, count, after, start=None):
    return ordered_call(
        functools.partial(in_place_kernel, count, start or 2 * count),
        [blocks],
        after,
        grid=(1,),
        in_specs=[pl.BlockSpec(blocks.shape, lambda i: (0, 0, 0))],
        out_specs=[
            pl.BlockSpec((128 * count, 256), lambda i: (0, 0)),
            pl.BlockSpec((2, count, 128, 128), lambda i: (0, 0, 0, 0)),
        ],
        out_shape=[struct((128 * count, 256), f32), struct((2, count, 128, 128), f32)],
        cost_estimate=cost("in_place"),
        name="in_place",
    )


def blocks_kernel(left, right, out):
    full = lax.dot_general(
        left[...],
        right[...],
        (((1,), (0,)), ((), ())),
        precision=lax.Precision.HIGHEST,
        preferred_element_type=f32,
    )
    same = iota((HG, HG), 0) // HEAD_DIM == iota((HG, HG), 1) // HEAD_DIM
    out[...] = jnp.where(same, full, 0.0)


def head_blocks_after(directions, after):
    times = HG // HEAD_DIM
    left = jnp.tile(directions, (times, 1))
    right = jnp.asarray(np.tile(dct_table(HEAD_DIM), (1, times)))
    whole = lambda a: pl.BlockSpec(a.shape, lambda i: (0, 0))
    return ordered_call(
        blocks_kernel,
        [left, right],
        after,
        grid=(1,),
        in_specs=[whole(left), whole(right)],
        out_specs=pl.BlockSpec((HG, HG), lambda i: (0, 0)),
        out_shape=struct((HG, HG), f32),
        cost_estimate=cost("blocks"),
        name="head_blocks",
    )


def per_device(
    links,
    hidden_in,
    cotangent,
    lengths,
    key_mask,
    ln1_gain,
    ln1_bias,
    ln2_gain,
    ln2_bias,
    w_qkv,
    b_qkv,
    w_out,
    b_out,
    w_up,
    b_up,
    w_down,
    b_down,
    feat_weight,
    directions,
):
    seqs, block, width = hidden_in.shape
    rows = seqs * block
    tuned = links.tuned
    place = lax.axis_index("seq")
    me = lax.axis_index("batch") if tuned else 0 * place
    core = lax.rem(place, 2)
    pos = jnp.stack([me, core]).astype(jnp.int32)
    places = place * block + jnp.arange(block, dtype=jnp.int32)
    valid = (places[None, :] < lengths[:, None]) & ((key_mask == 1) | (places[None, :] == 0))
    valid = valid.astype(f32).reshape(rows, 1)
    x = hidden_in.reshape(rows, width)
    g = cotangent.reshape(rows, width)
    row = lambda v: v.reshape(1, -1)
    gains = row(ln1_gain), row(ln1_bias), row(ln2_gain), row(ln2_bias)
    a1, a2, g_wide, x_wide = norms(x, g, *gains)
    x_other, g_other = links.core(x_wide), links.core(g_wide)

    forth = head_blocks(directions, True)
    turns = rotation_tables(places.astype(f32))
    weights = row(feat_weight)

    qf, kf, v, state = features(a1, w_qkv, row(b_qkv), weights, forth, turns, valid)
    forward = Carried(links, state, False)
    x_other = hold(x_other, [state])
    a1_o, a2_o, g_o = norms(
        x_other, hold(g_other, [state]), *gains, g_type=bf16, after=[state]
    )
    ffn = functools.partial(
        ffn_chunk,
        pos=pos,
        a2=(a2, a2_o),
        g=(g, g_o),
        w_up=w_up,
        w_down=w_down,
        b_up=row(b_up),
    )
    c0 = ffn(0, 1, after=[forward.near(a1_o)])
    g0 = Group(links, *c0[4:8])
    c1 = ffn(1, 2, earlier=c0[:4], more=1, after=[forward.far(c0[8])])
    first = list(c1[4:8])
    if tuned:
        g0.arrived(c1[8])
        first[0::2] = g0.second_in(*first[0::2], 4)
    g1 = Group(links, *first)
    state_in = forward.done(c1[8])
    mixed, dn, dd, state_grad, *mixed_send = mixing(
        pos, g, w_out, qf, kf, v, state_in, after=first[:1]
    )
    reverse = Carried(links, state_grad, True)
    mixed_other = [links.core(part) for part in mixed_send]
    back = head_blocks_after(directions, [mixed])
    held = [reverse.near(back)]
    out_pieces = out_grad(
        pos, mixed, [hold(part, [back]) for part in mixed_other], (g, g_o), after=held
    )
    c2 = ffn(3, 1, earlier=c1[:4], filled=out_pieces, after=[reverse.far(out_pieces[0])])
    held = [c2[8]]
    z0 = None
    if tuned:
        g1.arrived(c2[8])
        g0.second_with(g1)
        held = [g1.second()]
    state_later = reverse.done(held[0])
    g2 = Group(links, *c2[4:8])
    grad_proj, grad_send, bias_qkv, grad_feat = backward(
        pos,
        qf,
        kf,
        v,
        dn,
        dd,
        state_in,
        state_later,
        weights,
        back,
        turns,
        after=held,
    )
    grad_other = links.core(grad_send)
    if tuned:
        z0 = g0.done(grad_proj)
        early = reduce_z(z0)
    last_parts = qkv_grad(
        pos, (a1, a1_o), grad_proj, hold(grad_other, [grad_proj, z0]), after=[z0]
    )
    acts = c2[:4]
    held = [last_parts[0]]
    pieces = list(last_parts)
    if tuned:
        g2.arrived(last_parts[0])
        held = [g2.second()]
        z1 = g1.done(*held)
        later = Halves(links, z1)
        pieces[0::2] = [hold(piece, [z1]) for piece in pieces[0::2]]
        held = [z1]
    g3 = Group(links, *pieces)
    own_g = hidden_rows(pos, acts[2:], w_up, (x, x_other), after=held)
    held = [own_g[1]]
    if tuned:
        z2 = g2.done(own_g[1])
        middle = Halves(links, z2)
        held += [z2, early]
    own_r = hidden_rows(pos, acts[:2], w_down, sends=own_g[0], after=held)
    others = links.core(own_r[0])
    held = [own_r[1]]
    if tuned:
        held = [later.stage_two(own_r[1]), middle.stage_two(own_r[1])]
        g3.arrived(own_r[1])
        held.append(g3.second())
    partial, sums1 = first_norm(x, g, grad_proj, w_qkv, row(ln1_gain), after=held)
    half_up = jnp.concatenate([c[8].reshape(-1, 2, 2, 128) for c in (c0, c1, c2)], 0)
    half_up = half_up.transpose(1, 2, 0, 3).reshape(4, 1, 512)
    b_up_grad = jnp.where(core == np.arange(2)[None, :, None], half_up, 0.0).reshape(-1)
    vectors = [
        sums1[0],
        sums1[1],
        own_g[2][0],
        own_g[2][1],
        bias_qkv.reshape(-1),
        sums1[2],
        b_up_grad,
        grad_feat[0],
    ]
    lines = jnp.concatenate([v_.reshape(links.ns, -1) for v_ in vectors], 1)
    held = [partial]
    if tuned:
        lines = jnp.pad(lines.reshape(8, 13, 128), ((0, 0), (0, 3), (0, 0)))
        lines = reduce_z(lines.reshape(4, 32, 128))
        z3 = g3.done(partial)
        later = later.done(z3)
        tail = Line(links, z3)
        held = [z3]
    result, grad_input = ends(
        x,
        mixed,
        partial,
        own_r[1],
        own_g[1],
        hold(others, [partial]),
        w_out,
        row(b_out + b_down),
        row(ln2_gain),
        after=held,
    )

    if tuned:
        lines = hold(lines, [result]).reshape(2, 16, 128)
        pick = lambda i: lax.dynamic_index_in_dim(lines, i, 0, keepdims=False)
        lines, lines_other = pick(core), links.core(pick(1 - core))
        first_down, first_up = in_place(early, 1, [lines])
        lines = lines + hold(lines_other, [first_down])
        second_down, second_up = in_place(later, 2, [lines])
        lines = lines + hold(links.x(lines), [second_down])
        middle = middle.done(second_down)
        third_down, third_up = in_place(middle, 1, [lines], start=3)
        lines = lines + hold(links.y(lines), [third_down])
        tail = tail.done(third_down).reshape(6, 128, 128)
        shares, at = [], 0
        for v_ in vectors:
            n = v_.shape[0] // 1024
            shares.append(lines[at : at + n].reshape(-1))
            at += n
        halves = jnp.concatenate([first_up, second_up, third_up], 1)
        w_down_grad = jnp.concatenate([first_down, second_down, third_down], 0)
        w_out_grad = jnp.concatenate([middle[2], middle[5]], 1)
        blocks = [[tail[i] for i in (0, 3, 2)], [tail[i] for i in (1, 4, 5)]]
        blocks = jnp.stack([jnp.stack(b, 0) for b in blocks], 0)
        halves = jnp.concatenate([halves, blocks], 1)
        pick = lambda i: lax.dynamic_index_in_dim(halves, i, 0, keepdims=False)
        mine, other = pick(core), links.core(pick(1 - core))
        first, second = jnp.where(core == 0, mine, other), jnp.where(core == 0, other, mine)
        both = jnp.stack([first, second], 0)
        w_up_grad = both[:, :4].reshape(1024, 128).T
        w_qkv_grad = both[:, 4:].transpose(1, 0, 2, 3).reshape(768, 128).T
    else:
        total = lax.psum(jnp.concatenate(vectors), ("batch", "seq"))
        shares, at = [], 0
        for v_ in vectors:
            share = v_.shape[0] // links.ns
            shares.append(lax.dynamic_slice_in_dim(total, at + place * share, share, 0))
            at += v_.shape[0]

        def scatter(full):
            part = lax.psum_scatter(full, "batch", scatter_dimension=1, tiled=True)
            return lax.psum_scatter(part, "seq", scatter_dimension=0, tiled=True)

        def of_core(half, axis):
            zero = jnp.zeros_like(half)
            pair = jnp.where(core == 0, half, zero), jnp.where(core == 1, half, zero)
            return jnp.stack(pair, axis)

        both = lambda send, keep: jnp.stack([keep, send], 0)
        groups = (c0, c1, c2)
        slots = lambda pair, n, m, k: both(pair[0][:, :, m : m + n], pair[1][:, :, k : k + n])
        sizes = ((2, 0, 0), (4, 0, 0), (2, 0, 0))
        up = [slots(c[4:6], *size) for c, size in zip(groups, sizes)]
        up = jnp.concatenate(up, 3).reshape(2, 2, 4, 4, 2, 128, 128)
        up = of_core(up.transpose(2, 4, 6, 1, 0, 3, 5).reshape(1024, 4, 512), 2)
        down = [slots(c[6:8], *size) for c, size in zip(groups, sizes)]
        down = jnp.concatenate(down, 3).reshape(2, 2, 4, 4, 2, 128, 128)
        down = of_core(down.transpose(2, 3, 5, 0, 1, 4, 6).reshape(4, 512, 1024), 1)
        by_x = slots(out_pieces[:2], 1, 2, 2).swapaxes(0, 1)
        out = jnp.concatenate([by_x, slots(out_pieces[2:], 1, 2, 2)], 3)
        out = out.transpose(2, 4, 0, 1, 3, 5).reshape(4, 128, 1024)
        by_x = both(*last_parts[:2]).swapaxes(0, 1)
        by_y = both(*last_parts[2:])
        parts = [by_x[:, :, :, :2], by_y[:, :, :, :2]]
        parts.append(jnp.stack([by_x[:, :, :, 2], by_y[:, :, :, 2]], 3))
        qkv = [p.transpose(2, 3, 5, 0, 1, 4).reshape(1024, 4, 128) for p in parts]
        w_up_grad = scatter(up.reshape(1024, 4096))
        w_down_grad = scatter(down.reshape(4096, 1024))
        w_out_grad = scatter(of_core(out, 1).reshape(1024, 1024))
        w_qkv_grad = scatter(of_core(jnp.stack(qkv, 2), 3).reshape(1024, 3072))

    shape = hidden_in.shape
    return (
        result.reshape(shape),
        grad_input.reshape(shape),
        shares[0],
        shares[1],
        shares[2],
        shares[3],
        w_qkv_grad,
        shares[4],
        w_out_grad,
        shares[5],
        w_up_grad,
        shares[6],
        w_down_grad,
        shares[5],
        shares[7],
    )


def solution(mesh):
    links = Links(mesh)
    rows = P("batch", "seq", None)
    spread = P("seq", "batch")
    return jax.shard_map(
        functools.partial(per_device, links),
        mesh=mesh,
        in_specs=(rows, rows, P("batch"), P("batch", "seq")) + (P(),) * 14,
        out_specs=(rows, rows)
        + (P("seq"),) * 4
        + (spread, P("seq"), spread, P("seq"), spread, P("seq"), spread, P("seq"), P("seq")),
        check_vma=False,
    )
```

```python
import functools
import math

import jax
import jax.numpy as jnp
import numpy as np
from jax import lax
from jax.experimental import pallas as pl
from jax.experimental.pallas import tpu as pltpu
from jax.sharding import PartitionSpec as P

f32 = jnp.float32
bf16 = jnp.bfloat16
struct = jax.ShapeDtypeStruct
HEADS = 16
HEAD_DIM = 64
ROT = 16
LEN_BLK = 256
ROW_TILE = 256
HG = 256
ROOT_HALF = math.sqrt(0.5)
NORMAL_PEAK = 1.0 / math.sqrt(2.0 * math.pi)
norm_epsilon = 1e-05
rope_base = 10000.0
VMEM_BYTES = 60 * 1024 * 1024


def params():
    return pltpu.CompilerParams(vmem_limit_bytes=VMEM_BYTES)


def dot(a, b, ca, cb):
    return lax.dot_general(a, b, (((ca,), (cb,)), ((), ())), preferred_element_type=f32)


def iota(shape, dim):
    return lax.broadcasted_iota(jnp.int32, shape, dim)


def split(x):
    hi = x.astype(bf16)
    return hi, (x - hi.astype(f32)).astype(bf16)


def ordered_call(kernel, args, after, *, in_specs, grid, out_specs, out_shape, prefetch=0, **kw):
    after = [a for a in after if a is not None]
    n_in = len(args)

    def body(*refs):
        kernel(*refs[:n_in], *refs[n_in + len(after) :])

    in_specs = list(in_specs) + [pl.BlockSpec(memory_space=pl.ANY)] * len(after)
    return pl.pallas_call(
        body,
        grid_spec=pltpu.PrefetchScalarGridSpec(
            num_scalar_prefetch=prefetch, grid=grid, in_specs=in_specs, out_specs=out_specs
        ),
        out_shape=out_shape,
        compiler_params=params(),
        **kw,
    )(*args, *after)


def ffn_kernel(aliased, pos, a2_own, a2_other, g_own, g_other, *refs):
    w_ups, w_downs, biases = refs[:2], refs[2:4], refs[4:6]
    refs = refs[6 + aliased :]
    gelus, grads, (up_send, up_keep, down_send, down_keep, b_sum) = refs[:2], refs[2:4], refs[4:]
    me = pos[0]
    w_up = jnp.concatenate([w[...] for w in w_ups], axis=1)
    w_down = jnp.concatenate([w[...] for w in w_downs], axis=0)
    bias = jnp.concatenate([b[...] for b in biases], axis=1)
    d_up = d_down = total = None
    for half, (a2, g) in enumerate(((a2_own, g_own), (a2_other, g_other))):
        rows_in, grad_in = a2[...], g[...]
        pre = dot(rows_in, w_up, 1, 0) + bias
        grad_gelu = dot(grad_in, w_down, 1, 1)
        cdf = 0.5 + 0.5 * lax.erf(pre * ROOT_HALF)
        gelu = (pre * cdf).astype(bf16)
        slope = cdf + pre * (NORMAL_PEAK * jnp.exp(-0.5 * pre * pre))
        grad_pre = (grad_gelu * slope).astype(bf16)
        for j in range(2):
            gelus[j][half, 0] = gelu[:, 128 * j : 128 * j + 128]
            grads[j][half, 0] = grad_pre[:, 128 * j : 128 * j + 128]
        parts = (
            dot(grad_pre, rows_in, 0, 0),
            dot(gelu, grad_in, 0, 0),
            jnp.sum(grad_pre.astype(f32), axis=0, keepdims=True),
        )
        if half == 0:
            d_up, d_down, total = parts
        else:
            d_up, d_down, total = d_up + parts[0], d_down + parts[1], total + parts[2]
    b_sum[0] = total
    mx = lax.rem(me, 2)
    keep, send = swapped(mx, d_up[:128], d_up[128:])
    for n in range(8):
        up_send[0, n // 2, n % 2] = send[:, n * 128 : (n + 1) * 128]
        up_keep[0, n // 2, n % 2] = keep[:, n * 128 : (n + 1) * 128]
    for j in range(2):
        squares = relative(d_down[128 * j : 128 * j + 128], me)
        for rx in range(2):
            for half in range(2):
                part = slice(128 * half, 128 * half + 128)
                down_send[rx, j, half] = squares[rx][1][:, part]
                down_keep[rx, j, half] = squares[rx][0][:, part]


def swapped(bit, first, second):
    return jnp.where(bit == 0, first, second), jnp.where(bit == 0, second, first)


def relative(tile, me):
    by_y = swapped(lax.div(me, 2), tile[:, :512], tile[:, 512:])
    by_yx = [swapped(lax.rem(me, 2), part[:, :256], part[:, 256:]) for part in by_y]
    return [[by_yx[y][x] for y in range(2)] for x in range(2)]


def once(shape, where):
    return pl.BlockSpec(shape, where, pipeline_mode=pl.Buffered(1))


def ffn_chunk(first, count, pos, a2, g, w_up, w_down, b_up, earlier=(), filled=(), more=0, after=()):
    rows, width = a2[0].shape
    block = lambda j, k, i, p: (2 * (2 * i + j) + p[1]) * 4 + first + k
    cols = lambda j: (lambda k, i, p: (0, block(j, k, i, p)))
    lines = lambda j: (lambda k, i, p: (block(j, k, i, p), 0))
    whole = lambda k, i, p: (0, 0)
    place = lambda k, i, p: (0, i * 4 + first + k, 0, 0)
    in_specs = (
        [once((rows, width), whole)] * 4
        + [pl.BlockSpec((width, 128), cols(j)) for j in range(2)]
        + [pl.BlockSpec((128, width), lines(j)) for j in range(2)]
        + [pl.BlockSpec((1, 128), cols(j)) for j in range(2)]
    )
    args = [pos, *a2, *g, w_up, w_up, w_down, w_down, b_up, b_up]
    given = [*enumerate(earlier), *enumerate(filled, 4)]
    aliases = {len(args) + i: out for i, (out, _) in enumerate(given)}
    in_specs = in_specs + [pl.BlockSpec(memory_space=pl.ANY)] * len(given)
    args = args + [value for _, value in given]
    pieces = [struct((2, 4, 2 * count + extra, 128, 128), f32) for extra in (more, 0)] * 2
    pieces = [struct(v.shape, f32) for v in filled] or pieces
    return ordered_call(
        functools.partial(ffn_kernel, len(given)),
        args,
        after,
        prefetch=1,
        grid=(count, 2),
        in_specs=in_specs,
        out_specs=[pl.BlockSpec((2, 1, rows, 128), place)] * 4
        + [
            pl.BlockSpec(
                (1, 4, 2, 128, 128),
                lambda k, i, p: (lax.bitwise_xor(i, lax.div(p[0], 2)), 0, k, 0, 0),
            )
        ]
        * 2
        + [pl.BlockSpec((2, 2, 2, 128, 128), lambda k, i, p: (0, i, k, 0, 0))] * 2
        + [pl.BlockSpec((1, 1, 256), lambda k, i, p: (k * 2 + i, 0, 0))],
        out_shape=[struct((2, 8, rows, 128), bf16)] * 4
        + pieces
        + [struct((count * 2, 1, 256), f32)],
        input_output_aliases=aliases,
        cost_estimate=cost(f"ffn{first}"),
        name="ffn_chunk",
    )


def out_grad_kernel(pos, own, early, late, g_own, g_other, x_send, x_keep, y_send, y_keep):
    other = jnp.where(pl.program_id(0) < 2, early[...], late[...]).astype(bf16)
    tile = dot(own[...], g_own[...], 0, 0) + dot(other, g_other[...], 0, 0)
    squares = relative(tile, pos[0])
    for n in range(2):
        x_send[n, 0, 0] = squares[1][n][:, :128]
        x_keep[n, 0, 0] = squares[0][n][:, :128]
        y_send[n, 0, 0] = squares[n][1][:, 128:]
        y_keep[n, 0, 0] = squares[n][0][:, 128:]


def out_grad(pos, mixed, others, g, after=()):
    rows, width = g[0].shape
    whole = lambda z, p: (0, 0)
    return ordered_call(
        out_grad_kernel,
        [pos, mixed, *others, *g],
        after,
        prefetch=1,
        grid=(4,),
        in_specs=[
            pl.BlockSpec((rows, 128), lambda z, p: (0, 2 * z + p[1])),
            pl.BlockSpec((rows, 128), lambda z, p: (0, lax.min(z, 1))),
            pl.BlockSpec((rows, 128), lambda z, p: (0, lax.max(z - 2, 0))),
            once((rows, width), whole),
            once((rows, width), whole),
        ],
        out_specs=[pl.BlockSpec((2, 1, 1, 128, 128), lambda z, p: (0, z, 2, 0, 0))] * 4,
        out_shape=[struct((2, 4, 3, 128, 128), f32)] * 4,
        cost_estimate=cost("out_grad"),
        name="out_grad",
    )


def second_kernel(at, slots, u_keep, u_one, d_keep, d_one, *refs):
    x_o, y_o = refs[-2:]
    own = slice(at, at + slots)
    y_o[...] = (u_keep[...] + u_one[:, :, own]).reshape(y_o.shape)
    x_o[...] = (d_keep[...] + d_one[:, :, own]).reshape(x_o.shape)


def second_stage(keeps, ones, at, bundles=None, into=0):
    slots, total = keeps[0].shape[2], ones[0].shape[2]
    half = slots // 2
    keep = pl.BlockSpec((1, 2, slots, 128, 128), lambda i: (1, i, 0, 0, 0))
    one = pl.BlockSpec((1, 2, total, 128, 128), lambda i: (1, i, 0, 0, 0))
    if bundles:
        out = pl.BlockSpec((1, 4, half, 128, 128), lambda i: (i, 0, into // half, 0, 0))
        shapes = [struct(v.shape, f32) for v in bundles]
    else:
        out = pl.BlockSpec((2, slots, 128, 128), lambda i: (i, 0, 0, 0))
        shapes = [struct((4, slots, 128, 128), f32)] * 2
    return ordered_call(
        functools.partial(second_kernel, at, slots),
        [keeps[0], ones[0], keeps[1], ones[1], *(bundles or [])],
        [],
        grid=(2,),
        in_specs=[keep, one] * 2 + [pl.BlockSpec(memory_space=pl.ANY)] * len(bundles or []),
        out_specs=[out] * 2,
        out_shape=shapes,
        input_output_aliases={4: 0, 5: 1} if bundles else {},
        cost_estimate=cost("second_stage"),
        name="second_stage",
    )


def finish_kernel(at, slots, cut, direct, pos, u_keep, u_one, u_two, d_keep, d_one, d_two, *refs):
    outs = refs[-4:] if direct else refs[-2:]
    more = refs[: -len(outs)]
    own = slice(at, at + slots)
    step = pl.program_id(0)
    parts = []
    for keep, one, two in ((u_keep, u_one, u_two), (d_keep, d_one, d_two)):
        if cut is None:
            second = two[...]
        else:
            second = two[0, :, cut[0] : cut[1]].reshape(2, slots, 128, 128)
        parts.append((keep[0] + one[0, :, own] + second).reshape(2, slots * 128, 128))
    both = jnp.concatenate(parts + [rows[...] for rows in more], 1)
    if not direct:
        kept, sent = swapped(lax.rem(pos[2], 2), both[0], both[1])
        outs[0][0], outs[1][0] = kept, sent
        return

    def put(out, value):
        out[...] = value

    for low in range(2):
        ahead = lax.rem(2 * step + low - pos[2] + 4, 4)
        for n, out in enumerate(outs):
            pl.when(ahead == n)(functools.partial(put, out, both[low]))


def finish(pos, keeps, ones, at, twos, cut, more=(), direct=False):
    slots, total = keeps[0].shape[2], ones[0].shape[2]
    keep = pl.BlockSpec((1, 2, slots, 128, 128), lambda i, p: (0, i, 0, 0, 0))
    one = pl.BlockSpec((1, 2, total, 128, 128), lambda i, p: (0, i, 0, 0, 0))
    if cut is None:
        two = pl.BlockSpec((2, slots, 128, 128), lambda i, p: (i, 0, 0, 0))
    else:
        two = pl.BlockSpec((1, 4, twos[0].shape[2], 128, 128), lambda i, p: (i, 0, 0, 0, 0))
    lines = 256 * slots + sum(m.shape[1] for m in more)
    if direct:
        out = [pl.BlockSpec((lines, 128), lambda i, p: (0, 0))] * 4
        shapes = [struct((lines, 128), f32)] * 4
    else:
        out = [pl.BlockSpec((1, lines, 128), lambda i, p: (i, 0, 0))] * 2
        shapes = [struct((2, lines, 128), f32)] * 2
    return ordered_call(
        functools.partial(finish_kernel, at, slots, cut, direct),
        [pos, keeps[0], ones[0], twos[0], keeps[1], ones[1], twos[1], *more],
        [],
        prefetch=1,
        grid=(2,),
        in_specs=[keep, one, two] * 2
        + [pl.BlockSpec((2, m.shape[1], 128), lambda i, p: (i, 0, 0)) for m in more],
        out_specs=out,
        out_shape=shapes,
        cost_estimate=cost(f"finish{slots}"),
        name="finish",
    )


def qkv_grad_kernel(pos, a1_own, a1_other, *refs):
    own, other, (x_send, x_keep, y_send, y_keep) = refs[:3], refs[3:6], refs[6:]
    left = jnp.concatenate([r[0] for r in own], 1)
    left_other = jnp.concatenate([r[0].astype(bf16) for r in other], 1)
    tile = dot(left, a1_own[...], 0, 0) + dot(left_other, a1_other[...], 0, 0)
    step = pl.program_id(0)
    block = lambda j, n: tile[128 * j : 128 * j + 128, n * 128 : (n + 1) * 128]

    def put(out, whole, half):
        for z in range(4):
            out[0, z, 0] = block(whole, 2 * z)
            out[0, z, 1] = block(whole, 2 * z + 1)
            out[0, z, 2] = block(2, 2 * z + half)

    pl.when(lax.rem(step, 2) == 1)(lambda: put(x_send, 0, 0))
    pl.when(lax.rem(step, 2) == 0)(lambda: put(x_keep, 0, 0))
    pl.when(step >= 2)(lambda: put(y_send, 1, 1))
    pl.when(step < 2)(lambda: put(y_keep, 1, 1))


def qkv_grad(pos, a1, grad_proj, other, after=()):
    rows, width = a1[0].shape
    whole = lambda n, p: (0, 0)

    def source(j, halves):
        def where(n, p):
            unit = lax.bitwise_xor(n, p[0]) * 3 + j
            at = lax.rem(unit, 4)
            return (lax.div(unit, 4), 0, at * 2 + p[1] if halves else at)

        return where

    out = lambda at: pl.BlockSpec((1, 4, 3, 128, 128), lambda n, p: (at(n), 0, 0, 0, 0))
    return ordered_call(
        qkv_grad_kernel,
        [pos, *a1] + [grad_proj] * 3 + [other] * 3,
        after,
        prefetch=1,
        grid=(4,),
        in_specs=[once((rows, width), whole)] * 2
        + [pl.BlockSpec((1, rows, 128), source(j, True)) for j in range(3)]
        + [pl.BlockSpec((1, rows, 128), source(j, False)) for j in range(3)],
        out_specs=[
            out(lambda n: lax.div(n, 2)),
            out(lambda n: lax.div(n, 2)),
            out(lambda n: lax.max(n - 2, 0)),
            out(lambda n: lax.min(n, 1)),
        ],
        out_shape=[struct((2, 4, 3, 128, 128), f32)] * 4,
        cost_estimate=cost("qkv_grad"),
        name="qkv_grad",
    )


LONG, SHORT = 10**11, 1
WEIGHTS = {"first_norm": LONG, "hidden0": LONG, "blocks": LONG, "in_place": LONG, "ends": LONG, "finish2": LONG}


def cost(name):
    flops = WEIGHTS.get(name, SHORT)
    return pl.CostEstimate(flops=flops, bytes_accessed=1, transcendentals=0)


def rotate(x, cos, sin_first, sin_second):
    n = x.shape[1]
    half = ROT // 2
    return x * cos + pltpu.roll(x, n - half, 1) * sin_first + pltpu.roll(x, half, 1) * sin_second


def three(x, w_hi, w_lo):
    hi, lo = split(x)
    return dot(hi, w_hi, 1, 0) + dot(lo, w_hi, 1, 0) + dot(hi, w_lo, 1, 0)


def pair_mask():
    return (iota((128, 128), 0) // 64) == (iota((128, 128), 1) // 64)


def pack(first, second):
    mask = pair_mask()
    first = jnp.where(mask, first, 0.0)
    second = jnp.where(mask, second, 0.0)
    first = first + pltpu.roll(first, 64, 1)
    second = second + pltpu.roll(second, 64, 1)
    return jnp.where(iota((128, 128), 1) < 64, first, second)


def unpack(packed):
    mask = pair_mask()
    low = iota((128, 128), 1) < 64
    turned = pltpu.roll(packed, 64, 1)
    return (
        jnp.where(mask, jnp.where(low, packed, turned), 0.0),
        jnp.where(mask, jnp.where(low, turned, packed), 0.0),
    )


def to_column(row):
    eye = iota((128, 128), 0) == iota((128, 128), 1)
    return jnp.sum(jnp.where(eye, jnp.broadcast_to(row, (128, 128)), 0.0), axis=1, keepdims=True)


def each_head(x):
    mask = iota((1, 128), 1) < 64
    zero = jnp.zeros_like(x)
    return jnp.where(mask, x, zero), jnp.where(mask, zero, x)


def feature_kernel(
    pos, a1, wq, wk, wv, bq, bk, bv, fw, matrix, cos, sin1, sin2, valid, qf_o, kf_o, v_o, own, send
):
    x = a1[...]
    count = x.shape[0] // LEN_BLK
    rows = lambda i: slice(LEN_BLK * i, LEN_BLK * (i + 1))
    turns = cos[...], sin1[...], sin2[...]
    weight = fw[...]
    halves = split(matrix[...])
    q = [dot(x[rows(i)], wq[...], 1, 0) for i in range(count)]
    k = [dot(x[rows(i)], wk[...], 1, 0) for i in range(count)]
    q = [rotate(part + bq[...], *turns) for part in q]
    v = [(dot(x[rows(i)], wv[...], 1, 0) + bv[...]).astype(bf16) for i in range(count)]
    k = [rotate(part + bk[...], *turns) for part in k]
    q = [three(part, *halves) for part in q]
    k = [three(part, *halves) for part in k]
    for i in range(count):
        qf_o[rows(i)] = (weight * jnp.exp(q[i])).astype(bf16)
        kf = (weight * jnp.exp(k[i])).astype(bf16) * valid[rows(i)].astype(bf16)
        kf_o[rows(i)] = kf
        k[i] = kf
        v_o[rows(i)] = v[i]
    states = []
    for i in range(count):
        state = [
            dot(k[i][:, 128 * p : 128 * p + 128], v[i][:, 128 * p : 128 * p + 128], 0, 0)
            for p in range(2)
        ]
        norm = jnp.sum(k[i].astype(f32), axis=0, keepdims=True)
        lines = norm_rows(norm[:, :128], norm[:, 128:])
        states.append(jnp.concatenate([pack(state[0], state[1]), lines], 0))
    put_states(pos[1], states, own, send)


def norm_rows(first, second):
    line = iota((8, 128), 0)
    return jnp.where(line == 0, first, jnp.where(line == 1, second, 0.0))


def put_states(core, states, own, send):
    half = len(states) // 2
    for j in range(half):
        first, second = states[j], states[half + j]
        own[j, 0] = jnp.where(core == 0, first, second)
        send[j, 0] = jnp.where(core == 0, second, first)


def state_of(core, pair, i):
    here, there = pair
    half = here.shape[0]
    j = i % half
    return jnp.where(core == i // half, here[j, 0], there[j, 0])


def scores(qp, kp, causal):
    raw = dot(jnp.concatenate(each_head(qp), 0), kp, 1, 1)
    return [
        jnp.where(causal, raw[LEN_BLK * h : LEN_BLK * (h + 1)], 0.0).astype(bf16)
        for h in range(2)
    ]


def lower(n):
    return iota((n, n), 0) >= iota((n, n), 1)


def mix_kernel(pos, g, wo, qf, kf, v, here, there, mix_o, dn_o, dd_o, own, send, *sends):
    count = qf.shape[0] // LEN_BLK
    mask = pair_mask()
    lane = iota((1, 128), 1)
    first = lane < 64
    causal = lower(LEN_BLK)
    one0, one1 = each_head(jnp.ones((LEN_BLK, 128), bf16))
    cells = [(i, p) for i in range(count) for p in range(2)]
    rows = lambda i: slice(LEN_BLK * i, LEN_BLK * (i + 1))
    cols = lambda p: slice(128 * p, 128 * p + 128)
    q = {(i, p): qf[rows(i), cols(p)] for i, p in cells}
    s = {(i, p): scores(q[i, p], kf[rows(i), cols(p)], causal) for i, p in cells}
    grad_mixed = dot(g[...], wo[...], 1, 1)
    both = {}
    for i in range(count):
        carried = state_of(pos[1], (here, there), i)
        state = unpack(carried[:128])
        for p in range(2):
            column = to_column(carried[128 + p : 129 + p])
            norm = jnp.where(mask, jnp.broadcast_to(column, (128, 128)), 0.0)
            hi, lo = split(jnp.concatenate([state[p], norm], 1))
            qp = q[i, p]
            both[i, p] = dot(jnp.concatenate([qp, qp], 1), jnp.concatenate([hi, lo], 0), 1, 0)
    for i, p in cells:
        v0, v1 = each_head(v[rows(i), cols(p)])
        right = jnp.concatenate(
            [jnp.concatenate([v0, one0], 1), jnp.concatenate([v1, one1], 1)], 0
        )
        both[i, p] = both[i, p] + dot(jnp.concatenate(s[i, p], 1), right, 1, 0)
    mixes, dns, norms, grads, sums = {}, {}, {}, {}, {}
    for i, p in cells:
        inverse = 1.0 / both[i, p][:, 128:]
        mixed = both[i, p][:, :128] * inverse
        low = mixed.astype(bf16)
        mix_o[rows(i), cols(p)] = low
        mixes[i, p] = low
        dn = (grad_mixed[rows(i), cols(p)] * inverse).astype(bf16)
        dn_o[rows(i), cols(p)] = dn
        dns[i, p] = dn
        product = -(dn.astype(f32) * mixed)
        d0 = jnp.sum(jnp.where(first, product, 0.0), axis=1, keepdims=True)
        d1 = jnp.sum(jnp.where(first, 0.0, product), axis=1, keepdims=True)
        sums[i, p] = d0, d1
    for i, p in cells:
        grads[i, p] = dot(q[i, p], dns[i, p], 0, 0)
    for i, p in cells:
        d0, d1 = sums[i, p]
        norms[i, p] = column_sum(q[i, p].astype(f32) * jnp.where(first, d0, d1))
    states = []
    for i in range(count):
        lines = jnp.zeros((LEN_BLK, 128), f32)
        for p in range(2):
            d0, d1 = sums[i, p]
            lines = jnp.where(lane == 2 * p, d0, jnp.where(lane == 2 * p + 1, d1, lines))
        dd_o[0, rows(i)] = lines
        lines = norm_rows(norms[i, 0], norms[i, 1])
        states.append(jnp.concatenate([pack(grads[i, 0], grads[i, 1]), lines], 0))
        other_half = jnp.where(pos[1] == 0, mixes[i, 1].astype(f32), mixes[i, 0].astype(f32))

        def put(out, lines=rows(i), other_half=other_half):
            out[lines] = other_half

        for n, out in enumerate(sends):
            pl.when(lax.div(pl.program_id(0), 2) == n)(functools.partial(put, out))
    put_states(pos[1], states, own, send)


def back_kernel(
    pos, qf, kf, v, dn, dd, here, there, l_here, l_there, fw, matrix, cos, sin1, sin2, *outs
):
    gp_o, send_o, bias_o, fw_o = outs
    count = qf.shape[0] // LEN_BLK
    step = pl.program_id(1)
    before = [state_of(pos[1], (here, there), i) for i in range(count)]
    after = [state_of(pos[1], (l_here, l_there), i) for i in range(count)]
    causal = lower(LEN_BLK)
    lane = iota((1, 128), 1)
    first = lane < 64
    turns = cos[...], -sin1[...], -sin2[...]
    halves = split(matrix[...])
    cells = [(i, p) for i in range(count) for p in range(2)]
    rows = lambda i: slice(LEN_BLK * i, LEN_BLK * (i + 1))
    cols = lambda p: slice(128 * p, 128 * p + 128)
    q, k, vv, d, s, t, col = {}, {}, {}, {}, {}, {}, {}
    for i, p in cells:
        q[i, p], k[i, p] = qf[rows(i), cols(p)], kf[rows(i), cols(p)]
        vv[i, p], d[i, p] = v[rows(i), cols(p)], dn[rows(i), cols(p)]
        col[i, p] = [
            jnp.sum(jnp.where(lane == 2 * p + h, dd[0, rows(i)], 0.0), axis=1, keepdims=True)
            for h in range(2)
        ]
    for c in cells:
        s[c] = scores(q[c], k[c], causal)
        raw = dot(jnp.concatenate(each_head(d[c]), 0), vv[c], 1, 1)
        t[c] = [
            jnp.where(causal, raw[LEN_BLK * h : LEN_BLK * (h + 1)] + col[c][h], 0.0).astype(bf16)
            for h in range(2)
        ]
    dq, dk, dv = {}, {}, {}
    for i in range(count):
        state, later = unpack(before[i][:128]), unpack(after[i][:128])
        for p in range(2):
            c = i, p
            s_hi, s_lo = split(state[p])
            d_hi, d_lo = split(later[p])
            twice = lambda x: jnp.concatenate([x, x], 1)
            dq[c] = dot(twice(d[c]), jnp.concatenate([s_hi, s_lo], 1), 1, 1)
            dk[c] = dot(twice(vv[c]), jnp.concatenate([d_hi, d_lo], 1), 1, 1)
            dv[c] = dot(twice(k[c]), jnp.concatenate([d_hi, d_lo], 0), 1, 0)
    for c in cells:
        dq[c] = dq[c] + dot(jnp.concatenate(t[c], 1), jnp.concatenate(each_head(k[c]), 0), 1, 0)
        dk[c] = dk[c] + dot(jnp.concatenate(t[c], 0), jnp.concatenate(each_head(q[c]), 0), 0, 0)
        dv[c] = dv[c] + dot(jnp.concatenate(s[c], 0), jnp.concatenate(each_head(d[c]), 0), 0, 0)
    for i, p in cells:
        c = i, p
        norm = jnp.where(first, *col[c]) * before[i][128 + p : 129 + p]
        dq[c] = (dq[c] + norm) * q[c].astype(f32)
        dk[c] = (dk[c] + after[i][128 + p : 129 + p]) * k[c].astype(f32)
    whole = lambda parts: jnp.concatenate(
        [jnp.concatenate([parts[i, 0], parts[i, 1]], 1) for i in range(count)], 0
    )
    dq, dk, dv = whole(dq), whole(dk), whole(dv)
    tall = [jnp.concatenate([turn] * count, 0) for turn in turns]
    grads = (
        rotate(three(dq, *halves), *tall).astype(bf16),
        rotate(three(dk, *halves), *tall).astype(bf16),
        dv.astype(bf16),
    )
    for n in range(3):
        gp_o[n] = grads[n]
        wide = grads[n].astype(f32)
        other_half = jnp.where(pos[1] == 0, wide[:, 128:], wide[:, :128])
        send_o[n] = other_half
    totals = [column_sum(part.astype(f32)) for part in grads]
    totals.append(column_sum(dq + dk) / fw[...])

    @pl.when(step == 0)
    def _():
        for n in range(3):
            bias_o[n] = totals[n]
        fw_o[...] = totals[3]

    @pl.when(step > 0)
    def _():
        for n in range(3):
            bias_o[n] = bias_o[n] + totals[n]
        fw_o[...] = fw_o[...] + totals[3]


def attention_specs(seqs, per, more=0):
    rows = LEN_BLK * per
    return dict(
        grid=(4, seqs // per),
        wide=pl.BlockSpec((rows, 1024), lambda h, g, *_: (g, 0)),
        head=pl.BlockSpec((rows, HG), lambda h, g, *_: (g, h)),
        state=pl.BlockSpec((seqs // 2, 1, 136, 128), lambda h, g, *_: (0, h, 0, 0)),
        row=pl.BlockSpec((1, HG), lambda h, g, *_: (0, h)),
        table=pl.BlockSpec((256, 256), lambda h, g, *_: (0, 0)),
        dden=pl.BlockSpec((1, rows, 128), lambda h, g, *_: (h, g, 0)),
    )


def features(pos, a1, w_qkv, b_qkv, feat_weight, matrix, turns, valid, after=()):
    rows = a1.shape[0]
    seqs = per = rows // LEN_BLK
    s = attention_specs(seqs, per)
    weights = [pl.BlockSpec((1024, HG), lambda h, g, *_, o=o: (0, 4 * o + h)) for o in range(3)]
    biases = [pl.BlockSpec((1, HG), lambda h, g, *_, o=o: (0, 4 * o + h)) for o in range(3)]
    return ordered_call(
        feature_kernel,
        [pos, a1, w_qkv, w_qkv, w_qkv, b_qkv, b_qkv, b_qkv, feat_weight, matrix, *turns, valid],
        after,
        prefetch=1,
        grid=s["grid"],
        in_specs=[s["wide"], *weights, *biases, s["row"]]
        + [s["table"]] * 4
        + [pl.BlockSpec((LEN_BLK * per, 1), lambda h, g, *_: (g, 0))],
        out_specs=[s["head"]] * 3 + [s["state"]] * 2,
        out_shape=[struct((rows, 1024), bf16)] * 3
        + [struct((seqs // 2, 4, 136, 128), f32)] * 2,
        cost_estimate=cost("features"),
        name="features",
    )


def mixing(pos, g, w_out, qf, kf, v, state, after=()):
    rows = g.shape[0]
    seqs = per = rows // LEN_BLK
    steps = seqs // per
    s = attention_specs(seqs, per)
    return ordered_call(
        mix_kernel,
        [pos, g, w_out, qf, kf, v, *state],
        after,
        prefetch=1,
        grid=s["grid"],
        in_specs=[s["wide"], pl.BlockSpec((HG, 1024), lambda h, g, *_: (h, 0))]
        + [s["head"]] * 3
        + [s["state"]] * 2,
        out_specs=[
            s["head"],
            s["head"],
            s["dden"],
            s["state"],
            s["state"],
            pl.BlockSpec(
                (LEN_BLK * per, 128),
                lambda h, g, *_: (lax.select(h < 2, g, 0 * g + steps - 1), lax.min(h, 1)),
            ),
            pl.BlockSpec(
                (LEN_BLK * per, 128),
                lambda h, g, *_: (lax.select(h < 2, 0 * g, g), lax.max(h - 2, 0)),
            ),
        ],
        out_shape=[
            struct((rows, 1024), bf16),
            struct((rows, 1024), bf16),
            struct((4, rows, 128), f32),
            struct((seqs // 2, 4, 136, 128), f32),
            struct((seqs // 2, 4, 136, 128), f32),
            struct((rows, 256), f32),
            struct((rows, 256), f32),
        ],
        cost_estimate=cost("mixing"),
        name="mixing",
    )

def backward(pos, qf, kf, v, dn, dd, state, later, feat_weight, matrix, turns, after=(), per=4):
    rows = qf.shape[0]
    seqs = rows // LEN_BLK
    s = attention_specs(seqs, per)
    return ordered_call(
        back_kernel,
        [pos, qf, kf, v, dn, dd, *state, *later, feat_weight, matrix, *turns],
        after,
        prefetch=1,
        grid=s["grid"],
        in_specs=[s["head"]] * 4
        + [s["dden"]]
        + [s["state"]] * 4
        + [s["row"]]
        + [s["table"]] * 4,
        out_specs=[
            pl.BlockSpec((3, LEN_BLK * per, HG), lambda h, g, *_: (0, g, h)),
            pl.BlockSpec((3, LEN_BLK * per, 128), lambda h, g, *_: (0, g, h)),
            pl.BlockSpec((3, 1, HG), lambda h, g, *_: (0, 0, h)),
            s["row"],
        ],
        out_shape=[
            struct((3, rows, 1024), bf16),
            struct((3, rows, 512), f32),
            struct((3, 1, 1024), f32),
            struct((1, 1024), f32),
        ],
        cost_estimate=cost("backward"),
        name="backward",
    )


def norm_parts(x):
    centre = x - jnp.mean(x, axis=-1, keepdims=True)
    r = lax.rsqrt(jnp.mean(centre * centre, axis=-1, keepdims=True) + norm_epsilon)
    return centre * r, r


def norm_back(grad, xhat, r, gain):
    e = grad * gain
    return r * (
        e
        - jnp.mean(e, axis=-1, keepdims=True)
        - xhat * jnp.mean(e * xhat, axis=-1, keepdims=True)
    )


def add_sums(out, sums):
    step = pl.program_id(0)
    new = jnp.concatenate(sums, 0)

    @pl.when(step == 0)
    def _():
        out[...] = new

    @pl.when(step > 0)
    def _():
        out[...] = out[...] + new


def column_sum(x):
    return jnp.sum(x, axis=0, keepdims=True)


def tiles(tile, fixed):
    wide = lambda n: pl.BlockSpec((tile, n), lambda i, *_: (i, 0))
    keep = [once(a.shape, lambda i, *_: (0, 0)) for a in fixed]
    return wide, keep


def norms_kernel(x, g, gain1, bias1, gain2, bias2, a1_o, a2_o, g_o, *x_o):
    xhat, _ = norm_parts(x[...].astype(f32))
    a1_o[...] = (xhat * gain1[...] + bias1[...]).astype(bf16)
    a2_o[...] = (xhat * gain2[...] + bias2[...]).astype(bf16)
    g_o[...] = g[...].astype(g_o.dtype)
    for out in x_o:
        out[...] = x[...].astype(f32)


def norms(x, g, *vectors, after=(), g_type=f32):
    rows, tile = x.shape[0], 256
    wide, keep = tiles(tile, vectors)
    return ordered_call(
        norms_kernel,
        [x, g, *vectors],
        after,
        grid=(rows // tile,),
        in_specs=[wide(1024)] * 2 + keep,
        out_specs=[wide(1024)] * (4 if g_type == f32 else 3),
        out_shape=[struct((rows, 1024), bf16)] * 2
        + [struct((rows, 1024), g_type)] * (2 if g_type == f32 else 1),
        cost_estimate=cost("norms"),
        name="norms",
    )


def hidden_rows_kernel(grad, filled, pos, *refs):
    acts, weights, outs = refs[:2], refs[2:6], refs[6 + filled :]
    send, keep = outs[-2:] if not grad else outs[2:4]
    total = None
    for b in range(4):
        act = acts[b % 2]
        act = jnp.concatenate([act[0, 4 * (b // 2) + n] for n in range(4)], 1)
        part = dot(act, weights[b][...], 1, 1 if grad else 0)
        total = part if total is None else total + part
    step = pl.program_id(0)
    steps = pl.num_programs(0) // 2

    @pl.when(step < steps)
    def _():
        send[0] = total

    @pl.when(step >= steps)
    def _():
        keep[...] = total

    if grad:
        x_own, x_other, sum_o = outs[0], outs[1], outs[4]
        xhat, _ = norm_parts(jnp.where(step < steps, x_other[...], x_own[...].astype(f32)))
        sums = [column_sum(total * xhat), column_sum(total)]
        add_sums(sum_o, sums + [jnp.zeros((6, 1024), f32)])


def hidden_rows(pos, acts, weight, rows_in=None, sends=None, after=()):
    grad = rows_in is not None
    rows, tile = acts[0].shape[2], ROW_TILE
    steps = rows // tile
    act = pl.BlockSpec(
        (1, 8, tile, 128), lambda i, p: (1 - lax.div(i, steps), 0, lax.rem(i, steps), 0)
    )
    if grad:
        part = lambda b: once((1024, 512), lambda i, p: (0, 2 * b + p[1]))
    else:
        part = lambda b: once((512, 1024), lambda i, p: (2 * b + p[1], 0))
    filled = [] if sends is None else [sends]
    ours = pl.BlockSpec((tile, 1024), lambda i, p: (lax.max(i - steps, 0), 0))
    theirs = pl.BlockSpec((tile, 1024), lambda i, p: (lax.min(i, steps - 1), 0))
    return ordered_call(
        functools.partial(hidden_rows_kernel, grad, len(filled)),
        [pos, *acts] + [weight] * 4 + filled + list(rows_in or ()),
        after,
        prefetch=1,
        grid=(2 * steps,),
        in_specs=[act] * 2
        + [part(b) for b in range(4)]
        + [pl.BlockSpec(memory_space=pl.ANY)] * len(filled)
        + [ours, theirs][: 2 * grad],
        out_specs=[
            pl.BlockSpec((1, tile, 1024), lambda i, p: (int(grad), lax.min(i, steps - 1), 0)),
            ours,
        ]
        + [pl.BlockSpec((8, 1024), lambda i, p: (0, 0))] * grad,
        out_shape=[struct((2, rows, 1024), f32), struct((rows, 1024), f32)]
        + [struct((8, 1024), f32)] * grad,
        input_output_aliases={7: 0} if filled else {},
        cost_estimate=cost(f"hidden{grad:d}"),
        name="hidden_rows",
    )


def first_norm_kernel(x, g, gp, w_qkv, gain, part_o, sum_o):
    xhat, r = norm_parts(x[...].astype(f32))
    grad_res = g[...].astype(f32)
    grad = dot(jnp.concatenate([gp[0], gp[1], gp[2]], 1), w_qkv[...], 1, 1)
    part_o[...] = grad_res + norm_back(grad, xhat, r, gain[...])
    sums = [column_sum(v) for v in (grad * xhat, grad, grad_res)]
    add_sums(sum_o, sums + [jnp.zeros((5, 1024), f32)])


def first_norm(x, g, gp, w_qkv, gain, after=()):
    rows, tile = x.shape[0], ROW_TILE
    fixed = (w_qkv, gain)
    wide, keep = tiles(tile, fixed)
    return ordered_call(
        first_norm_kernel,
        [x, g, gp, *fixed],
        after,
        grid=(rows // tile,),
        in_specs=[wide(1024)] * 2 + [pl.BlockSpec((3, tile, 1024), lambda i: (0, i, 0))] + keep,
        out_specs=[wide(1024), pl.BlockSpec((8, 1024), lambda i: (0, 0))],
        out_shape=[struct((rows, 1024), f32), struct((8, 1024), f32)],
        cost_estimate=cost("first_norm"),
        name="first_norm",
    )


def ends_kernel(x, mixed, part, own_r, other_r, own_g, other_g, w_out, bias, gain, res_o, out_o):
    value = x[...].astype(f32)
    out = dot(mixed[...], w_out[...], 1, 0) + (own_r[...] + other_r[0])
    res_o[...] = (value + out + bias[...]).astype(bf16)
    xhat, r = norm_parts(value)
    out_o[...] = part[...] + norm_back(own_g[...] + other_g[0], xhat, r, gain[...])


def ends(x, mixed, part, own_r, own_g, others, w_out, bias, gain, after=()):
    rows, tile = x.shape[0], ROW_TILE
    fixed = (w_out, bias, gain)
    wide, keep = tiles(tile, fixed)
    half = lambda n: pl.BlockSpec((1, tile, 1024), lambda i: (n, i, 0))
    return ordered_call(
        ends_kernel,
        [x, mixed, part, own_r, others, own_g, others, *fixed],
        after,
        grid=(rows // tile,),
        in_specs=[wide(1024)] * 4 + [half(0), wide(1024), half(1)] + keep,
        out_specs=[wide(1024)] * 2,
        out_shape=[struct((rows, 1024), bf16), struct((rows, 1024), f32)],
        cost_estimate=cost("ends"),
        name="ends",
    )


class Links:
    def __init__(self, mesh):
        self.nb, self.ns = mesh.shape["batch"], mesh.shape["seq"]
        self.tuned = (self.nb, self.ns) == (4, 8)

    def send(self, value, move):
        pairs = []
        for b in range(self.nb):
            for s in range(self.ns):
                to = move(b, s)
                if to is not None:
                    pairs.append((b * self.ns + s, to[0] * self.ns + to[1]))
        return lax.ppermute(value, ("batch", "seq"), pairs)

    def core(self, value):
        return self.send(value, lambda b, s: (b, s ^ 1))

    def x(self, value):
        return self.send(value, lambda b, s: (b ^ 1, s))

    def y(self, value):
        return self.send(value, lambda b, s: (b ^ 2, s))

    def ring(self, value, by):
        s = lax.axis_index("seq")
        got = self.send(value, lambda b, s: (b, (s + by) % self.ns))
        kept = s >= by if by > 0 else s < self.ns + by
        return got, kept

    def shift(self, value, by):
        inside = lambda s: 0 <= s < self.ns
        return self.send(value, lambda b, s: (b, s + by) if inside(s + by) else None)


def hold(value, behind):
    behind = [b for b in behind if b is not None]
    return lax.optimization_barrier((value, *behind))[0] if behind else value


class Group:
    def __init__(self, links, x_send, x_keep, y_send, y_keep, at=0):
        self.links, self.at = links, at
        self.keeps = x_keep, y_keep
        self.slots = x_keep.shape[2]
        if links.tuned:
            self.ones = [links.x(x_send), links.y(y_send)]
            self.twos = None

    def arrived(self, *behind):
        self.ones = [hold(one, behind) for one in self.ones]

    def second(self):
        x_out, y_out = second_stage(self.keeps, self.ones, self.at)
        self.twos, self.cut = [self.links.y(y_out), self.links.x(x_out)], None
        return x_out

    def second_in(self, x_send, y_send, into):
        return second_stage(self.keeps, self.ones, self.at, (x_send, y_send), into)

    def second_with(self, group):
        total = group.ones[0].shape[2]
        self.twos = group.ones[::-1]
        self.cut = (0, group.at) if group.at else (group.slots, total)

    def done(self, pos, *behind, more=(), direct=False):
        twos = [hold(two, behind) for two in self.twos]
        return finish(pos, self.keeps, self.ones, self.at, twos, self.cut, more, direct)


class Carried:
    def __init__(self, links, own, sent, reverse):
        self.links, self.own, self.sent, self.reverse = links, own, sent, reverse
        self.sign = -1 if reverse else 1
        self.core = lax.rem(lax.axis_index("seq"), 2)
        if links.tuned:
            self.other = links.core(sent)

    def near(self, *behind):
        if not self.links.tuned:
            return None
        self.other = hold(self.other, behind)
        self.mine = self.own + self.other
        self.one, self.one_kept = self.links.ring(self.mine, self.sign * 2)
        return self.mine

    def far(self, *behind):
        if not self.links.tuned:
            return None
        self.one = jnp.where(self.one_kept, hold(self.one, behind), 0.0)
        self.sum = self.mine + self.one
        self.two, self.two_kept = self.links.ring(self.sum, self.sign * 4)
        return self.sum

    def done(self, *behind):
        links = self.links
        if not links.tuned:
            halves = jnp.stack([self.own, self.sent], 0)
            total, step = jnp.where(self.core == 0, halves, halves[::-1]), 1
            while step < links.ns:
                total = total + links.shift(total, self.sign * step)
                step *= 2
            total = links.shift(total, self.sign)
            return tuple(jnp.where(self.core == 0, total, total[::-1]))
        self.two = hold(self.two, behind)
        before = self.one + jnp.where(self.two_kept, self.two, 0.0)
        second = self.core == (0 if self.reverse else 1)
        here = before + jnp.where(second, self.other, 0.0)
        there = before + jnp.where(second, 0.0, self.own)
        return here, links.core(there)


class Line:
    def __init__(self, links, parts):
        self.mine = parts[0]
        self.parts = [
            links.send(parts[by], lambda b, s, by=by: (b, (s + 2 * by) % 8)) for by in (2, 1, 3)
        ]

    def done(self, *behind):
        total = self.mine
        for part in self.parts:
            total = total + hold(part, behind)
        return total


class Halves:
    def __init__(self, links, kept, sent):
        self.links, self.kept = links, kept
        self.z = lax.div(lax.axis_index("seq"), 2)
        self.one = links.send(sent, lambda b, s: (b, s ^ 2))

    def arrived(self, *behind):
        self.one = hold(self.one, behind)

    def stage_two(self, *behind):
        self.arrived(*behind)
        self.high = lax.div(self.z, 2)
        out = self.pick(1 - self.high)
        self.two = self.links.send(out, lambda b, s: (b, s ^ 4))
        return out

    def pick(self, i):
        at = lambda v: lax.dynamic_index_in_dim(v, i, 0, keepdims=False)
        return at(self.kept) + at(self.one)

    def landed(self, *behind):
        self.two = hold(self.two, behind)

    def done(self, *behind):
        self.landed(*behind)
        return self.pick(self.high) + self.two


def dct_table(order):
    degree = np.arange(order, dtype=np.float64)[:, None]
    sample = np.arange(order, dtype=np.float64)[None, :]
    table = np.cos(math.pi * (sample + 0.5) * degree / order) * math.sqrt(2.0 / order)
    return np.where(degree == 0.0, table * math.sqrt(0.5), table).astype(np.float32)


def rotation_tables(positions):
    half = ROT // 2
    at = jnp.arange(HG, dtype=jnp.int32) % HEAD_DIM
    inverse = rope_base ** (-2.0 * (at % half).astype(f32) / ROT)
    angles = positions[:, None] * inverse[None, :]
    at = at[None, :]
    sin = jnp.sin(angles)
    return (
        jnp.where(at < ROT, jnp.cos(angles), 1.0),
        jnp.where(at < half, -sin, 0.0),
        jnp.where((at >= half) & (at < ROT), sin, 0.0),
    )


def head_blocks(directions, transposed):
    times = HG // HEAD_DIM
    left = jnp.tile(directions, (times, 1))
    right = np.tile(dct_table(HEAD_DIM), (1, times))
    dims = (((0,), (1,)), ((), ())) if transposed else (((1,), (0,)), ((), ()))
    args = (jnp.asarray(right), left) if transposed else (left, jnp.asarray(right))
    full = lax.dot_general(*args, dims, precision=lax.Precision.HIGHEST)
    block = np.arange(HG) // HEAD_DIM
    return jnp.where(block[:, None] == block[None, :], full, 0.0)


def in_place_kernel(count, start, blocks, down_o, up_o):
    for k in range(count):
        lines = slice(128 * k, 128 * k + 128)
        for half in range(2):
            down_o[lines, 128 * half : 128 * half + 128] = blocks[start + 2 * k + half]
            up_o[half, k] = blocks[2 * k + half]


def in_place(rows, count, after, start=None):
    blocks = rows.reshape(-1, 128, 128)
    return ordered_call(
        functools.partial(in_place_kernel, count, start or 2 * count),
        [blocks],
        after,
        grid=(1,),
        in_specs=[pl.BlockSpec(blocks.shape, lambda i: (0, 0, 0))],
        out_specs=[
            pl.BlockSpec((128 * count, 256), lambda i: (0, 0)),
            pl.BlockSpec((2, count, 128, 128), lambda i: (0, 0, 0, 0)),
        ],
        out_shape=[struct((128 * count, 256), f32), struct((2, count, 128, 128), f32)],
        cost_estimate=cost("in_place"),
        name="in_place",
    )


def blocks_kernel(left, right, out):
    full = lax.dot_general(
        left[...],
        right[...],
        (((1,), (0,)), ((), ())),
        precision=lax.Precision.HIGHEST,
        preferred_element_type=f32,
    )
    same = iota((HG, HG), 0) // HEAD_DIM == iota((HG, HG), 1) // HEAD_DIM
    out[...] = jnp.where(same, full, 0.0)


def head_blocks_after(directions, after):
    times = HG // HEAD_DIM
    left = jnp.tile(directions, (times, 1))
    right = jnp.asarray(np.tile(dct_table(HEAD_DIM), (1, times)))
    whole = lambda a: pl.BlockSpec(a.shape, lambda i: (0, 0))
    return ordered_call(
        blocks_kernel,
        [left, right],
        after,
        grid=(1,),
        in_specs=[whole(left), whole(right)],
        out_specs=pl.BlockSpec((HG, HG), lambda i: (0, 0)),
        out_shape=struct((HG, HG), f32),
        cost_estimate=cost("blocks"),
        name="head_blocks",
    )


def per_device(
    links,
    hidden_in,
    cotangent,
    lengths,
    key_mask,
    ln1_gain,
    ln1_bias,
    ln2_gain,
    ln2_bias,
    w_qkv,
    b_qkv,
    w_out,
    b_out,
    w_up,
    b_up,
    w_down,
    b_down,
    feat_weight,
    directions,
):
    seqs, block, width = hidden_in.shape
    rows = seqs * block
    tuned = links.tuned
    place = lax.axis_index("seq")
    me = lax.axis_index("batch") if tuned else 0 * place
    core = lax.rem(place, 2)
    pos = jnp.stack([me, core, lax.div(place, 2)]).astype(jnp.int32)
    places = place * block + jnp.arange(block, dtype=jnp.int32)
    valid = (places[None, :] < lengths[:, None]) & ((key_mask == 1) | (places[None, :] == 0))
    valid = valid.astype(f32).reshape(rows, 1)
    x = hidden_in.reshape(rows, width)
    g = cotangent.reshape(rows, width)
    row = lambda v: v.reshape(1, -1)
    gains = row(ln1_gain), row(ln1_bias), row(ln2_gain), row(ln2_bias)
    a1, a2, g_wide, x_wide = norms(x, g, *gains)
    x_other, g_other = links.core(x_wide), links.core(g_wide)

    forth = head_blocks(directions, True)
    turns = rotation_tables(places.astype(f32))
    weights = row(feat_weight)

    qf, kf, v, state, state_sent = features(
        pos, a1, w_qkv, row(b_qkv), weights, forth, turns, valid
    )
    forward = Carried(links, state, state_sent, False)
    x_other = hold(x_other, [state])
    a1_o, a2_o, g_o = norms(
        x_other, hold(g_other, [state]), *gains, g_type=bf16, after=[state]
    )
    ffn = functools.partial(
        ffn_chunk,
        pos=pos,
        a2=(a2, a2_o),
        g=(g, g_o),
        w_up=w_up,
        w_down=w_down,
        b_up=row(b_up),
    )
    c0 = ffn(0, 1, after=[forward.near(a1_o)])
    g0 = Group(links, *c0[4:8])
    c1 = ffn(1, 2, earlier=c0[:4], more=1, after=[forward.far(c0[8])])
    first = list(c1[4:8])
    if tuned:
        g0.arrived(c1[8])
        first[0::2] = g0.second_in(*first[0::2], 4)
    g1 = Group(links, *first)
    state_in = forward.done(c1[8])
    mixed, dn, dd, grad_own, grad_sent, *mixed_send = mixing(
        pos, g, w_out, qf, kf, v, state_in, after=first[:1]
    )
    reverse = Carried(links, grad_own, grad_sent, True)
    mixed_other = [links.core(part) for part in mixed_send]
    back = head_blocks_after(directions, [mixed])
    held = [reverse.near(back)]
    out_pieces = out_grad(
        pos, mixed, [hold(part, [back]) for part in mixed_other], (g, g_o), after=held
    )
    c2 = ffn(3, 1, earlier=c1[:4], filled=out_pieces, after=[reverse.far(out_pieces[0])])
    held = [c2[8]]
    z0 = None
    if tuned:
        g1.arrived(c2[8])
        g0.second_with(g1)
        held = [g1.second()]
    state_later = reverse.done(held[0])
    g2 = Group(links, *c2[4:8])
    grad_proj, grad_send, bias_qkv, grad_feat = backward(
        pos,
        qf,
        kf,
        v,
        dn,
        dd,
        state_in,
        state_later,
        weights,
        back,
        turns,
        after=held,
    )
    grad_other = links.core(grad_send)
    held = [grad_proj]
    if tuned:
        z0, z0_sent = g0.done(pos, grad_proj)
        g2.arrived(z0)
        held = [z0, g2.second()]
    grad_other = hold(grad_other, held)
    if tuned:
        early = Halves(links, z0, hold(z0_sent, [grad_other]))
    last_parts = qkv_grad(pos, (a1, a1_o), grad_proj, grad_other, after=held)
    acts = c2[:4]
    held = [last_parts[0]]
    pieces = list(last_parts)
    if tuned:
        z1, z1_sent = g1.done(pos, last_parts[0])
        later = Halves(links, z1, z1_sent)
        pieces[0::2] = [hold(piece, [z1]) for piece in pieces[0::2]]
        early.arrived(last_parts[0])
        held = [z1, early.one]
    g3 = Group(links, *pieces)
    own_g = hidden_rows(pos, acts[2:], w_up, (x, x_other), after=held)
    held = [own_g[1]]
    if tuned:
        z2, z2_sent = g2.done(pos, own_g[1])
        middle = Halves(links, z2, z2_sent)
        held += [z2, early.stage_two()]
    own_r = hidden_rows(pos, acts[:2], w_down, sends=own_g[0], after=held)
    others = links.core(own_r[0])
    held = [own_r[1]]
    if tuned:
        early.landed(own_r[1])
        held = [later.stage_two(early.two), middle.stage_two(early.two)]
        g3.arrived(own_r[1])
        held.append(g3.second())
    partial, sums1 = first_norm(x, g, grad_proj, w_qkv, row(ln1_gain), after=held)
    half_up = jnp.concatenate([c[8].reshape(-1, 2, 2, 128) for c in (c0, c1, c2)], 0)
    half_up = half_up.transpose(1, 2, 0, 3).reshape(4, 1, 512)
    b_up_grad = jnp.where(core == np.arange(2)[None, :, None], half_up, 0.0).reshape(-1)
    vectors = [
        sums1[0],
        sums1[1],
        own_g[2][0],
        own_g[2][1],
        bias_qkv.reshape(-1),
        sums1[2],
        b_up_grad,
        grad_feat[0],
    ]
    lines = jnp.concatenate([v_.reshape(links.ns, -1) for v_ in vectors], 1)
    held = [partial]
    if tuned:
        lines = jnp.pad(lines.reshape(8, 13, 128), ((0, 0), (0, 3), (0, 0)))
        z3 = g3.done(pos, partial, more=(lines.reshape(4, 32, 128),), direct=True)
        later = later.done(z3[0])
        tail = Line(links, z3)
        held = [z3[0]]
    result, grad_input = ends(
        x,
        mixed,
        partial,
        own_r[1],
        own_g[1],
        hold(others, [partial]),
        w_out,
        row(b_out + b_down),
        row(ln2_gain),
        after=held,
    )

    if tuned:
        first_down, first_up = in_place(early.done(result), 1, [result])
        second_down, second_up = in_place(later, 2, [first_down])
        middle = middle.done(second_down)
        third_down, third_up = in_place(middle, 1, [second_down], start=3)
        tail = tail.done(third_down)
        lines = tail[768:].reshape(2, 16, 128)
        pick = lambda i: lax.dynamic_index_in_dim(lines, i, 0, keepdims=False)
        lines = pick(core) + links.core(pick(1 - core))
        corner = links.send(lines, lambda b, s: (b ^ 3, s))
        lines = lines + links.x(lines) + links.y(lines) + corner
        tail = tail[:768].reshape(6, 128, 128)
        shares, at = [], 0
        for v_ in vectors:
            n = v_.shape[0] // 1024
            shares.append(lines[at : at + n].reshape(-1))
            at += n
        halves = jnp.concatenate([first_up, second_up, third_up], 1)
        w_down_grad = jnp.concatenate([first_down, second_down, third_down], 0)
        w_out_grad = jnp.concatenate([middle[256:384], middle[640:768]], 1)
        blocks = [[tail[i] for i in (0, 3, 2)], [tail[i] for i in (1, 4, 5)]]
        blocks = jnp.stack([jnp.stack(b, 0) for b in blocks], 0)
        halves = jnp.concatenate([halves, blocks], 1)
        pick = lambda i: lax.dynamic_index_in_dim(halves, i, 0, keepdims=False)
        mine, other = pick(core), links.core(pick(1 - core))
        first, second = jnp.where(core == 0, mine, other), jnp.where(core == 0, other, mine)
        both = jnp.stack([first, second], 0)
        w_up_grad = both[:, :4].reshape(1024, 128).T
        w_qkv_grad = both[:, 4:].transpose(1, 0, 2, 3).reshape(768, 128).T
    else:
        total = lax.psum(jnp.concatenate(vectors), ("batch", "seq"))
        shares, at = [], 0
        for v_ in vectors:
            share = v_.shape[0] // links.ns
            shares.append(lax.dynamic_slice_in_dim(total, at + place * share, share, 0))
            at += v_.shape[0]

        def scatter(full):
            part = lax.psum_scatter(full, "batch", scatter_dimension=1, tiled=True)
            return lax.psum_scatter(part, "seq", scatter_dimension=0, tiled=True)

        def of_core(half, axis):
            zero = jnp.zeros_like(half)
            pair = jnp.where(core == 0, half, zero), jnp.where(core == 1, half, zero)
            return jnp.stack(pair, axis)

        both = lambda send, keep: jnp.stack([keep, send], 0)
        groups = (c0, c1, c2)
        slots = lambda pair, n, m, k: both(pair[0][:, :, m : m + n], pair[1][:, :, k : k + n])
        sizes = ((2, 0, 0), (4, 0, 0), (2, 0, 0))
        up = [slots(c[4:6], *size) for c, size in zip(groups, sizes)]
        up = jnp.concatenate(up, 3).reshape(2, 2, 4, 4, 2, 128, 128)
        up = of_core(up.transpose(2, 4, 6, 1, 0, 3, 5).reshape(1024, 4, 512), 2)
        down = [slots(c[6:8], *size) for c, size in zip(groups, sizes)]
        down = jnp.concatenate(down, 3).reshape(2, 2, 4, 4, 2, 128, 128)
        down = of_core(down.transpose(2, 3, 5, 0, 1, 4, 6).reshape(4, 512, 1024), 1)
        by_x = slots(out_pieces[:2], 1, 2, 2).swapaxes(0, 1)
        out = jnp.concatenate([by_x, slots(out_pieces[2:], 1, 2, 2)], 3)
        out = out.transpose(2, 4, 0, 1, 3, 5).reshape(4, 128, 1024)
        by_x = both(*last_parts[:2]).swapaxes(0, 1)
        by_y = both(*last_parts[2:])
        parts = [by_x[:, :, :, :2], by_y[:, :, :, :2]]
        parts.append(jnp.stack([by_x[:, :, :, 2], by_y[:, :, :, 2]], 3))
        qkv = [p.transpose(2, 3, 5, 0, 1, 4).reshape(1024, 4, 128) for p in parts]
        w_up_grad = scatter(up.reshape(1024, 4096))
        w_down_grad = scatter(down.reshape(4096, 1024))
        w_out_grad = scatter(of_core(out, 1).reshape(1024, 1024))
        w_qkv_grad = scatter(of_core(jnp.stack(qkv, 2), 3).reshape(1024, 3072))

    shape = hidden_in.shape
    return (
        result.reshape(shape),
        grad_input.reshape(shape),
        shares[0],
        shares[1],
        shares[2],
        shares[3],
        w_qkv_grad,
        shares[4],
        w_out_grad,
        shares[5],
        w_up_grad,
        shares[6],
        w_down_grad,
        shares[5],
        shares[7],
    )


def solution(mesh):
    links = Links(mesh)
    rows = P("batch", "seq", None)
    spread = P("seq", "batch")
    return jax.shard_map(
        functools.partial(per_device, links),
        mesh=mesh,
        in_specs=(rows, rows, P("batch"), P("batch", "seq")) + (P(),) * 14,
        out_specs=(rows, rows)
        + (P("seq"),) * 4
        + (spread, P("seq"), spread, P("seq"), spread, P("seq"), spread, P("seq"), P("seq")),
        check_vma=False,
    )
```

```python
import functools
import math

import jax
import jax.numpy as jnp
import numpy as np
from jax import lax
from jax.experimental import pallas as pl
from jax.experimental.pallas import tpu as pltpu
from jax.sharding import PartitionSpec as P

f32 = jnp.float32
bf16 = jnp.bfloat16
struct = jax.ShapeDtypeStruct
HEADS = 16
HEAD_DIM = 64
ROT = 16
LEN_BLK = 256
ROW_TILE = 256
HG = 256
ROOT_HALF = math.sqrt(0.5)
NORMAL_PEAK = 1.0 / math.sqrt(2.0 * math.pi)
norm_epsilon = 1e-05
rope_base = 10000.0
VMEM_BYTES = 60 * 1024 * 1024


def params():
    return pltpu.CompilerParams(vmem_limit_bytes=VMEM_BYTES)


def dot(a, b, ca, cb):
    return lax.dot_general(a, b, (((ca,), (cb,)), ((), ())), preferred_element_type=f32)


def iota(shape, dim):
    return lax.broadcasted_iota(jnp.int32, shape, dim)


def split(x):
    hi = x.astype(bf16)
    return hi, (x - hi.astype(f32)).astype(bf16)


def ordered_call(kernel, args, after, *, in_specs, grid, out_specs, out_shape, prefetch=0, **kw):
    after = [a for a in after if a is not None]
    n_in = len(args)

    def body(*refs):
        kernel(*refs[:n_in], *refs[n_in + len(after) :])

    in_specs = list(in_specs) + [pl.BlockSpec(memory_space=pl.ANY)] * len(after)
    return pl.pallas_call(
        body,
        grid_spec=pltpu.PrefetchScalarGridSpec(
            num_scalar_prefetch=prefetch, grid=grid, in_specs=in_specs, out_specs=out_specs
        ),
        out_shape=out_shape,
        compiler_params=params(),
        **kw,
    )(*args, *after)


def ffn_kernel(aliased, pos, a2_own, a2_other, g_own, g_other, *refs):
    w_ups, w_downs, biases = refs[:2], refs[2:4], refs[4:6]
    refs = refs[6 + aliased :]
    gelus, grads, (up_send, up_keep, down_send, down_keep, b_sum) = refs[:2], refs[2:4], refs[4:]
    me = pos[0]
    w_up = jnp.concatenate([w[...] for w in w_ups], axis=1)
    w_down = jnp.concatenate([w[...] for w in w_downs], axis=0)
    bias = jnp.concatenate([b[...] for b in biases], axis=1)
    d_up = d_down = total = None
    for half, (a2, g) in enumerate(((a2_own, g_own), (a2_other, g_other))):
        rows_in, grad_in = a2[...], g[...]
        pre = dot(rows_in, w_up, 1, 0) + bias
        grad_gelu = dot(grad_in, w_down, 1, 1)
        cdf = 0.5 + 0.5 * lax.erf(pre * ROOT_HALF)
        gelu = (pre * cdf).astype(bf16)
        slope = cdf + pre * (NORMAL_PEAK * jnp.exp(-0.5 * pre * pre))
        grad_pre = (grad_gelu * slope).astype(bf16)
        for j in range(2):
            gelus[j][half, 0] = gelu[:, 128 * j : 128 * j + 128]
            grads[j][half, 0] = grad_pre[:, 128 * j : 128 * j + 128]
        parts = (
            dot(grad_pre, rows_in, 0, 0),
            dot(gelu, grad_in, 0, 0),
            jnp.sum(grad_pre.astype(f32), axis=0, keepdims=True),
        )
        if half == 0:
            d_up, d_down, total = parts
        else:
            d_up, d_down, total = d_up + parts[0], d_down + parts[1], total + parts[2]
    b_sum[0] = total
    mx = lax.rem(me, 2)
    keep, send = swapped(mx, d_up[:128], d_up[128:])
    for n in range(8):
        up_send[0, n // 2, n % 2] = send[:, n * 128 : (n + 1) * 128]
        up_keep[0, n // 2, n % 2] = keep[:, n * 128 : (n + 1) * 128]
    for j in range(2):
        squares = relative(d_down[128 * j : 128 * j + 128], me)
        for rx in range(2):
            for half in range(2):
                part = slice(128 * half, 128 * half + 128)
                down_send[rx, j, half] = squares[rx][1][:, part]
                down_keep[rx, j, half] = squares[rx][0][:, part]


def swapped(bit, first, second):
    return jnp.where(bit == 0, first, second), jnp.where(bit == 0, second, first)


def relative(tile, me):
    by_y = swapped(lax.div(me, 2), tile[:, :512], tile[:, 512:])
    by_yx = [swapped(lax.rem(me, 2), part[:, :256], part[:, 256:]) for part in by_y]
    return [[by_yx[y][x] for y in range(2)] for x in range(2)]


def once(shape, where):
    return pl.BlockSpec(shape, where, pipeline_mode=pl.Buffered(1))


def ffn_chunk(first, count, pos, a2, g, w_up, w_down, b_up, earlier=(), filled=(), more=0, after=()):
    rows, width = a2[0].shape
    block = lambda j, k, i, p: (2 * (2 * i + j) + p[1]) * 4 + first + k
    cols = lambda j: (lambda k, i, p: (0, block(j, k, i, p)))
    lines = lambda j: (lambda k, i, p: (block(j, k, i, p), 0))
    whole = lambda k, i, p: (0, 0)
    place = lambda k, i, p: (0, i * 4 + first + k, 0, 0)
    in_specs = (
        [once((rows, width), whole)] * 4
        + [pl.BlockSpec((width, 128), cols(j)) for j in range(2)]
        + [pl.BlockSpec((128, width), lines(j)) for j in range(2)]
        + [pl.BlockSpec((1, 128), cols(j)) for j in range(2)]
    )
    args = [pos, *a2, *g, w_up, w_up, w_down, w_down, b_up, b_up]
    given = [*enumerate(earlier), *enumerate(filled, 4)]
    aliases = {len(args) + i: out for i, (out, _) in enumerate(given)}
    in_specs = in_specs + [pl.BlockSpec(memory_space=pl.ANY)] * len(given)
    args = args + [value for _, value in given]
    pieces = [struct((2, 4, 2 * count + extra, 128, 128), f32) for extra in (more, 0)] * 2
    pieces = [struct(v.shape, f32) for v in filled] or pieces
    return ordered_call(
        functools.partial(ffn_kernel, len(given)),
        args,
        after,
        prefetch=1,
        grid=(count, 2),
        in_specs=in_specs,
        out_specs=[pl.BlockSpec((2, 1, rows, 128), place)] * 4
        + [
            pl.BlockSpec(
                (1, 4, 2, 128, 128),
                lambda k, i, p: (lax.bitwise_xor(i, lax.div(p[0], 2)), 0, k, 0, 0),
            )
        ]
        * 2
        + [pl.BlockSpec((2, 2, 2, 128, 128), lambda k, i, p: (0, i, k, 0, 0))] * 2
        + [pl.BlockSpec((1, 1, 256), lambda k, i, p: (k * 2 + i, 0, 0))],
        out_shape=[struct((2, 8, rows, 128), bf16)] * 4
        + pieces
        + [struct((count * 2, 1, 256), f32)],
        input_output_aliases=aliases,
        cost_estimate=cost(f"ffn{first}"),
        name="ffn_chunk",
    )


def out_grad_kernel(pos, own, early, late, g_own, g_other, x_send, x_keep, y_send, y_keep):
    other = jnp.where(pl.program_id(0) < 2, early[...], late[...]).astype(bf16)
    tile = dot(own[...], g_own[...], 0, 0) + dot(other, g_other[...], 0, 0)
    squares = relative(tile, pos[0])
    for n in range(2):
        x_send[n, 0, 0] = squares[1][n][:, :128]
        x_keep[n, 0, 0] = squares[0][n][:, :128]
        y_send[n, 0, 0] = squares[n][1][:, 128:]
        y_keep[n, 0, 0] = squares[n][0][:, 128:]


def out_grad(pos, mixed, others, g, after=()):
    rows, width = g[0].shape
    whole = lambda z, p: (0, 0)
    return ordered_call(
        out_grad_kernel,
        [pos, mixed, *others, *g],
        after,
        prefetch=1,
        grid=(4,),
        in_specs=[
            pl.BlockSpec((rows, 128), lambda z, p: (0, 2 * z + p[1])),
            pl.BlockSpec((rows, 128), lambda z, p: (0, lax.min(z, 1))),
            pl.BlockSpec((rows, 128), lambda z, p: (0, lax.max(z - 2, 0))),
            once((rows, width), whole),
            once((rows, width), whole),
        ],
        out_specs=[pl.BlockSpec((2, 1, 1, 128, 128), lambda z, p: (0, z, 2, 0, 0))] * 4,
        out_shape=[struct((2, 4, 3, 128, 128), f32)] * 4,
        cost_estimate=cost("out_grad"),
        name="out_grad",
    )


def second_kernel(at, slots, u_keep, u_one, d_keep, d_one, *refs):
    x_o, y_o = refs[-2:]
    own = slice(at, at + slots)
    y_o[...] = (u_keep[...] + u_one[:, :, own]).reshape(y_o.shape)
    x_o[...] = (d_keep[...] + d_one[:, :, own]).reshape(x_o.shape)


def second_stage(keeps, ones, at, bundles=None, into=0):
    slots, total = keeps[0].shape[2], ones[0].shape[2]
    half = slots // 2
    keep = pl.BlockSpec((1, 2, slots, 128, 128), lambda i: (1, i, 0, 0, 0))
    one = pl.BlockSpec((1, 2, total, 128, 128), lambda i: (1, i, 0, 0, 0))
    if bundles:
        out = pl.BlockSpec((1, 4, half, 128, 128), lambda i: (i, 0, into // half, 0, 0))
        shapes = [struct(v.shape, f32) for v in bundles]
    else:
        out = pl.BlockSpec((2, slots, 128, 128), lambda i: (i, 0, 0, 0))
        shapes = [struct((4, slots, 128, 128), f32)] * 2
    return ordered_call(
        functools.partial(second_kernel, at, slots),
        [keeps[0], ones[0], keeps[1], ones[1], *(bundles or [])],
        [],
        grid=(2,),
        in_specs=[keep, one] * 2 + [pl.BlockSpec(memory_space=pl.ANY)] * len(bundles or []),
        out_specs=[out] * 2,
        out_shape=shapes,
        input_output_aliases={4: 0, 5: 1} if bundles else {},
        cost_estimate=cost("second_stage"),
        name="second_stage",
    )


def finish_kernel(at, slots, cut, direct, pos, u_keep, u_one, u_two, d_keep, d_one, d_two, *refs):
    outs = refs[-4:] if direct else refs[-2:]
    more = refs[: -len(outs)]
    own = slice(at, at + slots)
    step = pl.program_id(0)
    parts = []
    for keep, one, two in ((u_keep, u_one, u_two), (d_keep, d_one, d_two)):
        if cut is None:
            second = two[...]
        else:
            second = two[0, :, cut[0] : cut[1]].reshape(2, slots, 128, 128)
        parts.append((keep[0] + one[0, :, own] + second).reshape(2, slots * 128, 128))
    both = jnp.concatenate(parts + [rows[...] for rows in more], 1)
    if not direct:
        kept, sent = swapped(lax.rem(pos[2], 2), both[0], both[1])
        outs[0][0], outs[1][0] = kept, sent
        return

    def put(out, value):
        out[...] = value

    for low in range(2):
        ahead = lax.rem(2 * step + low - pos[2] + 4, 4)
        for n, out in enumerate(outs):
            pl.when(ahead == n)(functools.partial(put, out, both[low]))


def finish(pos, keeps, ones, at, twos, cut, more=(), direct=False):
    slots, total = keeps[0].shape[2], ones[0].shape[2]
    keep = pl.BlockSpec((1, 2, slots, 128, 128), lambda i, p: (0, i, 0, 0, 0))
    one = pl.BlockSpec((1, 2, total, 128, 128), lambda i, p: (0, i, 0, 0, 0))
    if cut is None:
        two = pl.BlockSpec((2, slots, 128, 128), lambda i, p: (i, 0, 0, 0))
    else:
        two = pl.BlockSpec((1, 4, twos[0].shape[2], 128, 128), lambda i, p: (i, 0, 0, 0, 0))
    lines = 256 * slots + sum(m.shape[1] for m in more)
    if direct:
        out = [pl.BlockSpec((lines, 128), lambda i, p: (0, 0))] * 4
        shapes = [struct((lines, 128), f32)] * 4
    else:
        out = [pl.BlockSpec((1, lines, 128), lambda i, p: (i, 0, 0))] * 2
        shapes = [struct((2, lines, 128), f32)] * 2
    return ordered_call(
        functools.partial(finish_kernel, at, slots, cut, direct),
        [pos, keeps[0], ones[0], twos[0], keeps[1], ones[1], twos[1], *more],
        [],
        prefetch=1,
        grid=(2,),
        in_specs=[keep, one, two] * 2
        + [pl.BlockSpec((2, m.shape[1], 128), lambda i, p: (i, 0, 0)) for m in more],
        out_specs=out,
        out_shape=shapes,
        cost_estimate=cost(f"finish{slots}"),
        name="finish",
    )


def qkv_grad_kernel(pos, a1_own, a1_other, *refs):
    own, other, (x_send, x_keep, y_send, y_keep) = refs[:3], refs[3:6], refs[6:]
    left = jnp.concatenate([r[0] for r in own], 1)
    left_other = jnp.concatenate([r[0].astype(bf16) for r in other], 1)
    tile = dot(left, a1_own[...], 0, 0) + dot(left_other, a1_other[...], 0, 0)
    step = pl.program_id(0)
    block = lambda j, n: tile[128 * j : 128 * j + 128, n * 128 : (n + 1) * 128]

    def put(out, whole, half):
        for z in range(4):
            out[0, z, 0] = block(whole, 2 * z)
            out[0, z, 1] = block(whole, 2 * z + 1)
            out[0, z, 2] = block(2, 2 * z + half)

    pl.when(lax.rem(step, 2) == 1)(lambda: put(x_send, 0, 0))
    pl.when(lax.rem(step, 2) == 0)(lambda: put(x_keep, 0, 0))
    pl.when(step >= 2)(lambda: put(y_send, 1, 1))
    pl.when(step < 2)(lambda: put(y_keep, 1, 1))


def qkv_grad(pos, a1, grad_proj, other, after=()):
    rows, width = a1[0].shape
    whole = lambda n, p: (0, 0)

    def source(j, halves):
        def where(n, p):
            unit = lax.bitwise_xor(n, p[0]) * 3 + j
            at = lax.rem(unit, 4)
            return (lax.div(unit, 4), 0, at * 2 + p[1] if halves else at)

        return where

    out = lambda at: pl.BlockSpec((1, 4, 3, 128, 128), lambda n, p: (at(n), 0, 0, 0, 0))
    return ordered_call(
        qkv_grad_kernel,
        [pos, *a1] + [grad_proj] * 3 + [other] * 3,
        after,
        prefetch=1,
        grid=(4,),
        in_specs=[once((rows, width), whole)] * 2
        + [pl.BlockSpec((1, rows, 128), source(j, True)) for j in range(3)]
        + [pl.BlockSpec((1, rows, 128), source(j, False)) for j in range(3)],
        out_specs=[
            out(lambda n: lax.div(n, 2)),
            out(lambda n: lax.div(n, 2)),
            out(lambda n: lax.max(n - 2, 0)),
            out(lambda n: lax.min(n, 1)),
        ],
        out_shape=[struct((2, 4, 3, 128, 128), f32)] * 4,
        cost_estimate=cost("qkv_grad"),
        name="qkv_grad",
    )


LONG, SHORT = 10**11, 1
WEIGHTS = {"first_norm": LONG, "hidden0": LONG, "blocks": LONG, "in_place": LONG, "ends": LONG, "finish2": LONG}


def cost(name):
    flops = WEIGHTS.get(name, SHORT)
    return pl.CostEstimate(flops=flops, bytes_accessed=1, transcendentals=0)


def rotate(x, cos, sin_first, sin_second):
    n = x.shape[1]
    half = ROT // 2
    return x * cos + pltpu.roll(x, n - half, 1) * sin_first + pltpu.roll(x, half, 1) * sin_second


def three(x, w_hi, w_lo):
    hi, lo = split(x)
    return dot(hi, w_hi, 1, 0) + dot(lo, w_hi, 1, 0) + dot(hi, w_lo, 1, 0)


def pair_mask():
    return (iota((128, 128), 0) // 64) == (iota((128, 128), 1) // 64)


def pack(first, second):
    mask = pair_mask()
    first = jnp.where(mask, first, 0.0)
    second = jnp.where(mask, second, 0.0)
    first = first + pltpu.roll(first, 64, 1)
    second = second + pltpu.roll(second, 64, 1)
    return jnp.where(iota((128, 128), 1) < 64, first, second)


def unpack(packed):
    mask = pair_mask()
    low = iota((128, 128), 1) < 64
    turned = pltpu.roll(packed, 64, 1)
    return (
        jnp.where(mask, jnp.where(low, packed, turned), 0.0),
        jnp.where(mask, jnp.where(low, turned, packed), 0.0),
    )


def to_column(row):
    eye = iota((128, 128), 0) == iota((128, 128), 1)
    return jnp.sum(jnp.where(eye, jnp.broadcast_to(row, (128, 128)), 0.0), axis=1, keepdims=True)


def column_of(row):
    n = row.shape[1]
    eye = iota((n, n), 0) == iota((n, n), 1)
    return jnp.sum(jnp.where(eye, jnp.broadcast_to(row, (n, n)), 0.0), axis=1, keepdims=True)


def each_head(x):
    mask = iota((1, 128), 1) < 64
    zero = jnp.zeros_like(x)
    return jnp.where(mask, x, zero), jnp.where(mask, zero, x)


def feature_kernel(
    pos, a1, wq, wk, wv, bq, bk, bv, fw, matrix, cos, sin1, sin2, valid, qf_o, kf_o, v_o, own, send
):
    x = a1[...]
    count = x.shape[0] // LEN_BLK
    rows = lambda i: slice(LEN_BLK * i, LEN_BLK * (i + 1))
    turns = cos[...], sin1[...], sin2[...]
    weight = fw[...]
    halves = split(matrix[...])
    q = [dot(x[rows(i)], wq[...], 1, 0) for i in range(count)]
    k = [dot(x[rows(i)], wk[...], 1, 0) for i in range(count)]
    q = [rotate(part + bq[...], *turns) for part in q]
    v = [(dot(x[rows(i)], wv[...], 1, 0) + bv[...]).astype(bf16) for i in range(count)]
    k = [rotate(part + bk[...], *turns) for part in k]
    q = [three(part, *halves) for part in q]
    k = [three(part, *halves) for part in k]
    for i in range(count):
        qf_o[rows(i)] = (weight * jnp.exp(q[i])).astype(bf16)
        kf = (weight * jnp.exp(k[i])).astype(bf16) * column_of(valid[i : i + 1]).astype(bf16)
        kf_o[rows(i)] = kf
        k[i] = kf
        v_o[rows(i)] = v[i]
    states = []
    for i in range(count):
        state = [
            dot(k[i][:, 128 * p : 128 * p + 128], v[i][:, 128 * p : 128 * p + 128], 0, 0)
            for p in range(2)
        ]
        norm = jnp.sum(k[i].astype(f32), axis=0, keepdims=True)
        lines = norm_rows(norm[:, :128], norm[:, 128:])
        states.append(jnp.concatenate([pack(state[0], state[1]), lines], 0))
    put_states(pos[1], states, own, send)


def norm_rows(first, second):
    line = iota((8, 128), 0)
    return jnp.where(line == 0, first, jnp.where(line == 1, second, 0.0))


def put_states(core, states, own, send):
    half = len(states) // 2
    for j in range(half):
        first, second = states[j], states[half + j]
        own[j, 0] = jnp.where(core == 0, first, second)
        send[j, 0] = jnp.where(core == 0, second, first)


def state_of(core, pair, i):
    here, there = pair
    half = here.shape[0]
    j = i % half
    return jnp.where(core == i // half, here[j, 0], there[j, 0])


def scores(qp, kp, causal):
    raw = dot(jnp.concatenate(each_head(qp), 0), kp, 1, 1)
    return [
        jnp.where(causal, raw[LEN_BLK * h : LEN_BLK * (h + 1)], 0.0).astype(bf16)
        for h in range(2)
    ]


def lower(n):
    return iota((n, n), 0) >= iota((n, n), 1)


def mix_kernel(pos, g, wo, qf, kf, v, here, there, mix_o, dn_o, dd_o, own, send, *sends):
    count = qf.shape[0] // LEN_BLK
    mask = pair_mask()
    lane = iota((1, 128), 1)
    first = lane < 64
    causal = lower(LEN_BLK)
    one0, one1 = each_head(jnp.ones((LEN_BLK, 128), bf16))
    cells = [(i, p) for i in range(count) for p in range(2)]
    rows = lambda i: slice(LEN_BLK * i, LEN_BLK * (i + 1))
    cols = lambda p: slice(128 * p, 128 * p + 128)
    q = {(i, p): qf[rows(i), cols(p)] for i, p in cells}
    s = {(i, p): scores(q[i, p], kf[rows(i), cols(p)], causal) for i, p in cells}
    grad_mixed = dot(g[...], wo[...], 1, 1)
    both = {}
    for i in range(count):
        carried = state_of(pos[1], (here, there), i)
        state = unpack(carried[:128])
        for p in range(2):
            column = to_column(carried[128 + p : 129 + p])
            norm = jnp.where(mask, jnp.broadcast_to(column, (128, 128)), 0.0)
            hi, lo = split(jnp.concatenate([state[p], norm], 1))
            qp = q[i, p]
            both[i, p] = dot(jnp.concatenate([qp, qp], 1), jnp.concatenate([hi, lo], 0), 1, 0)
    for i, p in cells:
        v0, v1 = each_head(v[rows(i), cols(p)])
        right = jnp.concatenate(
            [jnp.concatenate([v0, one0], 1), jnp.concatenate([v1, one1], 1)], 0
        )
        both[i, p] = both[i, p] + dot(jnp.concatenate(s[i, p], 1), right, 1, 0)
    mixes, dns, norms, grads, sums = {}, {}, {}, {}, {}
    for i, p in cells:
        inverse = 1.0 / both[i, p][:, 128:]
        mixed = both[i, p][:, :128] * inverse
        low = mixed.astype(bf16)
        mix_o[rows(i), cols(p)] = low
        mixes[i, p] = low
        dn = (grad_mixed[rows(i), cols(p)] * inverse).astype(bf16)
        dn_o[rows(i), cols(p)] = dn
        dns[i, p] = dn
        product = -(dn.astype(f32) * mixed)
        d0 = jnp.sum(jnp.where(first, product, 0.0), axis=1, keepdims=True)
        d1 = jnp.sum(jnp.where(first, 0.0, product), axis=1, keepdims=True)
        sums[i, p] = d0, d1
    for i, p in cells:
        grads[i, p] = dot(q[i, p], dns[i, p], 0, 0)
    for i, p in cells:
        d0, d1 = sums[i, p]
        norms[i, p] = column_sum(q[i, p].astype(f32) * jnp.where(first, d0, d1))
    states = []
    for i in range(count):
        lines = jnp.zeros((LEN_BLK, 128), f32)
        for p in range(2):
            d0, d1 = sums[i, p]
            lines = jnp.where(lane == 2 * p, d0, jnp.where(lane == 2 * p + 1, d1, lines))
        dd_o[0, rows(i)] = lines
        lines = norm_rows(norms[i, 0], norms[i, 1])
        states.append(jnp.concatenate([pack(grads[i, 0], grads[i, 1]), lines], 0))
        other_half = jnp.where(pos[1] == 0, mixes[i, 1].astype(f32), mixes[i, 0].astype(f32))

        def put(out, lines=rows(i), other_half=other_half):
            out[lines] = other_half

        for n, out in enumerate(sends):
            pl.when(lax.div(pl.program_id(0), 2) == n)(functools.partial(put, out))
    put_states(pos[1], states, own, send)


def back_kernel(
    pos, qf, kf, v, dn, dd, here, there, l_here, l_there, fw, matrix, cos, sin1, sin2, *outs
):
    gp_o, send_o, bias_o, fw_o = outs
    count = qf.shape[0] // LEN_BLK
    step = pl.program_id(1)
    before = [state_of(pos[1], (here, there), i) for i in range(count)]
    after = [state_of(pos[1], (l_here, l_there), i) for i in range(count)]
    causal = lower(LEN_BLK)
    lane = iota((1, 128), 1)
    first = lane < 64
    turns = cos[...], -sin1[...], -sin2[...]
    halves = split(matrix[...])
    cells = [(i, p) for i in range(count) for p in range(2)]
    rows = lambda i: slice(LEN_BLK * i, LEN_BLK * (i + 1))
    cols = lambda p: slice(128 * p, 128 * p + 128)
    q, k, vv, d, s, t, col = {}, {}, {}, {}, {}, {}, {}
    for i, p in cells:
        q[i, p], k[i, p] = qf[rows(i), cols(p)], kf[rows(i), cols(p)]
        vv[i, p], d[i, p] = v[rows(i), cols(p)], dn[rows(i), cols(p)]
        col[i, p] = [
            jnp.sum(jnp.where(lane == 2 * p + h, dd[0, rows(i)], 0.0), axis=1, keepdims=True)
            for h in range(2)
        ]
    for c in cells:
        s[c] = scores(q[c], k[c], causal)
        raw = dot(jnp.concatenate(each_head(d[c]), 0), vv[c], 1, 1)
        t[c] = [
            jnp.where(causal, raw[LEN_BLK * h : LEN_BLK * (h + 1)] + col[c][h], 0.0).astype(bf16)
            for h in range(2)
        ]
    dq, dk, dv = {}, {}, {}
    for i in range(count):
        state, later = unpack(before[i][:128]), unpack(after[i][:128])
        for p in range(2):
            c = i, p
            s_hi, s_lo = split(state[p])
            d_hi, d_lo = split(later[p])
            twice = lambda x: jnp.concatenate([x, x], 1)
            dq[c] = dot(twice(d[c]), jnp.concatenate([s_hi, s_lo], 1), 1, 1)
            dk[c] = dot(twice(vv[c]), jnp.concatenate([d_hi, d_lo], 1), 1, 1)
            dv[c] = dot(twice(k[c]), jnp.concatenate([d_hi, d_lo], 0), 1, 0)
    for c in cells:
        dq[c] = dq[c] + dot(jnp.concatenate(t[c], 1), jnp.concatenate(each_head(k[c]), 0), 1, 0)
        dk[c] = dk[c] + dot(jnp.concatenate(t[c], 0), jnp.concatenate(each_head(q[c]), 0), 0, 0)
        dv[c] = dv[c] + dot(jnp.concatenate(s[c], 0), jnp.concatenate(each_head(d[c]), 0), 0, 0)
    for i, p in cells:
        c = i, p
        norm = jnp.where(first, *col[c]) * before[i][128 + p : 129 + p]
        dq[c] = (dq[c] + norm) * q[c].astype(f32)
        dk[c] = (dk[c] + after[i][128 + p : 129 + p]) * k[c].astype(f32)
    whole = lambda parts: jnp.concatenate(
        [jnp.concatenate([parts[i, 0], parts[i, 1]], 1) for i in range(count)], 0
    )
    dq, dk, dv = whole(dq), whole(dk), whole(dv)
    tall = [jnp.concatenate([turn] * count, 0) for turn in turns]
    grads = (
        rotate(three(dq, *halves), *tall).astype(bf16),
        rotate(three(dk, *halves), *tall).astype(bf16),
        dv.astype(bf16),
    )
    for n in range(3):
        gp_o[n] = grads[n]
        wide = grads[n].astype(f32)
        other_half = jnp.where(pos[1] == 0, wide[:, 128:], wide[:, :128])
        send_o[n] = other_half
    totals = [column_sum(part.astype(f32)) for part in grads]
    totals.append(column_sum(dq + dk) / fw[...])

    @pl.when(step == 0)
    def _():
        for n in range(3):
            bias_o[n] = totals[n]
        fw_o[...] = totals[3]

    @pl.when(step > 0)
    def _():
        for n in range(3):
            bias_o[n] = bias_o[n] + totals[n]
        fw_o[...] = fw_o[...] + totals[3]


def attention_specs(seqs, per, more=0):
    rows = LEN_BLK * per
    return dict(
        grid=(4, seqs // per),
        wide=pl.BlockSpec((rows, 1024), lambda h, g, *_: (g, 0)),
        head=pl.BlockSpec((rows, HG), lambda h, g, *_: (g, h)),
        state=pl.BlockSpec((seqs // 2, 1, 136, 128), lambda h, g, *_: (0, h, 0, 0)),
        row=pl.BlockSpec((1, HG), lambda h, g, *_: (0, h)),
        table=pl.BlockSpec((256, 256), lambda h, g, *_: (0, 0)),
        dden=pl.BlockSpec((1, rows, 128), lambda h, g, *_: (h, g, 0)),
    )


def features(pos, a1, w_qkv, b_qkv, feat_weight, matrix, turns, valid, after=()):
    rows = a1.shape[0]
    seqs = per = rows // LEN_BLK
    s = attention_specs(seqs, per)
    weights = [pl.BlockSpec((1024, HG), lambda h, g, *_, o=o: (0, 4 * o + h)) for o in range(3)]
    biases = [pl.BlockSpec((1, HG), lambda h, g, *_, o=o: (0, 4 * o + h)) for o in range(3)]
    return ordered_call(
        feature_kernel,
        [pos, a1, w_qkv, w_qkv, w_qkv, b_qkv, b_qkv, b_qkv, feat_weight, matrix, *turns, valid],
        after,
        prefetch=1,
        grid=s["grid"],
        in_specs=[s["wide"], *weights, *biases, s["row"]]
        + [s["table"]] * 4
        + [pl.BlockSpec((per, LEN_BLK), lambda h, g, *_: (g, 0))],
        out_specs=[s["head"]] * 3 + [s["state"]] * 2,
        out_shape=[struct((rows, 1024), bf16)] * 3
        + [struct((seqs // 2, 4, 136, 128), f32)] * 2,
        cost_estimate=cost("features"),
        name="features",
    )


def mixing(pos, g, w_out, qf, kf, v, state, after=()):
    rows = g.shape[0]
    seqs = per = rows // LEN_BLK
    steps = seqs // per
    s = attention_specs(seqs, per)
    return ordered_call(
        mix_kernel,
        [pos, g, w_out, qf, kf, v, *state],
        after,
        prefetch=1,
        grid=s["grid"],
        in_specs=[s["wide"], pl.BlockSpec((HG, 1024), lambda h, g, *_: (h, 0))]
        + [s["head"]] * 3
        + [s["state"]] * 2,
        out_specs=[
            s["head"],
            s["head"],
            s["dden"],
            s["state"],
            s["state"],
            pl.BlockSpec(
                (LEN_BLK * per, 128),
                lambda h, g, *_: (lax.select(h < 2, g, 0 * g + steps - 1), lax.min(h, 1)),
            ),
            pl.BlockSpec(
                (LEN_BLK * per, 128),
                lambda h, g, *_: (lax.select(h < 2, 0 * g, g), lax.max(h - 2, 0)),
            ),
        ],
        out_shape=[
            struct((rows, 1024), bf16),
            struct((rows, 1024), bf16),
            struct((4, rows, 128), f32),
            struct((seqs // 2, 4, 136, 128), f32),
            struct((seqs // 2, 4, 136, 128), f32),
            struct((rows, 256), f32),
            struct((rows, 256), f32),
        ],
        cost_estimate=cost("mixing"),
        name="mixing",
    )

def backward(pos, qf, kf, v, dn, dd, state, later, feat_weight, matrix, turns, after=(), per=4):
    rows = qf.shape[0]
    seqs = rows // LEN_BLK
    s = attention_specs(seqs, per)
    return ordered_call(
        back_kernel,
        [pos, qf, kf, v, dn, dd, *state, *later, feat_weight, matrix, *turns],
        after,
        prefetch=1,
        grid=s["grid"],
        in_specs=[s["head"]] * 4
        + [s["dden"]]
        + [s["state"]] * 4
        + [s["row"]]
        + [s["table"]] * 4,
        out_specs=[
            pl.BlockSpec((3, LEN_BLK * per, HG), lambda h, g, *_: (0, g, h)),
            pl.BlockSpec((3, LEN_BLK * per, 128), lambda h, g, *_: (0, g, h)),
            pl.BlockSpec((3, 1, HG), lambda h, g, *_: (0, 0, h)),
            s["row"],
        ],
        out_shape=[
            struct((3, rows, 1024), bf16),
            struct((3, rows, 512), f32),
            struct((3, 1, 1024), f32),
            struct((1, 1024), f32),
        ],
        cost_estimate=cost("backward"),
        name="backward",
    )


def norm_parts(x):
    centre = x - jnp.mean(x, axis=-1, keepdims=True)
    r = lax.rsqrt(jnp.mean(centre * centre, axis=-1, keepdims=True) + norm_epsilon)
    return centre * r, r


def norm_back(grad, xhat, r, gain):
    e = grad * gain
    return r * (
        e
        - jnp.mean(e, axis=-1, keepdims=True)
        - xhat * jnp.mean(e * xhat, axis=-1, keepdims=True)
    )


def add_sums(out, sums):
    step = pl.program_id(0)
    new = jnp.concatenate(sums, 0)

    @pl.when(step == 0)
    def _():
        out[...] = new

    @pl.when(step > 0)
    def _():
        out[...] = out[...] + new


def column_sum(x):
    return jnp.sum(x, axis=0, keepdims=True)


def tiles(tile, fixed):
    wide = lambda n: pl.BlockSpec((tile, n), lambda i, *_: (i, 0))
    keep = [once(a.shape, lambda i, *_: (0, 0)) for a in fixed]
    return wide, keep


def norms_kernel(x, g, gain1, bias1, gain2, bias2, a1_o, a2_o, g_o, *x_o):
    xhat, _ = norm_parts(x[...].astype(f32))
    a1_o[...] = (xhat * gain1[...] + bias1[...]).astype(bf16)
    a2_o[...] = (xhat * gain2[...] + bias2[...]).astype(bf16)
    g_o[...] = g[...].astype(g_o.dtype)
    for out in x_o:
        out[...] = x[...].astype(f32)


def norms(x, g, *vectors, after=(), g_type=f32):
    rows, tile = x.shape[0], 256
    wide, keep = tiles(tile, vectors)
    return ordered_call(
        norms_kernel,
        [x, g, *vectors],
        after,
        grid=(rows // tile,),
        in_specs=[wide(1024)] * 2 + keep,
        out_specs=[wide(1024)] * (4 if g_type == f32 else 3),
        out_shape=[struct((rows, 1024), bf16)] * 2
        + [struct((rows, 1024), g_type)] * (2 if g_type == f32 else 1),
        cost_estimate=cost("norms"),
        name="norms",
    )


def hidden_rows_kernel(grad, filled, pos, *refs):
    acts, weights, outs = refs[:2], refs[2:6], refs[6 + filled :]
    send, keep = outs[-2:] if not grad else outs[2:4]
    total = None
    for b in range(4):
        act = acts[b % 2]
        act = jnp.concatenate([act[0, 4 * (b // 2) + n] for n in range(4)], 1)
        part = dot(act, weights[b][...], 1, 1 if grad else 0)
        total = part if total is None else total + part
    step = pl.program_id(0)
    steps = pl.num_programs(0) // 2

    @pl.when(step < steps)
    def _():
        send[0] = total

    @pl.when(step >= steps)
    def _():
        keep[...] = total

    if grad:
        x_own, x_other, sum_o = outs[0], outs[1], outs[4]
        xhat, _ = norm_parts(jnp.where(step < steps, x_other[...], x_own[...].astype(f32)))
        sums = [column_sum(total * xhat), column_sum(total)]
        add_sums(sum_o, sums + [jnp.zeros((6, 1024), f32)])


def hidden_rows(pos, acts, weight, rows_in=None, sends=None, after=()):
    grad = rows_in is not None
    rows, tile = acts[0].shape[2], ROW_TILE
    steps = rows // tile
    act = pl.BlockSpec(
        (1, 8, tile, 128), lambda i, p: (1 - lax.div(i, steps), 0, lax.rem(i, steps), 0)
    )
    if grad:
        part = lambda b: once((1024, 512), lambda i, p: (0, 2 * b + p[1]))
    else:
        part = lambda b: once((512, 1024), lambda i, p: (2 * b + p[1], 0))
    filled = [] if sends is None else [sends]
    ours = pl.BlockSpec((tile, 1024), lambda i, p: (lax.max(i - steps, 0), 0))
    theirs = pl.BlockSpec((tile, 1024), lambda i, p: (lax.min(i, steps - 1), 0))
    return ordered_call(
        functools.partial(hidden_rows_kernel, grad, len(filled)),
        [pos, *acts] + [weight] * 4 + filled + list(rows_in or ()),
        after,
        prefetch=1,
        grid=(2 * steps,),
        in_specs=[act] * 2
        + [part(b) for b in range(4)]
        + [pl.BlockSpec(memory_space=pl.ANY)] * len(filled)
        + [ours, theirs][: 2 * grad],
        out_specs=[
            pl.BlockSpec((1, tile, 1024), lambda i, p: (int(grad), lax.min(i, steps - 1), 0)),
            ours,
        ]
        + [pl.BlockSpec((8, 1024), lambda i, p: (0, 0))] * grad,
        out_shape=[struct((2, rows, 1024), f32), struct((rows, 1024), f32)]
        + [struct((8, 1024), f32)] * grad,
        input_output_aliases={7: 0} if filled else {},
        cost_estimate=cost(f"hidden{grad:d}"),
        name="hidden_rows",
    )


def first_norm_kernel(x, g, gp, w_qkv, gain, part_o, sum_o):
    xhat, r = norm_parts(x[...].astype(f32))
    grad_res = g[...].astype(f32)
    grad = dot(jnp.concatenate([gp[0], gp[1], gp[2]], 1), w_qkv[...], 1, 1)
    part_o[...] = grad_res + norm_back(grad, xhat, r, gain[...])
    sums = [column_sum(v) for v in (grad * xhat, grad, grad_res)]
    add_sums(sum_o, sums + [jnp.zeros((5, 1024), f32)])


def first_norm(x, g, gp, w_qkv, gain, after=()):
    rows, tile = x.shape[0], ROW_TILE
    fixed = (w_qkv, gain)
    wide, keep = tiles(tile, fixed)
    return ordered_call(
        first_norm_kernel,
        [x, g, gp, *fixed],
        after,
        grid=(rows // tile,),
        in_specs=[wide(1024)] * 2 + [pl.BlockSpec((3, tile, 1024), lambda i: (0, i, 0))] + keep,
        out_specs=[wide(1024), pl.BlockSpec((8, 1024), lambda i: (0, 0))],
        out_shape=[struct((rows, 1024), f32), struct((8, 1024), f32)],
        cost_estimate=cost("first_norm"),
        name="first_norm",
    )


def ends_kernel(x, mixed, part, own_r, other_r, own_g, other_g, w_out, bias, gain, res_o, out_o):
    value = x[...].astype(f32)
    out = dot(mixed[...], w_out[...], 1, 0) + (own_r[...] + other_r[0])
    res_o[...] = (value + out + bias[...]).astype(bf16)
    xhat, r = norm_parts(value)
    out_o[...] = part[...] + norm_back(own_g[...] + other_g[0], xhat, r, gain[...])


def ends(x, mixed, part, own_r, own_g, others, w_out, bias, gain, after=()):
    rows, tile = x.shape[0], ROW_TILE
    fixed = (w_out, bias, gain)
    wide, keep = tiles(tile, fixed)
    half = lambda n: pl.BlockSpec((1, tile, 1024), lambda i: (n, i, 0))
    return ordered_call(
        ends_kernel,
        [x, mixed, part, own_r, others, own_g, others, *fixed],
        after,
        grid=(rows // tile,),
        in_specs=[wide(1024)] * 4 + [half(0), wide(1024), half(1)] + keep,
        out_specs=[wide(1024)] * 2,
        out_shape=[struct((rows, 1024), bf16), struct((rows, 1024), f32)],
        cost_estimate=cost("ends"),
        name="ends",
    )


class Links:
    def __init__(self, mesh):
        self.nb, self.ns = mesh.shape["batch"], mesh.shape["seq"]
        self.tuned = (self.nb, self.ns) == (4, 8)

    def send(self, value, move):
        pairs = []
        for b in range(self.nb):
            for s in range(self.ns):
                to = move(b, s)
                if to is not None:
                    pairs.append((b * self.ns + s, to[0] * self.ns + to[1]))
        return lax.ppermute(value, ("batch", "seq"), pairs)

    def core(self, value):
        return self.send(value, lambda b, s: (b, s ^ 1))

    def x(self, value):
        return self.send(value, lambda b, s: (b ^ 1, s))

    def y(self, value):
        return self.send(value, lambda b, s: (b ^ 2, s))

    def ring(self, value, by):
        s = lax.axis_index("seq")
        got = self.send(value, lambda b, s: (b, (s + by) % self.ns))
        kept = s >= by if by > 0 else s < self.ns + by
        return got, kept

    def shift(self, value, by):
        inside = lambda s: 0 <= s < self.ns
        return self.send(value, lambda b, s: (b, s + by) if inside(s + by) else None)


def hold(value, behind):
    behind = [b for b in behind if b is not None]
    return lax.optimization_barrier((value, *behind))[0] if behind else value


class Group:
    def __init__(self, links, x_send, x_keep, y_send, y_keep, at=0):
        self.links, self.at = links, at
        self.keeps = x_keep, y_keep
        self.slots = x_keep.shape[2]
        if links.tuned:
            self.ones = [links.x(x_send), links.y(y_send)]
            self.twos = None

    def arrived(self, *behind):
        self.ones = [hold(one, behind) for one in self.ones]

    def second(self):
        x_out, y_out = second_stage(self.keeps, self.ones, self.at)
        self.twos, self.cut = [self.links.y(y_out), self.links.x(x_out)], None
        return x_out

    def second_in(self, x_send, y_send, into):
        return second_stage(self.keeps, self.ones, self.at, (x_send, y_send), into)

    def second_with(self, group):
        total = group.ones[0].shape[2]
        self.twos = group.ones[::-1]
        self.cut = (0, group.at) if group.at else (group.slots, total)

    def done(self, pos, *behind, more=(), direct=False):
        twos = [hold(two, behind) for two in self.twos]
        return finish(pos, self.keeps, self.ones, self.at, twos, self.cut, more, direct)


class Carried:
    def __init__(self, links, own, sent, reverse):
        self.links, self.own, self.sent, self.reverse = links, own, sent, reverse
        self.sign = -1 if reverse else 1
        self.core = lax.rem(lax.axis_index("seq"), 2)
        if links.tuned:
            self.other = links.core(sent)

    def near(self, *behind):
        if not self.links.tuned:
            return None
        self.other = hold(self.other, behind)
        self.mine = self.own + self.other
        self.one, self.one_kept = self.links.ring(self.mine, self.sign * 2)
        return self.mine

    def far(self, *behind):
        if not self.links.tuned:
            return None
        self.one = jnp.where(self.one_kept, hold(self.one, behind), 0.0)
        self.sum = self.mine + self.one
        self.two, self.two_kept = self.links.ring(self.sum, self.sign * 4)
        return self.sum

    def done(self, *behind):
        links = self.links
        if not links.tuned:
            halves = jnp.stack([self.own, self.sent], 0)
            total, step = jnp.where(self.core == 0, halves, halves[::-1]), 1
            while step < links.ns:
                total = total + links.shift(total, self.sign * step)
                step *= 2
            total = links.shift(total, self.sign)
            return tuple(jnp.where(self.core == 0, total, total[::-1]))
        self.two = hold(self.two, behind)
        before = self.one + jnp.where(self.two_kept, self.two, 0.0)
        second = self.core == (0 if self.reverse else 1)
        here = before + jnp.where(second, self.other, 0.0)
        there = before + jnp.where(second, 0.0, self.own)
        return here, links.core(there)


class Line:
    def __init__(self, links, parts):
        self.mine = parts[0]
        self.parts = [
            links.send(parts[by], lambda b, s, by=by: (b, (s + 2 * by) % 8)) for by in (2, 1, 3)
        ]

    def done(self, *behind):
        total = self.mine
        for part in self.parts:
            total = total + hold(part, behind)
        return total


class Halves:
    def __init__(self, links, kept, sent):
        self.links, self.kept = links, kept
        self.z = lax.div(lax.axis_index("seq"), 2)
        self.one = links.send(sent, lambda b, s: (b, s ^ 2))

    def arrived(self, *behind):
        self.one = hold(self.one, behind)

    def stage_two(self, *behind):
        self.arrived(*behind)
        self.high = lax.div(self.z, 2)
        out = self.pick(1 - self.high)
        self.two = self.links.send(out, lambda b, s: (b, s ^ 4))
        return out

    def pick(self, i):
        at = lambda v: lax.dynamic_index_in_dim(v, i, 0, keepdims=False)
        return at(self.kept) + at(self.one)

    def landed(self, *behind):
        self.two = hold(self.two, behind)

    def done(self, *behind):
        self.landed(*behind)
        return self.pick(self.high) + self.two


def dct_table(order):
    degree = np.arange(order, dtype=np.float64)[:, None]
    sample = np.arange(order, dtype=np.float64)[None, :]
    table = np.cos(math.pi * (sample + 0.5) * degree / order) * math.sqrt(2.0 / order)
    return np.where(degree == 0.0, table * math.sqrt(0.5), table).astype(np.float32)


def rotation_tables(positions):
    half = ROT // 2
    at = jnp.arange(HG, dtype=jnp.int32) % HEAD_DIM
    inverse = rope_base ** (-2.0 * (at % half).astype(f32) / ROT)
    angles = positions[:, None] * inverse[None, :]
    at = at[None, :]
    sin = jnp.sin(angles)
    return (
        jnp.where(at < ROT, jnp.cos(angles), 1.0),
        jnp.where(at < half, -sin, 0.0),
        jnp.where((at >= half) & (at < ROT), sin, 0.0),
    )


def head_blocks(directions, transposed):
    times = HG // HEAD_DIM
    left = jnp.tile(directions, (times, 1))
    right = np.tile(dct_table(HEAD_DIM), (1, times))
    dims = (((0,), (1,)), ((), ())) if transposed else (((1,), (0,)), ((), ()))
    args = (jnp.asarray(right), left) if transposed else (left, jnp.asarray(right))
    full = lax.dot_general(*args, dims, precision=lax.Precision.HIGHEST)
    block = np.arange(HG) // HEAD_DIM
    return jnp.where(block[:, None] == block[None, :], full, 0.0)


def in_place_kernel(count, start, blocks, down_o, up_o):
    for k in range(count):
        lines = slice(128 * k, 128 * k + 128)
        for half in range(2):
            down_o[lines, 128 * half : 128 * half + 128] = blocks[start + 2 * k + half]
            up_o[half, k] = blocks[2 * k + half]


def in_place(rows, count, after, start=None):
    blocks = rows.reshape(-1, 128, 128)
    return ordered_call(
        functools.partial(in_place_kernel, count, start or 2 * count),
        [blocks],
        after,
        grid=(1,),
        in_specs=[pl.BlockSpec(blocks.shape, lambda i: (0, 0, 0))],
        out_specs=[
            pl.BlockSpec((128 * count, 256), lambda i: (0, 0)),
            pl.BlockSpec((2, count, 128, 128), lambda i: (0, 0, 0, 0)),
        ],
        out_shape=[struct((128 * count, 256), f32), struct((2, count, 128, 128), f32)],
        cost_estimate=cost("in_place"),
        name="in_place",
    )


def blocks_kernel(left, right, out):
    full = lax.dot_general(
        left[...],
        right[...],
        (((1,), (0,)), ((), ())),
        precision=lax.Precision.HIGHEST,
        preferred_element_type=f32,
    )
    same = iota((HG, HG), 0) // HEAD_DIM == iota((HG, HG), 1) // HEAD_DIM
    out[...] = jnp.where(same, full, 0.0)


def head_blocks_after(directions, after):
    times = HG // HEAD_DIM
    left = jnp.tile(directions, (times, 1))
    right = jnp.asarray(np.tile(dct_table(HEAD_DIM), (1, times)))
    whole = lambda a: pl.BlockSpec(a.shape, lambda i: (0, 0))
    return ordered_call(
        blocks_kernel,
        [left, right],
        after,
        grid=(1,),
        in_specs=[whole(left), whole(right)],
        out_specs=pl.BlockSpec((HG, HG), lambda i: (0, 0)),
        out_shape=struct((HG, HG), f32),
        cost_estimate=cost("blocks"),
        name="head_blocks",
    )


def per_device(
    links,
    hidden_in,
    cotangent,
    lengths,
    key_mask,
    ln1_gain,
    ln1_bias,
    ln2_gain,
    ln2_bias,
    w_qkv,
    b_qkv,
    w_out,
    b_out,
    w_up,
    b_up,
    w_down,
    b_down,
    feat_weight,
    directions,
):
    seqs, block, width = hidden_in.shape
    rows = seqs * block
    tuned = links.tuned
    place = lax.axis_index("seq")
    me = lax.axis_index("batch") if tuned else 0 * place
    core = lax.rem(place, 2)
    pos = jnp.stack([me, core, lax.div(place, 2)]).astype(jnp.int32)
    places = place * block + jnp.arange(block, dtype=jnp.int32)
    valid = (places[None, :] < lengths[:, None]) & ((key_mask == 1) | (places[None, :] == 0))
    valid = valid.astype(f32)
    x = hidden_in.reshape(rows, width)
    g = cotangent.reshape(rows, width)
    row = lambda v: v.reshape(1, -1)
    gains = row(ln1_gain), row(ln1_bias), row(ln2_gain), row(ln2_bias)
    a1, a2, g_wide, x_wide = norms(x, g, *gains)
    x_other, g_other = links.core(x_wide), links.core(g_wide)

    forth = head_blocks(directions, True)
    turns = rotation_tables(places.astype(f32))
    weights = row(feat_weight)

    qf, kf, v, state, state_sent = features(
        pos, a1, w_qkv, row(b_qkv), weights, forth, turns, valid
    )
    forward = Carried(links, state, state_sent, False)
    x_other = hold(x_other, [state])
    a1_o, a2_o, g_o = norms(
        x_other, hold(g_other, [state]), *gains, g_type=bf16, after=[state]
    )
    ffn = functools.partial(
        ffn_chunk,
        pos=pos,
        a2=(a2, a2_o),
        g=(g, g_o),
        w_up=w_up,
        w_down=w_down,
        b_up=row(b_up),
    )
    c0 = ffn(0, 1, after=[forward.near(a1_o)])
    g0 = Group(links, *c0[4:8])
    c1 = ffn(1, 2, earlier=c0[:4], more=1, after=[forward.far(c0[8])])
    first = list(c1[4:8])
    if tuned:
        g0.arrived(c1[8])
        first[0::2] = g0.second_in(*first[0::2], 4)
    g1 = Group(links, *first)
    state_in = forward.done(c1[8])
    mixed, dn, dd, grad_own, grad_sent, *mixed_send = mixing(
        pos, g, w_out, qf, kf, v, state_in, after=first[:1]
    )
    reverse = Carried(links, grad_own, grad_sent, True)
    mixed_other = [links.core(part) for part in mixed_send]
    back = head_blocks_after(directions, [mixed])
    held = [reverse.near(back)]
    out_pieces = out_grad(
        pos, mixed, [hold(part, [back]) for part in mixed_other], (g, g_o), after=held
    )
    c2 = ffn(3, 1, earlier=c1[:4], filled=out_pieces, after=[reverse.far(out_pieces[0])])
    held = [c2[8]]
    z0 = None
    if tuned:
        g1.arrived(c2[8])
        g0.second_with(g1)
        held = [g1.second()]
    state_later = reverse.done(held[0])
    g2 = Group(links, *c2[4:8])
    grad_proj, grad_send, bias_qkv, grad_feat = backward(
        pos,
        qf,
        kf,
        v,
        dn,
        dd,
        state_in,
        state_later,
        weights,
        back,
        turns,
        after=held,
    )
    grad_other = links.core(grad_send)
    held = [grad_proj]
    if tuned:
        z0, z0_sent = g0.done(pos, grad_proj)
        g2.arrived(z0)
        held = [z0, g2.second()]
    grad_other = hold(grad_other, held)
    if tuned:
        early = Halves(links, z0, hold(z0_sent, [grad_other]))
    last_parts = qkv_grad(pos, (a1, a1_o), grad_proj, grad_other, after=held)
    acts = c2[:4]
    held = [last_parts[0]]
    pieces = list(last_parts)
    if tuned:
        z1, z1_sent = g1.done(pos, last_parts[0])
        later = Halves(links, z1, z1_sent)
        pieces[0::2] = [hold(piece, [z1]) for piece in pieces[0::2]]
        early.arrived(last_parts[0])
        held = [z1, early.one]
    g3 = Group(links, *pieces)
    own_g = hidden_rows(pos, acts[2:], w_up, (x, x_other), after=held)
    held = [own_g[1]]
    if tuned:
        z2, z2_sent = g2.done(pos, own_g[1])
        middle = Halves(links, z2, z2_sent)
        held += [z2, early.stage_two()]
    own_r = hidden_rows(pos, acts[:2], w_down, sends=own_g[0], after=held)
    others = links.core(own_r[0])
    held = [own_r[1]]
    if tuned:
        early.landed(own_r[1])
        held = [later.stage_two(early.two)]
        g3.arrived(*held)
        held.append(g3.second())
        held.append(middle.stage_two(*held))
    partial, sums1 = first_norm(x, g, grad_proj, w_qkv, row(ln1_gain), after=held)
    half_up = jnp.concatenate([c[8].reshape(-1, 2, 2, 128) for c in (c0, c1, c2)], 0)
    half_up = half_up.transpose(1, 2, 0, 3).reshape(4, 1, 512)
    b_up_grad = jnp.where(core == np.arange(2)[None, :, None], half_up, 0.0).reshape(-1)
    vectors = [
        sums1[0],
        sums1[1],
        own_g[2][0],
        own_g[2][1],
        bias_qkv.reshape(-1),
        sums1[2],
        b_up_grad,
        grad_feat[0],
    ]
    lines = jnp.concatenate([v_.reshape(links.ns, -1) for v_ in vectors], 1)
    held = [partial]
    if tuned:
        lines = jnp.pad(lines.reshape(8, 13, 128), ((0, 0), (0, 3), (0, 0)))
        z3 = g3.done(pos, partial, more=(lines.reshape(4, 32, 128),), direct=True)
        later = later.done(z3[0])
        tail = Line(links, z3)
        held = [z3[0]]
    result, grad_input = ends(
        x,
        mixed,
        partial,
        own_r[1],
        own_g[1],
        hold(others, [partial]),
        w_out,
        row(b_out + b_down),
        row(ln2_gain),
        after=held,
    )

    if tuned:
        first_down, first_up = in_place(early.done(result), 1, [result])
        second_down, second_up = in_place(later, 2, [first_down])
        middle = middle.done(second_down)
        third_down, third_up = in_place(middle, 1, [second_down], start=3)
        tail = tail.done(third_down)
        lines = tail[768:].reshape(2, 16, 128)
        pick = lambda i: lax.dynamic_index_in_dim(lines, i, 0, keepdims=False)
        lines = pick(core) + links.core(pick(1 - core))
        corner = links.send(lines, lambda b, s: (b ^ 3, s))
        lines = lines + links.x(lines) + links.y(lines) + corner
        tail = tail[:768].reshape(6, 128, 128)
        shares, at = [], 0
        for v_ in vectors:
            n = v_.shape[0] // 1024
            shares.append(lines[at : at + n].reshape(-1))
            at += n
        halves = jnp.concatenate([first_up, second_up, third_up], 1)
        w_down_grad = jnp.concatenate([first_down, second_down, third_down], 0)
        w_out_grad = jnp.concatenate([middle[256:384], middle[640:768]], 1)
        blocks = [[tail[i] for i in (0, 3, 2)], [tail[i] for i in (1, 4, 5)]]
        blocks = jnp.stack([jnp.stack(b, 0) for b in blocks], 0)
        halves = jnp.concatenate([halves, blocks], 1)
        pick = lambda i: lax.dynamic_index_in_dim(halves, i, 0, keepdims=False)
        mine, other = pick(core), links.core(pick(1 - core))
        first, second = jnp.where(core == 0, mine, other), jnp.where(core == 0, other, mine)
        both = jnp.stack([first, second], 0)
        w_up_grad = both[:, :4].reshape(1024, 128).T
        w_qkv_grad = both[:, 4:].transpose(1, 0, 2, 3).reshape(768, 128).T
    else:
        total = lax.psum(jnp.concatenate(vectors), ("batch", "seq"))
        shares, at = [], 0
        for v_ in vectors:
            share = v_.shape[0] // links.ns
            shares.append(lax.dynamic_slice_in_dim(total, at + place * share, share, 0))
            at += v_.shape[0]

        def scatter(full):
            part = lax.psum_scatter(full, "batch", scatter_dimension=1, tiled=True)
            return lax.psum_scatter(part, "seq", scatter_dimension=0, tiled=True)

        def of_core(half, axis):
            zero = jnp.zeros_like(half)
            pair = jnp.where(core == 0, half, zero), jnp.where(core == 1, half, zero)
            return jnp.stack(pair, axis)

        both = lambda send, keep: jnp.stack([keep, send], 0)
        groups = (c0, c1, c2)
        slots = lambda pair, n, m, k: both(pair[0][:, :, m : m + n], pair[1][:, :, k : k + n])
        sizes = ((2, 0, 0), (4, 0, 0), (2, 0, 0))
        up = [slots(c[4:6], *size) for c, size in zip(groups, sizes)]
        up = jnp.concatenate(up, 3).reshape(2, 2, 4, 4, 2, 128, 128)
        up = of_core(up.transpose(2, 4, 6, 1, 0, 3, 5).reshape(1024, 4, 512), 2)
        down = [slots(c[6:8], *size) for c, size in zip(groups, sizes)]
        down = jnp.concatenate(down, 3).reshape(2, 2, 4, 4, 2, 128, 128)
        down = of_core(down.transpose(2, 3, 5, 0, 1, 4, 6).reshape(4, 512, 1024), 1)
        by_x = slots(out_pieces[:2], 1, 2, 2).swapaxes(0, 1)
        out = jnp.concatenate([by_x, slots(out_pieces[2:], 1, 2, 2)], 3)
        out = out.transpose(2, 4, 0, 1, 3, 5).reshape(4, 128, 1024)
        by_x = both(*last_parts[:2]).swapaxes(0, 1)
        by_y = both(*last_parts[2:])
        parts = [by_x[:, :, :, :2], by_y[:, :, :, :2]]
        parts.append(jnp.stack([by_x[:, :, :, 2], by_y[:, :, :, 2]], 3))
        qkv = [p.transpose(2, 3, 5, 0, 1, 4).reshape(1024, 4, 128) for p in parts]
        w_up_grad = scatter(up.reshape(1024, 4096))
        w_down_grad = scatter(down.reshape(4096, 1024))
        w_out_grad = scatter(of_core(out, 1).reshape(1024, 1024))
        w_qkv_grad = scatter(of_core(jnp.stack(qkv, 2), 3).reshape(1024, 3072))

    shape = hidden_in.shape
    return (
        result.reshape(shape),
        grad_input.reshape(shape),
        shares[0],
        shares[1],
        shares[2],
        shares[3],
        w_qkv_grad,
        shares[4],
        w_out_grad,
        shares[5],
        w_up_grad,
        shares[6],
        w_down_grad,
        shares[5],
        shares[7],
    )


def solution(mesh):
    links = Links(mesh)
    rows = P("batch", "seq", None)
    spread = P("seq", "batch")
    return jax.shard_map(
        functools.partial(per_device, links),
        mesh=mesh,
        in_specs=(rows, rows, P("batch"), P("batch", "seq")) + (P(),) * 14,
        out_specs=(rows, rows)
        + (P("seq"),) * 4
        + (spread, P("seq"), spread, P("seq"), spread, P("seq"), spread, P("seq"), P("seq")),
        check_vma=False,
    )
```
